32 devices in a mesh: tok: 4 (over y, x), feat: 8 (over z, core).
Axes of the slice: x: 2, y: 2, z: 4, core: 2. Of those that a mesh axis runs over, the one named last changes fastest.
Arguments:
- resid: bfloat16 [1024, 8192], P(None, ('tok', 'feat')), may hold values from -6 to 6
- resid_grad: bfloat16 [1024, 8192], P(None, ('tok', 'feat')), may hold values from -6 to 6
- active: int32 [8, 20], P('tok'), may hold values from 0 to 39, all different within a row
- w_enc: bfloat16 [8192, 5120], P(None, 'feat'), may hold values from -0.0625 to 0.0625
- b_enc: float32 [5120], P('feat'), may hold values from -3 to 3
- w_dec: bfloat16 [5120, 8192], P('feat'), may hold values from -0.25 to 0.25
- b_dec: float32 [8192], P('feat'), may hold values from -3 to 3
Outputs:
- feature_attr: float32 [1024, 5120], P('tok', 'feat')
- error: float32 [1024, 8192], P('tok', 'feat')
- error_attr: float32 [1024], P('tok')
The draws below stay inside these ranges and needn't reach their ends.
Inputs may be any that keep to these rules, and one draw needn't show every extreme that they name: `active`: each row lists 20 different feature blocks; every block is listed by some tile.
All inputs are finite; a program needn't handle non-finite values.
Results may differ from the reference program's by a relative error of at most 0.012.
Values may be sent and summed in bfloat16 or wider, within the bound.
No kernel may reach another device: no remote copies, remote signals or barrier semaphores. Data moves between devices by JAX's collectives and lax.ppermute only.
A program may use at most 128 MiB of HBM per device.

```python
import jax
import jax.numpy as jnp
from jax import lax

D = 8192
BLOCK = 128
BLK_DEV = 5
TILE = 128
ACT = 20
TOKENS = 1024
NBLK = 40
NFEAT = 5120
TILES = 8
N_FEAT = 8


def with_spikes(array, stream_key, source, target, blocks, factor):
    def block_of(position):
        return (jnp.arange(array.shape[position]) // (array.shape[position] // blocks)).reshape((-1,) + (1,) * (array.ndim - 1 - position))

    near = jax.random.permutation(stream_key, blocks)[block_of(target)]
    other_side = (block_of(target) + blocks // 2) % blocks
    return jnp.where((block_of(source) == near) | (block_of(source) == other_side), factor * array, array)


def block_levels(own_key, extent, pieces, smallest, high):
    def one(axis_at, parts):
        heights = jax.random.uniform(jax.random.fold_in(jax.random.fold_in(own_key, 6), axis_at), (parts,), jnp.float32, smallest / len(pieces), high / len(pieces))
        return jnp.repeat(jnp.exp(heights), extent[axis_at] // parts).reshape((-1,) + (1,) * (len(extent) - axis_at - 1))

    loudness = one(*pieces[0])
    for cut in pieces[1:]:
        loudness = loudness * one(*cut)
    return loudness


def choose_distinct(key, rows, count, top, lift):
    ranking = jax.random.permutation(jax.random.fold_in(key, 1), count)
    boost = ranking
    for power in range(3):
        boost = boost * boost // count
    boost = boost * lift // count
    lots = jax.random.randint(jax.random.fold_in(key, 2), (rows, count), 0, 4096) + boost
    holders = jax.random.permutation(jax.random.fold_in(key, 3), rows)[jnp.arange(count) % rows]
    lots = jnp.where(jnp.arange(rows)[:, None] == holders[None, :], 1 << 14, lots)
    merit = lots * count + jnp.arange(count)
    return lax.top_k(merit.astype(jnp.int32), top)[1].astype(jnp.int32)


def noise(own_key, extent, deviation, reach, cuts=(), kind=jnp.bfloat16):
    values = jax.random.normal(own_key, extent, jnp.float32) * deviation
    if len(cuts) > 0:
        values = block_levels(own_key, extent, cuts, -0.22, 0.18) * values
    return jnp.clip(values, min=-reach, max=reach).astype(kind)


def gaussian_with(rng, extent, spread, bound, shards, heavy, kind=jnp.bfloat16):
    array = spread * jax.random.normal(rng, extent, jnp.float32)
    if shards:
        array = array * block_levels(rng, extent, shards, -0.22, 0.18)
    return jnp.clip(with_spikes(array, jax.random.fold_in(rng, 3), *heavy), -bound, bound).astype(kind)


def setup_inputs(seed: int = 0) -> dict:
    key_of = jax.random.split(jax.random.key(seed), 8)
    resid = noise(key_of[0], (TOKENS, D), 1.0, 6.0, ((1, 32),))
    resid_grad = noise(key_of[1], (TOKENS, D), 1.0, 6.0, ((1, 32),))
    active = choose_distinct(key_of[2], TILES, NBLK, ACT, 8192)
    w_enc = noise(key_of[3], (D, NFEAT), D ** -0.5, 0.0625, ((1, 8),))
    b_enc = noise(key_of[4], (NFEAT,), 0.5, 3.0, ((0, 8),), jnp.float32)
    w_dec = gaussian_with(key_of[5], (NFEAT, D), (ACT * BLOCK // 2) ** -0.5, 0.25, ((0, 8),), (0, 1, 8, 2.0))
    b_dec = noise(key_of[6], (D,), 0.5, 3.0, ((0, 8),), jnp.float32)
    return dict(resid=resid, resid_grad=resid_grad, active=active, w_enc=w_enc, b_enc=b_enc, w_dec=w_dec, b_dec=b_dec)


def reference(resid, resid_grad, active, w_enc, b_enc, w_dec, b_dec):
    pre = jnp.dot(resid, w_enc, preferred_element_type=jnp.float32) + b_enc
    block_ids = jnp.arange(NBLK, dtype=jnp.int32)
    hits = jnp.any(active[:, :, None] == block_ids[None, None, :], axis=1).astype(jnp.float32)
    shaped = jnp.maximum(pre, 0.0).reshape(TILES, TILE, NBLK, BLOCK) * hits[:, None, :, None]
    acts = shaped.reshape(TOKENS, NFEAT).astype(jnp.bfloat16)
    group = BLK_DEV * BLOCK
    acts_groups = jnp.transpose(acts.reshape(TOKENS, N_FEAT, group), (1, 0, 2))
    dec_groups = w_dec.reshape(N_FEAT, group, D)

    def add_group(total, pair):
        part = jnp.dot(pair[0], pair[1], preferred_element_type=jnp.float32).astype(jnp.bfloat16)
        return total + part.astype(jnp.float32), None

    summed, _ = lax.scan(add_group, jnp.zeros((TOKENS, D), jnp.float32), (acts_groups, dec_groups))
    recon = summed + b_dec
    error = resid.astype(jnp.float32) - recon
    error_attr = jnp.sum(error * resid_grad.astype(jnp.float32), axis=1)
    proj = lax.dot_general(resid_grad, w_dec, (((1,), (1,)), ((), ())), preferred_element_type=jnp.float32)
    feature_attr = acts.astype(jnp.float32) * proj
    return feature_attr, error, error_attr
```

```python
import functools

import jax
import jax.numpy as jnp
from jax import lax
from jax.experimental import pallas as pl
from jax.experimental.pallas import tpu as pltpu
from jax.sharding import PartitionSpec as P

BLOCK = 128
TILE = 128
STREAMS = ((0, 1), (2, 3))
PARAMS = pltpu.CompilerParams(vmem_limit_bytes=40 << 20)
F32 = jnp.float32
BF16 = jnp.bfloat16


def whole(shape):
    zeros = (0,) * len(shape)
    return pl.BlockSpec(shape, lambda *_: zeros)


def cost(flops, moved):
    return pl.CostEstimate(flops=flops, bytes_accessed=moved, transcendentals=0)


def pieces(refs, streams):
    return [refs[a].at[b] for a, stream in enumerate(streams) for b in range(len(stream))]


def enc_body(streams, first, last, table, *refs):
    count = len(streams)
    near, far = pieces(refs[:count], streams), pieces(refs[count:2 * count], streams)
    refs = refs[2 * count:]
    w_ref, bias_ref, hit_ref = refs[:3]
    refs = refs[3:]
    if not first:
        acc_ref, refs = refs[0], refs[2:]
    out_ref, own_ref = refs[:2]
    core = pl.program_id(0)
    for side, blocks in ((0, near), (1, far)):

        @pl.when(core == side)
        def _():
            total = None
            for s, x in enumerate(blocks):
                term = jnp.dot(x[...], w_ref[table[0] ^ s, 0], preferred_element_type=F32)
                total = term if total is None else total + term

                @pl.when(table[1] == s)
                def _():
                    own_ref[0] = x[...]

            if side == 0:
                target = refs[2] if last else out_ref
                target[...] = total if first else total + acc_ref[...]
            elif last:
                pre = refs[2][...] + total + bias_ref[...]
                tiles = hit_ref.shape[0]
                shaped = jnp.maximum(pre, 0.0).reshape(tiles, TILE, -1) * hit_ref[...][:, None, :]
                out_ref[...] = shaped.reshape(pre.shape).astype(BF16)
            else:
                out_ref[...] += total


def encode(table, near, far, w4, bias, hit, carry, streams, first, last):
    n_tok, n_feat, width, feats = w4.shape
    rows = near[0].shape[1]
    specs = [whole(a.shape) for a in near] + [whole(a.shape) for a in far]
    specs += [
        pl.BlockSpec((n_tok, 1, width, feats), lambda c, t: (0, t[2 + c], 0, 0)),
        whole(bias.shape),
        whole(hit.shape),
    ]
    args = [*near, *far, w4, bias, hit]
    aliases = {}
    if not first:
        acc, own = carry
        specs += [whole(acc.shape), pl.BlockSpec(memory_space=pl.ANY)]
        args += [acc, own]
        aliases = {len(args): 1}
    scratch = [pltpu.VMEM((rows, feats), F32)] if last else []
    return pl.pallas_call(
        functools.partial(enc_body, streams, first, last),
        grid_spec=pltpu.PrefetchScalarGridSpec(
            num_scalar_prefetch=1,
            grid=(2,),
            in_specs=specs,
            out_specs=[
                whole((rows, feats)),
                pl.BlockSpec((1, rows, width), lambda c, t: (t[2 + c], 0, 0)),
            ],
            scratch_shapes=scratch,
        ),
        out_shape=[
            jax.ShapeDtypeStruct((rows, feats), BF16 if last else F32),
            jax.ShapeDtypeStruct((n_feat, rows, width), BF16),
        ],
        input_output_aliases=aliases,
        compiler_params=PARAMS,
        cost_estimate=cost(4 * rows * n_tok * width * feats, 4 * n_tok * width * (feats + rows)),
        name="encode",
    )(table, *args)


def proj_body(streams, first, last, n_tok, table, *refs):
    count = len(streams)
    near, far = pieces(refs[:count], streams), pieces(refs[count:2 * count], streams)
    refs = refs[2 * count:]
    w_refs, acts_ref = refs[:n_tok], refs[n_tok]
    refs = refs[n_tok + 1:]
    if not first:
        acc_ref, refs = refs[0], refs[2:]
    out_ref, own_ref = refs[:2]
    core = pl.program_id(0)
    for side, blocks in ((0, near), (1, far)):

        @pl.when(core == side)
        def _():
            total = None
            for s, x in enumerate(blocks):
                term = lax.dot_general(
                    x[...], w_refs[s][...], (((1,), (1,)), ((), ())), preferred_element_type=F32
                )
                total = term if total is None else total + term

                @pl.when(table[1] == s)
                def _():
                    own_ref[0] = x[...]

            if side == 0:
                out_ref[...] = total if first else total + acc_ref[...]
            elif last:
                attr = acts_ref[...].astype(F32) * (out_ref[...] + total)
                out_ref[...] = attr
                refs[2][...] = jnp.sum(attr, axis=1, keepdims=True)
            else:
                out_ref[...] += total


def project(table, near, far, w_dec, acts, carry, streams, first, last, n_feat):
    rows, width = near[0].shape[1:]
    feats = w_dec.shape[0]
    n_tok = sum(len(s) for s in streams)
    specs = [whole(a.shape) for a in near] + [whole(a.shape) for a in far]
    for s in range(n_tok):
        specs.append(
            pl.BlockSpec(
                (feats, width), lambda c, t, s=s: (0, (t[0] ^ s) * n_feat + t[2 + c])
            )
        )
    args = [*near, *far] + [w_dec] * n_tok
    specs.append(whole(acts.shape))
    args.append(acts)
    aliases = {}
    if not first:
        acc, own = carry
        specs += [whole(acc.shape), pl.BlockSpec(memory_space=pl.ANY)]
        args += [acc, own]
        aliases = {len(args): 1}
    out_specs = [
        whole((rows, feats)),
        pl.BlockSpec((1, rows, width), lambda c, t: (t[2 + c], 0, 0)),
    ]
    out_shape = [
        jax.ShapeDtypeStruct((rows, feats), F32),
        jax.ShapeDtypeStruct((n_feat, rows, width), BF16),
    ]
    if last:
        out_specs.append(whole((rows, 1)))
        out_shape.append(jax.ShapeDtypeStruct((rows, 1), F32))
    return pl.pallas_call(
        functools.partial(proj_body, streams, first, last, n_tok),
        grid_spec=pltpu.PrefetchScalarGridSpec(
            num_scalar_prefetch=1, grid=(2,), in_specs=specs, out_specs=out_specs
        ),
        out_shape=out_shape,
        input_output_aliases=aliases,
        compiler_params=PARAMS,
        cost_estimate=cost(4 * rows * n_tok * width * feats, 4 * n_tok * width * (feats + rows)),
        name="project",
    )(table, *args)


def dec_body(table, acts_ref, w_ref, far_ref, near_ref):
    for side, out_ref in ((0, far_ref), (1, near_ref)):

        @pl.when(pl.program_id(0) == side)
        def _():
            out_ref[...] = jnp.dot(
                acts_ref[...], w_ref[...], preferred_element_type=F32
            ).astype(BF16)


def decode(table, acts, w_dec, share):
    rows, feats = acts.shape
    out = jax.ShapeDtypeStruct((rows, share), BF16)
    return pl.pallas_call(
        dec_body,
        grid_spec=pltpu.PrefetchScalarGridSpec(
            num_scalar_prefetch=1,
            grid=(2,),
            in_specs=[whole(acts.shape), pl.BlockSpec((feats, share), lambda c, t: (0, t[c]))],
            out_specs=[whole(out.shape), whole(out.shape)],
        ),
        out_shape=[out, out],
        compiler_params=PARAMS,
        cost_estimate=cost(4 * rows * feats * share, 4 * share * (feats + rows)),
        name="decode",
    )(table, acts, w_dec)


def local_body(table, x_ref, g_ref, bias_ref, fa_ref, out_ref):
    term = (x_ref[0].astype(F32) - bias_ref[...]) * g_ref[0].astype(F32)
    term = jnp.sum(term, axis=1, keepdims=True)
    step = pl.program_id(0)

    @pl.when(step == 0)
    def _():
        out_ref[...] = term - fa_ref[...]

    @pl.when(step > 0)
    def _():
        out_ref[...] += term


def local_terms(table, own_x, own_g, bias, fa_sum):
    _, rows, width = own_x.shape
    picked = pl.BlockSpec((1, rows, width), lambda r, t: (t[0] + r, 0, 0))
    return pl.pallas_call(
        local_body,
        grid_spec=pltpu.PrefetchScalarGridSpec(
            num_scalar_prefetch=1,
            grid=(bias.shape[1] // width,),
            in_specs=[picked, picked, pl.BlockSpec((1, width), lambda r, t: (0, r)), whole((rows, 1))],
            out_specs=whole((rows, 1)),
        ),
        out_shape=jax.ShapeDtypeStruct((rows, 1), F32),
        compiler_params=PARAMS,
        name="local_terms",
    )(table, own_x, own_g, bias, fa_sum)


def error_body(table, x_ref, near_ref, far_ref, come_ref, bias_ref, out_ref):
    recon = near_ref[...].astype(F32) + far_ref[...].astype(F32)
    recon = recon + come_ref[...].astype(F32) + bias_ref[...]
    out_ref[...] = x_ref[0].astype(F32) - recon


def final_error(table, own_x, near, far, come, bias):
    _, rows, width = own_x.shape
    share = bias.shape[1]
    part = pl.BlockSpec((rows, width), lambda r, t: (0, r))
    return pl.pallas_call(
        error_body,
        grid_spec=pltpu.PrefetchScalarGridSpec(
            num_scalar_prefetch=1,
            grid=(share // width,),
            in_specs=[
                pl.BlockSpec((1, rows, width), lambda r, t: (t[0] + r, 0, 0)),
                part,
                part,
                part,
                pl.BlockSpec((1, width), lambda r, t: (0, r)),
            ],
            out_specs=part,
        ),
        out_shape=jax.ShapeDtypeStruct((rows, share), F32),
        compiler_params=PARAMS,
        name="final_error",
    )(table, own_x, near, far, come, bias)


def ring_program(resid, resid_grad, active, w_enc, b_enc, w_dec, b_dec):
    n_tok, n_feat = lax.axis_size("tok"), lax.axis_size("feat")
    i, j = lax.axis_index("tok"), lax.axis_index("feat")
    chips = n_feat // 2
    chip, core = j // 2, j % 2
    width = resid.shape[1]
    rows = resid.shape[0] // n_tok
    feats = w_enc.shape[1]
    share = n_tok * width
    streams = STREAMS

    def exchange(array):
        def block(s):
            mine = lax.dynamic_slice_in_dim(array, (i ^ s) * rows, rows, 0)
            if s == 0:
                return mine
            return lax.ppermute(mine, "tok", [(a, a ^ s) for a in range(n_tok)])

        blocks = [block(s) for s in range(n_tok)]
        return [jnp.stack([blocks[s] for s in stream]) for stream in streams]

    ring = [(a, (a + 2) % n_feat) for a in range(n_feat)]
    swap = [(a, a ^ 1) for a in range(n_feat)]

    def gather(shards, after=None):
        near, far = [list(shards)], []
        for k in range(1, chips):
            step = []
            for n, held in enumerate(near[-1]):
                if k == 1 and after is not None:
                    held, _ = lax.optimization_barrier((held, after[n]))
                step.append(lax.ppermute(held, "feat", ring))
            near.append(step)
        for step in near:
            far.append([lax.ppermute(held, "feat", swap) for held in step])
        return near, far

    near_x, far_x = gather(exchange(resid))
    near_g, far_g = gather(exchange(resid_grad), after=near_x[-1])

    blocks = feats // BLOCK
    block_ids = j * blocks + jnp.arange(blocks, dtype=jnp.int32)
    hits = jnp.any(active[:, :, None] == block_ids[None, None, :], axis=1).astype(F32)
    hit = jnp.repeat(hits, BLOCK, axis=1)
    bias = b_enc.reshape(1, feats)
    b_row = b_dec.reshape(1, share)
    ratio = n_feat // n_tok
    own_sub = i ^ (j // ratio)
    own_start = ((j % ratio) * n_tok).astype(jnp.int32).reshape(1)

    def table(k):
        source = 2 * ((chip + chips - k) % chips)
        return jnp.stack([i, own_sub, source + core, source + 1 - core]).astype(jnp.int32)

    tables = [table(k) for k in range(chips)]
    w4 = w_enc.reshape(n_tok, n_feat, width, feats)
    carry = None
    for k in range(chips):
        carry = encode(
            tables[k], near_x[k], far_x[k], w4, bias, hit, carry, streams, k == 0, k == chips - 1
        )
    acts, own_x = carry

    come = None
    for k in range(chips - 1, -1, -1):
        dest = 2 * ((chip + k) % chips)
        far_out, near_out = decode(
            jnp.stack([dest + 1 - core, dest + core]).astype(jnp.int32), acts, w_dec, share
        )
        far_in = lax.ppermute(far_out, "feat", swap)
        if k == 0:
            break
        total = near_out.astype(F32) + far_in.astype(F32)
        if come is not None:
            total = total + come.astype(F32)
        come = lax.ppermute(total.astype(BF16), "feat", ring)

    carry = None
    for k in range(chips):
        carry = project(
            tables[k], near_g[k], far_g[k], w_dec, acts, carry, streams, k == 0, k == chips - 1, n_feat
        )
    feature_attr, own_g, fa_sum = carry

    attr = local_terms(own_start, own_x, own_g, b_row, fa_sum).reshape(-1, TILE)
    reach = 1
    while reach < n_feat:
        attr = attr + lax.ppermute(attr, "feat", [(a, a ^ reach) for a in range(n_feat)])
        reach *= 2

    error = final_error(own_start, own_x, near_out, far_in, come, b_row)
    return feature_attr, error, attr.reshape(rows)


def gathered_program(resid, resid_grad, active, w_enc, b_enc, w_dec, b_dec):
    n_tok = lax.axis_size("tok")
    n_feat = lax.axis_size("feat")
    width = resid.shape[1]

    def rows_of(array):
        part = lax.all_to_all(array, "tok", split_axis=0, concat_axis=1, tiled=True)
        part = part.reshape(part.shape[0], n_tok, 1, width)
        part = lax.all_gather(part, "feat", axis=2, tiled=True)
        return part.reshape(part.shape[0], n_tok * n_feat * width)

    rows_x, rows_g = rows_of(resid), rows_of(resid_grad)
    tok_rows = rows_x.shape[0]
    feat_dev = w_enc.shape[1]
    blocks = feat_dev // BLOCK
    tiles_dev = active.shape[0]
    block_ids = lax.axis_index("feat") * blocks + jnp.arange(blocks, dtype=jnp.int32)
    hits = jnp.any(active[:, :, None] == block_ids[None, None, :], axis=1).astype(F32)
    pre = jnp.dot(rows_x, w_enc, preferred_element_type=F32) + b_enc
    shaped = jnp.maximum(pre, 0.0).reshape(tiles_dev, TILE, blocks, BLOCK) * hits[:, None, :, None]
    acts = shaped.reshape(tok_rows, feat_dev).astype(BF16)
    partial_recon = jnp.dot(acts, w_dec, preferred_element_type=F32)
    recon_share = lax.psum_scatter(
        partial_recon.astype(BF16), "feat", scatter_dimension=1, tiled=True
    ).astype(F32)
    share = recon_share.shape[1]
    start = lax.axis_index("feat") * share
    own_x = lax.dynamic_slice_in_dim(rows_x, start, share, 1)
    own_g = lax.dynamic_slice_in_dim(rows_g, start, share, 1)
    recon = recon_share + b_dec
    error = own_x.astype(F32) - recon
    local_sums = jnp.sum(error * own_g.astype(F32), axis=1)
    error_attr = lax.psum(local_sums, "feat")
    proj = lax.dot_general(rows_g, w_dec, (((1,), (1,)), ((), ())), preferred_element_type=F32)
    return acts.astype(F32) * proj, error, error_attr


def per_device(resid, *rest):
    n_tok, n_feat = lax.axis_size("tok"), lax.axis_size("feat")
    fits = resid.shape[1] % 128 == 0 and n_tok == 4 and n_feat % n_tok == 0
    return (ring_program if fits else gathered_program)(resid, *rest)


def solution(mesh):
    placed = (
        P(None, ("tok", "feat")),
        P(None, ("tok", "feat")),
        P("tok", None),
        P(None, "feat"),
        P("feat"),
        P("feat", None),
        P("feat"),
    )
    return jax.shard_map(
        per_device,
        mesh=mesh,
        in_specs=placed,
        out_specs=(P("tok", "feat"), P("tok", "feat"), P("tok")),
        check_vma=False,
    )
```

```python
import functools

import jax
import jax.numpy as jnp
from jax import lax
from jax.experimental import pallas as pl
from jax.experimental.pallas import tpu as pltpu
from jax.sharding import PartitionSpec as P

BLOCK = 128
TILE = 128
X_STREAMS = ((0,), (1, 2), (3,))
G_STREAMS = ((0, 1, 2, 3),)
HALVES = 1
PARAMS = pltpu.CompilerParams(vmem_limit_bytes=56 << 20)
F32 = jnp.float32
BF16 = jnp.bfloat16


def whole(shape):
    zeros = (0,) * len(shape)
    return pl.BlockSpec(shape, lambda *_: zeros)


def cost(flops, moved):
    return pl.CostEstimate(flops=flops, bytes_accessed=moved, transcendentals=0)


def after(value, *others):
    return lax.optimization_barrier((value, others))[0]


def pieces(refs, streams):
    return [refs[a].at[b] for a, stream in enumerate(streams) for b in range(len(stream))]


def take_slots(table, slots, own_ref, total_ref, carry_ref, product):
    step = pl.program_id(0)
    for q, blocks in enumerate(slots):

        @pl.when((step == q) & (table[3 + 2 * q] == 1))
        def _():
            total = None
            for s, x in enumerate(blocks):
                term = product(s, x)
                total = term if total is None else total + term

                @pl.when(table[1] == s)
                def _():
                    own_ref[0] = x[...]

            if q > 0:
                total = total + total_ref[...]
            elif carry_ref is not None:
                total = total + carry_ref[...]
            total_ref[...] = total


def enc_body(streams, count, first, last, table, *refs):
    size = len(streams)
    slots = [pieces(refs[q * size:(q + 1) * size], streams) for q in range(count)]
    refs = refs[count * size:]
    w_ref, bias_ref, hit_ref = refs[:3]
    refs = refs[3:]
    carry_ref = None
    if not first:
        carry_ref, refs = refs[0], refs[2:]
    out_ref, own_ref = refs[:2]
    total_ref = refs[2] if last else out_ref

    def product(s, x):
        return jnp.dot(x[...], w_ref[table[0] ^ s, 0], preferred_element_type=F32)

    take_slots(table, slots, own_ref, total_ref, carry_ref, product)
    if last:

        @pl.when(pl.program_id(0) == count - 1)
        def _():
            pre = total_ref[...] + bias_ref[...]
            tiles = hit_ref.shape[0]
            shaped = jnp.maximum(pre, 0.0).reshape(tiles, TILE, -1) * hit_ref[...][:, None, :]
            out_ref[...] = shaped.reshape(pre.shape).astype(BF16)


def encode(table, slots, w4, bias, hit, carry, streams, last):
    n_tok, n_feat, width, feats = w4.shape
    rows = slots[0][0].shape[1]
    first = carry is None
    flat = [a for slot in slots for a in slot]
    specs = [whole(a.shape) for a in flat] + [
        pl.BlockSpec((n_tok, 1, width, feats), lambda q, t: (0, t[2 + 2 * q], 0, 0)),
        whole(bias.shape),
        whole(hit.shape),
    ]
    args = [*flat, w4, bias, hit]
    aliases = {}
    if not first:
        specs += [whole(carry[0].shape), pl.BlockSpec(memory_space=pl.ANY)]
        args += carry
        aliases = {len(args): 1}
    count = len(slots)
    return pl.pallas_call(
        functools.partial(enc_body, streams, count, first, last),
        grid_spec=pltpu.PrefetchScalarGridSpec(
            num_scalar_prefetch=1,
            grid=(count,),
            in_specs=specs,
            out_specs=[
                whole((rows, feats)),
                pl.BlockSpec((1, rows, width), lambda q, t: (t[2 + 2 * q], 0, 0)),
            ],
            scratch_shapes=[pltpu.VMEM((rows, feats), F32)] if last else [],
        ),
        out_shape=[
            jax.ShapeDtypeStruct((rows, feats), BF16 if last else F32),
            jax.ShapeDtypeStruct((n_feat, rows, width), BF16),
        ],
        input_output_aliases=aliases,
        compiler_params=PARAMS,
        cost_estimate=cost(
            2 * count * rows * n_tok * width * feats, 2 * count * n_tok * width * (feats + rows)
        ),
        name="encode",
    )(table, *args)


def proj_body(streams, count, first, last, n_tok, table, *refs):
    size = len(streams)
    slots = [pieces(refs[q * size:(q + 1) * size], streams) for q in range(count)]
    refs = refs[count * size:]
    w_refs, acts_ref = refs[:n_tok], refs[n_tok]
    refs = refs[n_tok + 1:]
    carry_ref = None
    if not first:
        carry_ref, refs = refs[0], refs[2:]
    out_ref, own_ref = refs[:2]

    def product(s, x):
        return lax.dot_general(
            x[...], w_refs[s][...], (((1,), (1,)), ((), ())), preferred_element_type=F32
        )

    take_slots(table, slots, own_ref, out_ref, carry_ref, product)
    if last:

        @pl.when(pl.program_id(0) == count - 1)
        def _():
            attr = acts_ref[...].astype(F32) * out_ref[...]
            out_ref[...] = attr
            refs[2][...] = jnp.sum(attr, axis=1, keepdims=True)


def project(table, slots, w_dec, acts, carry, streams, last, n_feat):
    rows, width = slots[0][0].shape[1:]
    feats = w_dec.shape[0]
    n_tok = sum(len(s) for s in streams)
    first = carry is None
    flat = [a for slot in slots for a in slot]
    specs = [whole(a.shape) for a in flat]
    for s in range(n_tok):
        specs.append(
            pl.BlockSpec(
                (feats, width), lambda q, t, s=s: (0, (t[0] ^ s) * n_feat + t[2 + 2 * q])
            )
        )
    specs.append(whole(acts.shape))
    args = [*flat] + [w_dec] * n_tok + [acts]
    aliases = {}
    if not first:
        specs += [whole(carry[0].shape), pl.BlockSpec(memory_space=pl.ANY)]
        args += carry
        aliases = {len(args): 1}
    out_specs = [
        whole((rows, feats)),
        pl.BlockSpec((1, rows, width), lambda q, t: (t[2 + 2 * q], 0, 0)),
    ]
    out_shape = [
        jax.ShapeDtypeStruct((rows, feats), F32),
        jax.ShapeDtypeStruct((n_feat, rows, width), BF16),
    ]
    if last:
        out_specs.append(whole((rows, 1)))
        out_shape.append(jax.ShapeDtypeStruct((rows, 1), F32))
    count = len(slots)
    return pl.pallas_call(
        functools.partial(proj_body, streams, count, first, last, n_tok),
        grid_spec=pltpu.PrefetchScalarGridSpec(
            num_scalar_prefetch=1, grid=(count,), in_specs=specs, out_specs=out_specs
        ),
        out_shape=out_shape,
        input_output_aliases=aliases,
        compiler_params=PARAMS,
        cost_estimate=cost(
            2 * count * rows * n_tok * width * feats, 2 * count * n_tok * width * (feats + rows)
        ),
        name="project",
    )(table, *args)


def dec_body(table, acts_ref, w_ref, *out_refs):
    for side in range(2):

        @pl.when(pl.program_id(0) == side)
        def _():
            part = jnp.dot(acts_ref[...], w_ref[...], preferred_element_type=F32).astype(BF16)
            rows = part.shape[0] // HALVES
            for h in range(HALVES):
                out_refs[side * HALVES + h][...] = part[h * rows:(h + 1) * rows]


def decode(table, acts, w_dec, share):
    rows, feats = acts.shape
    outs = [jax.ShapeDtypeStruct((rows // HALVES, share), BF16)] * (2 * HALVES)
    outs = pl.pallas_call(
        dec_body,
        grid_spec=pltpu.PrefetchScalarGridSpec(
            num_scalar_prefetch=1,
            grid=(2,),
            in_specs=[whole(acts.shape), pl.BlockSpec((feats, share), lambda c, t: (0, t[c]))],
            out_specs=[whole(out.shape) for out in outs],
        ),
        out_shape=outs,
        compiler_params=PARAMS,
        cost_estimate=cost(4 * rows * feats * share, 4 * share * (feats + rows)),
        name="decode",
    )(table, acts, w_dec)
    return outs[:HALVES], outs[HALVES:]


def local_body(table, x_ref, g_ref, bias_ref, fa_ref, out_ref):
    total = -fa_ref[...]
    for r in range(x_ref.shape[0]):
        width = x_ref.shape[2]
        term = x_ref[r].astype(F32) - bias_ref[:, r * width:(r + 1) * width]
        total += jnp.sum(term * g_ref[r].astype(F32), axis=1, keepdims=True)
    out_ref[...] = total


def local_terms(table, own_x, own_g, bias, fa_sum):
    _, rows, width = own_x.shape
    picked = pl.BlockSpec((bias.shape[1] // width, rows, width), lambda r, t: (t[0], 0, 0))
    return pl.pallas_call(
        local_body,
        grid_spec=pltpu.PrefetchScalarGridSpec(
            num_scalar_prefetch=1,
            grid=(1,),
            in_specs=[picked, picked, whole(bias.shape), whole((rows, 1))],
            out_specs=whole((rows, 1)),
        ),
        out_shape=jax.ShapeDtypeStruct((rows, 1), F32),
        compiler_params=PARAMS,
        name="local_terms",
    )(table, own_x, own_g, bias, fa_sum)


def error_body(table, x_ref, bias_ref, *refs):
    terms, out_ref = refs[:-1], refs[-1]
    for h in range(HALVES):
        recon = bias_ref[...]
        for term in terms[h::HALVES]:
            recon = recon + term[...].astype(F32)
        rows = recon.shape[0]
        here = slice(h * rows, (h + 1) * rows)
        width = x_ref.shape[2]
        for r in range(x_ref.shape[0]):
            cols = slice(r * width, (r + 1) * width)
            out_ref[here, cols] = x_ref[r, here, :].astype(F32) - recon[:, cols]


def final_error(table, own_x, bias, terms):
    _, rows, width = own_x.shape
    share = bias.shape[1]
    count = share // width // 2
    flat = [half for term in terms for half in term]
    return pl.pallas_call(
        error_body,
        grid_spec=pltpu.PrefetchScalarGridSpec(
            num_scalar_prefetch=1,
            grid=(2,),
            in_specs=[
                pl.BlockSpec((count, rows, width), lambda r, t: (2 * t[0] + r, 0, 0)),
                pl.BlockSpec((1, share // 2), lambda r, t: (0, r)),
            ]
            + [pl.BlockSpec((rows // HALVES, share // 2), lambda r, t: (0, r)) for _ in flat],
            out_specs=pl.BlockSpec((rows, share // 2), lambda r, t: (0, r)),
        ),
        out_shape=jax.ShapeDtypeStruct((rows, share), F32),
        compiler_params=PARAMS,
        cost_estimate=cost(8 * rows * share, 14 * rows * share),
        name="final_error",
    )(table, own_x, bias, *flat)


def line_program(resid, resid_grad, active, w_enc, b_enc, w_dec, b_dec):
    n_tok, n_feat = lax.axis_size("tok"), lax.axis_size("feat")
    i, j = lax.axis_index("tok"), lax.axis_index("feat")
    chips = n_feat // 2
    chip, core = j // 2, j % 2
    width = resid.shape[1]
    rows = resid.shape[0] // n_tok
    feats = w_enc.shape[1]
    share = n_tok * width

    def along(pairs):
        return [(2 * a + c, 2 * b + c) for a, b in pairs for c in range(2)]

    def send(array, pairs):
        return lax.ppermute(array, "feat", along(pairs))

    def cross(array, low=0, high=chips - 1):
        pairs = [(2 * a + c, 2 * a + 1 - c) for a in range(low, high + 1) for c in range(2)]
        return lax.ppermute(array, "feat", pairs)

    def exchange(array, streams):
        def block(s):
            mine = lax.dynamic_slice_in_dim(array, (i ^ s) * rows, rows, 0)
            if s == 0:
                return mine
            return lax.ppermute(mine, "tok", [(a, a ^ s) for a in range(n_tok)])

        blocks = [block(s) for s in range(n_tok)]
        return [jnp.stack([blocks[s] for s in stream]) for stream in streams]

    def table(sources):
        numbers = [i, i ^ (j // (n_feat // n_tok))]
        seen = jnp.int32(0)
        for offset, valid in sources:
            place = chip + offset if isinstance(offset, int) else offset
            held = jnp.where(valid, place, seen)
            for side in range(2):
                numbers += [2 * held + (core ^ side), jnp.asarray(valid)]
            seen = held
        return jnp.stack([jnp.asarray(n).astype(jnp.int32) for n in numbers])

    own_start = (j % (n_feat // n_tok)).astype(jnp.int32).reshape(1)
    blocks = feats // BLOCK
    block_ids = j * blocks + jnp.arange(blocks, dtype=jnp.int32)
    hits = jnp.any(active[:, :, None] == block_ids[None, None, :], axis=1).astype(F32)
    hit = jnp.repeat(hits, BLOCK, axis=1)
    bias = b_enc.reshape(1, feats)
    b_row = b_dec.reshape(1, share)
    w4 = w_enc.reshape(n_tok, n_feat, width, feats)

    shard_x = exchange(resid, X_STREAMS)
    shard_g = exchange(resid_grad, G_STREAMS)

    ring = [(a, (a + 1) % chips) for a in range(chips)]
    near_x = [shard_x]
    far_x = [[cross(a) for a in shard_x]]
    for k in range(1, chips):
        held = near_x[-1]
        if k == 2:
            held = [after(a, *shard_g) for a in held]
        if k == 3:
            held = [*held[:-1], after(held[-1], carry_x)]
        near_x.append([send(a, ring) for a in held])
        far_x.append([cross(a) for a in near_x[-1]])
        if k == 1:
            slots = [near_x[0], far_x[0], near_x[1], far_x[1]]
            sources = [(chip, True), ((chip + chips - 1) % chips, True)]
            carry_x = encode(table(sources), slots, w4, bias, hit, None, X_STREAMS, False)
    slots = [near_x[2], far_x[2], near_x[3], far_x[3]]
    sources = [((chip + chips - k) % chips, True) for k in (2, 3)]
    acts, own_x = encode(table(sources), slots, w4, bias, hit, carry_x, X_STREAMS, True)

    up_pairs = [(a, a + 1) for a in range(chips - 1)]
    down_pairs = [(a + 1, a) for a in range(chips - 1)]
    last_x = near_x[-1]
    shard_g = [after(a, *last_x) for a in shard_g]
    up_1 = [send(a, up_pairs) for a in shard_g]
    down_1 = [send(a, down_pairs) for a in shard_g]

    parts = {}
    for k in (3, 2, 1, 0):
        dest = 2 * (chip ^ k)
        ids = jnp.stack([dest + 1 - core, dest + core]).astype(jnp.int32)
        far_out, near_out = decode(ids, acts, w_dec, share)
        parts[k] = (near_out, [cross(a) for a in far_out], far_out)

    held_up = [after(a, parts[3][2]) for a in up_1]
    held_down = [after(a, parts[3][2]) for a in down_1]
    up_2 = [send(a, up_pairs[1:]) for a in held_up]
    down_2 = [send(a, down_pairs[:-1]) for a in held_down]
    two_g = [a + b for a, b in zip(up_2, down_2)]
    three_g = [send(a, [(2, 3), (1, 0)]) for a in two_g]

    def pair_sum(k, h):
        return parts[k][0][h].astype(F32) + parts[k][1][h].astype(F32)

    second, third, ups, downs = [], [], [], []
    for h in range(HALVES):
        sum_3, sum_1 = pair_sum(3, h), pair_sum(1, h)
        come = send(sum_3.astype(BF16), [(0, 1), (3, 2)])
        going = (pair_sum(2, h) + come.astype(F32)).astype(BF16)
        second.append(going)
        up = send(going, up_pairs[:2])
        down = send(going, down_pairs[1:])
        going_up = (jnp.where(chip == 1, sum_3, sum_1) + up.astype(F32)).astype(BF16)
        going_down = (jnp.where(chip == 2, sum_3, sum_1) + down.astype(F32)).astype(BF16)
        third += [going_up, going_down]
        ups.append(send(going_up, up_pairs))
        downs.append(send(going_down, down_pairs))

    slots = [shard_g, [cross(a) for a in shard_g]]
    slots += [up_1, [cross(a, 1) for a in up_1], down_1, [cross(a, 0, chips - 2) for a in down_1]]
    sources = [(0, True), (-1, chip >= 1), (1, chip <= chips - 2)]
    carry = project(table(sources), slots, w_dec, after(acts, *second), None, G_STREAMS, False, n_feat)
    slots = [two_g, [cross(a) for a in two_g], three_g, [cross(a) for a in three_g]]
    sources = [(chip ^ 2, True), (chip ^ 3, (chip == 0) | (chip == chips - 1))]
    feature_attr, own_g, fa_sum = project(
        table(sources), slots, w_dec, after(acts, *third), carry, G_STREAMS, True, n_feat
    )

    attr = local_terms(own_start, own_x, own_g, b_row, fa_sum).reshape(-1, TILE)
    reach = 1
    while reach < n_feat:
        attr = attr + lax.ppermute(attr, "feat", [(a, a ^ reach) for a in range(n_feat)])
        reach *= 2

    error = final_error(own_start, own_x, b_row, [parts[0][0], parts[0][1], ups, downs])
    return feature_attr, error, attr.reshape(rows)


def gathered_program(resid, resid_grad, active, w_enc, b_enc, w_dec, b_dec):
    n_tok = lax.axis_size("tok")
    n_feat = lax.axis_size("feat")
    width = resid.shape[1]

    def rows_of(array):
        part = lax.all_to_all(array, "tok", split_axis=0, concat_axis=1, tiled=True)
        part = part.reshape(part.shape[0], n_tok, 1, width)
        part = lax.all_gather(part, "feat", axis=2, tiled=True)
        return part.reshape(part.shape[0], n_tok * n_feat * width)

    rows_x, rows_g = rows_of(resid), rows_of(resid_grad)
    tok_rows = rows_x.shape[0]
    feat_dev = w_enc.shape[1]
    blocks = feat_dev // BLOCK
    tiles_dev = active.shape[0]
    block_ids = lax.axis_index("feat") * blocks + jnp.arange(blocks, dtype=jnp.int32)
    hits = jnp.any(active[:, :, None] == block_ids[None, None, :], axis=1).astype(F32)
    pre = jnp.dot(rows_x, w_enc, preferred_element_type=F32) + b_enc
    shaped = jnp.maximum(pre, 0.0).reshape(tiles_dev, TILE, blocks, BLOCK) * hits[:, None, :, None]
    acts = shaped.reshape(tok_rows, feat_dev).astype(BF16)
    partial_recon = jnp.dot(acts, w_dec, preferred_element_type=F32)
    recon_share = lax.psum_scatter(
        partial_recon.astype(BF16), "feat", scatter_dimension=1, tiled=True
    ).astype(F32)
    share = recon_share.shape[1]
    start = lax.axis_index("feat") * share
    own_x = lax.dynamic_slice_in_dim(rows_x, start, share, 1)
    own_g = lax.dynamic_slice_in_dim(rows_g, start, share, 1)
    recon = recon_share + b_dec
    error = own_x.astype(F32) - recon
    local_sums = jnp.sum(error * own_g.astype(F32), axis=1)
    error_attr = lax.psum(local_sums, "feat")
    proj = lax.dot_general(rows_g, w_dec, (((1,), (1,)), ((), ())), preferred_element_type=F32)
    return acts.astype(F32) * proj, error, error_attr


def per_device(resid, *rest):
    fits = resid.shape[1] % 128 == 0 and lax.axis_size("tok") == 4 and lax.axis_size("feat") == 8
    return (line_program if fits else gathered_program)(resid, *rest)


def solution(mesh):
    placed = (
        P(None, ("tok", "feat")),
        P(None, ("tok", "feat")),
        P("tok", None),
        P(None, "feat"),
        P("feat"),
        P("feat", None),
        P("feat"),
    )
    return jax.shard_map(
        per_device,
        mesh=mesh,
        in_specs=placed,
        out_specs=(P("tok", "feat"), P("tok", "feat"), P("tok")),
        check_vma=False,
    )
```

```python
import functools

import jax
import jax.numpy as jnp
from jax import lax
from jax.experimental import pallas as pl
from jax.experimental.pallas import tpu as pltpu
from jax.sharding import PartitionSpec as P

BLOCK = 128
TILE = 128
X_STREAMS = ((0,), (1, 2, 3))
G_STREAMS = ((0, 1, 2, 3),)
PARAMS = pltpu.CompilerParams(vmem_limit_bytes=56 << 20)
F32 = jnp.float32
BF16 = jnp.bfloat16
LIGHT = pl.CostEstimate(flops=1, bytes_accessed=1, transcendentals=0)


def whole(shape):
    zeros = (0,) * len(shape)
    return pl.BlockSpec(shape, lambda *_: zeros)


def after(value, *others):
    return lax.optimization_barrier((value, others))[0]


def pieces(refs, streams):
    return [refs[a].at[b] for a, stream in enumerate(streams) for b in range(len(stream))]


def enc_body(streams, count, first, last, table, *refs):
    size = len(streams)
    slots = [pieces(refs[q * size:(q + 1) * size], streams) for q in range(count)]
    refs = refs[count * size:]
    n_tok = len(slots[0])
    w_refs = refs[:n_tok]
    bias_ref, hit_ref = refs[n_tok:n_tok + 2]
    refs = refs[n_tok + 2:]
    carry_ref = None
    if not first:
        carry_ref, refs = refs[0], refs[2:]
    out_ref, own_ref = refs[:2]
    total_ref = refs[2] if last else out_ref
    step = pl.program_id(0)
    for q, blocks in enumerate(slots):

        @pl.when(step == q)
        def _():
            total = None
            for x, w_ref in zip(blocks, w_refs):
                term = jnp.dot(x[...], w_ref[0, 0], preferred_element_type=F32)
                total = term if total is None else total + term
            if q > 0:
                total = total + total_ref[...]
            elif not first:
                total = total + carry_ref[...]
            if last and q == count - 1:
                pre = total + bias_ref[...]
                tiles = hit_ref.shape[0]
                shaped = jnp.maximum(pre, 0.0).reshape(tiles, TILE, -1) * hit_ref[...][:, None, :]
                out_ref[...] = shaped.reshape(pre.shape).astype(BF16)
            else:
                total_ref[...] = total
            for s, x in enumerate(blocks):

                @pl.when(table[1] == s)
                def _():
                    own_ref[0] = x[...]


def encode(table, slots, w4, bias, hit, carry, streams, last):
    n_tok, n_feat, width, feats = w4.shape
    rows = slots[0][0].shape[1]
    first = carry is None
    flat = [a for slot in slots for a in slot]
    specs = [whole(a.shape) for a in flat]
    for s in range(n_tok):
        specs.append(
            pl.BlockSpec((1, 1, width, feats), lambda q, t, s=s: (t[0] ^ s, t[2 + q], 0, 0))
        )
    specs += [whole(bias.shape), whole(hit.shape)]
    args = [*flat] + [w4] * n_tok + [bias, hit]
    aliases = {}
    if not first:
        specs += [whole(carry[0].shape), pl.BlockSpec(memory_space=pl.ANY)]
        args += carry
        aliases = {len(args): 1}
    count = len(slots)
    return pl.pallas_call(
        functools.partial(enc_body, streams, count, first, last),
        grid_spec=pltpu.PrefetchScalarGridSpec(
            num_scalar_prefetch=1,
            grid=(count,),
            in_specs=specs,
            out_specs=[
                whole((rows, feats)),
                pl.BlockSpec((1, rows, width), lambda q, t: (t[2 + q], 0, 0)),
            ],
            scratch_shapes=[pltpu.VMEM((rows, feats), F32)] if last else [],
        ),
        out_shape=[
            jax.ShapeDtypeStruct((rows, feats), BF16 if last else F32),
            jax.ShapeDtypeStruct((n_feat, rows, width), BF16),
        ],
        input_output_aliases=aliases,
        compiler_params=PARAMS,
        cost_estimate=LIGHT,
        name="encode",
    )(table, *args)


def dec_body(table, acts_ref, w_ref, *out_refs):
    for q, out_ref in enumerate(out_refs):

        @pl.when(pl.program_id(0) == q)
        def _():
            out_ref[...] = jnp.dot(
                acts_ref[...], w_ref[...], preferred_element_type=F32
            ).astype(BF16)


def decode(table, acts, w_dec, share, count):
    rows, feats = acts.shape
    outs = [jax.ShapeDtypeStruct((rows, share), BF16)] * count
    return pl.pallas_call(
        dec_body,
        grid_spec=pltpu.PrefetchScalarGridSpec(
            num_scalar_prefetch=1,
            grid=(count,),
            in_specs=[whole(acts.shape), pl.BlockSpec((feats, share), lambda q, t: (0, t[q]))],
            out_specs=[whole(out.shape) for out in outs],
        ),
        out_shape=outs,
        compiler_params=PARAMS,
        cost_estimate=LIGHT,
        name="decode",
    )(table, acts, w_dec)


def proj_body(n_tok, table, g_ref, *refs):
    w_refs, (acts_ref, x_ref, bias_ref, out_ref, sum_ref) = refs[:n_tok], refs[n_tok:]
    step, steps = pl.program_id(0), pl.num_programs(0)
    total = None
    for s, w_ref in enumerate(w_refs):
        term = lax.dot_general(
            g_ref[0, s], w_ref[...], (((1,), (1,)), ((), ())), preferred_element_type=F32
        )
        total = term if total is None else total + term

    @pl.when(step == 0)
    def _():
        out_ref[...] = total
        sum_ref[...] = jnp.zeros_like(sum_ref)

    @pl.when((step > 0) & (step < steps - 1))
    def _():
        out_ref[...] += total

    @pl.when(step // n_tok == table[2])
    def _():
        term = (x_ref[0].astype(F32) - bias_ref[...]) * g_ref[0, table[1]].astype(F32)
        sum_ref[...] += jnp.sum(term, axis=1, keepdims=True)

    @pl.when(step == steps - 1)
    def _():
        attr = acts_ref[...].astype(F32) * (out_ref[...] + total)
        out_ref[...] = attr
        sum_ref[...] -= jnp.sum(attr, axis=1, keepdims=True)


def project(table, rows_g, w_dec, acts, own_x, bias):
    n_feat, n_tok, rows, width = rows_g.shape
    feats = w_dec.shape[0]
    specs = [pl.BlockSpec((1, n_tok, rows, width), lambda q, t: (q, 0, 0, 0))]
    for s in range(n_tok):
        specs.append(pl.BlockSpec((feats, width), lambda q, t, s=s: (0, (t[0] ^ s) * n_feat + q)))
    specs += [
        whole(acts.shape),
        pl.BlockSpec((1, rows, width), lambda q, t: (t[2] * n_tok + q % n_tok, 0, 0)),
        pl.BlockSpec((1, width), lambda q, t: (0, q % n_tok)),
    ]
    return pl.pallas_call(
        functools.partial(proj_body, n_tok),
        grid_spec=pltpu.PrefetchScalarGridSpec(
            num_scalar_prefetch=1,
            grid=(n_feat,),
            in_specs=specs,
            out_specs=[whole((rows, feats)), whole((rows, 1))],
        ),
        out_shape=[
            jax.ShapeDtypeStruct((rows, feats), F32),
            jax.ShapeDtypeStruct((rows, 1), F32),
        ],
        compiler_params=PARAMS,
        cost_estimate=LIGHT,
        name="project",
    )(table, rows_g, *[w_dec] * n_tok, acts, own_x, bias)


def error_body(table, x_ref, bias_ref, *refs):
    terms, out_ref = refs[:-1], refs[-1]
    recon = bias_ref[...]
    for term in terms:
        recon = recon + term[...].astype(F32)
    width = x_ref.shape[2]
    for r in range(x_ref.shape[0]):
        cols = slice(r * width, (r + 1) * width)
        out_ref[:, cols] = x_ref[r].astype(F32) - recon[:, cols]


def final_error(table, own_x, bias, terms):
    _, rows, width = own_x.shape
    share = bias.shape[1]
    part = pl.BlockSpec((rows, share // 2), lambda r, t: (0, r))
    return pl.pallas_call(
        error_body,
        grid_spec=pltpu.PrefetchScalarGridSpec(
            num_scalar_prefetch=1,
            grid=(2,),
            in_specs=[
                pl.BlockSpec(
                    (share // width // 2, rows, width), lambda r, t: (2 * t[2] + r, 0, 0)
                ),
                pl.BlockSpec((1, share // 2), lambda r, t: (0, r)),
            ]
            + [part] * len(terms),
            out_specs=part,
        ),
        out_shape=jax.ShapeDtypeStruct((rows, share), F32),
        compiler_params=PARAMS,
        cost_estimate=LIGHT,
        name="final_error",
    )(table, own_x, bias, *terms)


def line_program(resid, resid_grad, active, w_enc, b_enc, w_dec, b_dec):
    n_tok, n_feat = lax.axis_size("tok"), lax.axis_size("feat")
    i, j = lax.axis_index("tok"), lax.axis_index("feat")
    chips = n_feat // 2
    chip, core = j // 2, j % 2
    width = resid.shape[1]
    rows = resid.shape[0] // n_tok
    feats = w_enc.shape[1]
    share = n_tok * width

    def along(pairs):
        return [(2 * a + c, 2 * b + c) for a, b in pairs for c in range(2)]

    def send(array, pairs):
        return lax.ppermute(array, "feat", along(pairs))

    def cross(array):
        return lax.ppermute(array, "feat", [(a, a ^ 1) for a in range(n_feat)])

    def exchange(array, streams):
        def block(s):
            mine = lax.dynamic_slice_in_dim(array, (i ^ s) * rows, rows, 0)
            if s == 0:
                return mine
            return lax.ppermute(mine, "tok", [(a, a ^ s) for a in range(n_tok)])

        blocks = [block(s) for s in range(n_tok)]
        return [jnp.stack([blocks[s] for s in stream]) for stream in streams]

    own_sub = i ^ (j // (n_feat // n_tok))

    def numbers(*values):
        return jnp.stack([jnp.asarray(v).astype(jnp.int32) for v in values])

    def table(*steps):
        sources = [2 * ((chip + chips - k) % chips) + (core ^ side) for k in steps for side in (0, 1)]
        return numbers(i, own_sub, *sources)

    own_table = numbers(i, own_sub, j % (n_feat // n_tok))
    blocks = feats // BLOCK
    block_ids = j * blocks + jnp.arange(blocks, dtype=jnp.int32)
    hits = jnp.any(active[:, :, None] == block_ids[None, None, :], axis=1).astype(F32)
    hit = jnp.repeat(hits, BLOCK, axis=1)
    bias = b_enc.reshape(1, feats)
    b_row = b_dec.reshape(1, share)
    w4 = w_enc.reshape(n_tok, n_feat, width, feats)

    shard_x = exchange(resid, X_STREAMS)
    shard_g = exchange(resid_grad, G_STREAMS)

    ring = [(a, (a + 1) % chips) for a in range(chips)]
    near_x = [shard_x]
    far_x = [[cross(a) for a in shard_x]]
    carry = None
    for k in range(1, chips):
        first, rest = near_x[-1]
        first = send(first, ring)
        rest = after(rest, first)
        if k == 2:
            rest = after(rest, *shard_g)
        if k == 3:
            slots = [near_x[0], far_x[0], near_x[1], far_x[1]]
            carry = encode(table(0, 1), slots, w4, bias, hit, None, X_STREAMS, False)
            rest = after(rest, carry)
        near_x.append([first, send(rest, ring)])
        far_x.append([cross(a) for a in near_x[-1]])
    slots = [near_x[2], far_x[2], near_x[3], far_x[3]]
    acts, own_x = encode(table(2, 3), slots, w4, bias, hit, carry, X_STREAMS, True)

    shard_g = after(shard_g[0], near_x[-1])
    rows_g = lax.all_gather(shard_g, "feat", axis=0)

    order = (3, 2, 1, 0)
    dests = [2 * (chip ^ k) + (1 - core if side == 0 else core) for k in order for side in (0, 1)]
    outs = decode(numbers(*dests), acts, w_dec, share, len(dests))
    parts = {k: (outs[2 * n + 1], cross(outs[2 * n])) for n, k in enumerate(order)}

    def pair_sum(k):
        return parts[k][0].astype(F32) + parts[k][1].astype(F32)

    up_pairs = [(a, a + 1) for a in range(chips - 1)]
    down_pairs = [(a + 1, a) for a in range(chips - 1)]
    sum_3, sum_1 = pair_sum(3), pair_sum(1)
    come = send(sum_3.astype(BF16), [(0, 1), (3, 2)])
    going = (pair_sum(2) + come.astype(F32)).astype(BF16)
    up = send(going, up_pairs[:2])
    down = send(going, down_pairs[1:])
    going_up = (jnp.where(chip == 1, sum_3, sum_1) + up.astype(F32)).astype(BF16)
    going_down = (jnp.where(chip == 2, sum_3, sum_1) + down.astype(F32)).astype(BF16)
    up = send(going_up, up_pairs)
    down = send(going_down, down_pairs)

    feature_attr, attr = project(own_table, rows_g, w_dec, acts, own_x, b_row)
    attr = attr.reshape(-1, TILE)
    reach = 1
    while reach < n_feat:
        attr = attr + lax.ppermute(attr, "feat", [(a, a ^ reach) for a in range(n_feat)])
        reach *= 2

    error = final_error(own_table, own_x, b_row, [*parts[0], up, down])
    return feature_attr, error, attr.reshape(rows)


def gathered_program(resid, resid_grad, active, w_enc, b_enc, w_dec, b_dec):
    n_tok = lax.axis_size("tok")
    n_feat = lax.axis_size("feat")
    width = resid.shape[1]

    def rows_of(array):
        part = lax.all_to_all(array, "tok", split_axis=0, concat_axis=1, tiled=True)
        part = part.reshape(part.shape[0], n_tok, 1, width)
        part = lax.all_gather(part, "feat", axis=2, tiled=True)
        return part.reshape(part.shape[0], n_tok * n_feat * width)

    rows_x, rows_g = rows_of(resid), rows_of(resid_grad)
    tok_rows = rows_x.shape[0]
    feat_dev = w_enc.shape[1]
    blocks = feat_dev // BLOCK
    tiles_dev = active.shape[0]
    block_ids = lax.axis_index("feat") * blocks + jnp.arange(blocks, dtype=jnp.int32)
    hits = jnp.any(active[:, :, None] == block_ids[None, None, :], axis=1).astype(F32)
    pre = jnp.dot(rows_x, w_enc, preferred_element_type=F32) + b_enc
    shaped = jnp.maximum(pre, 0.0).reshape(tiles_dev, TILE, blocks, BLOCK) * hits[:, None, :, None]
    acts = shaped.reshape(tok_rows, feat_dev).astype(BF16)
    partial_recon = jnp.dot(acts, w_dec, preferred_element_type=F32)
    recon_share = lax.psum_scatter(
        partial_recon.astype(BF16), "feat", scatter_dimension=1, tiled=True
    ).astype(F32)
    share = recon_share.shape[1]
    start = lax.axis_index("feat") * share
    own_x = lax.dynamic_slice_in_dim(rows_x, start, share, 1)
    own_g = lax.dynamic_slice_in_dim(rows_g, start, share, 1)
    recon = recon_share + b_dec
    error = own_x.astype(F32) - recon
    local_sums = jnp.sum(error * own_g.astype(F32), axis=1)
    error_attr = lax.psum(local_sums, "feat")
    proj = lax.dot_general(rows_g, w_dec, (((1,), (1,)), ((), ())), preferred_element_type=F32)
    return acts.astype(F32) * proj, error, error_attr


def per_device(resid, *rest):
    fits = resid.shape[1] % 128 == 0 and lax.axis_size("tok") == 4 and lax.axis_size("feat") == 8
    return (line_program if fits else gathered_program)(resid, *rest)


def solution(mesh):
    placed = (
        P(None, ("tok", "feat")),
        P(None, ("tok", "feat")),
        P("tok", None),
        P(None, "feat"),
        P("feat"),
        P("feat", None),
        P("feat"),
    )
    return jax.shard_map(
        per_device,
        mesh=mesh,
        in_specs=placed,
        out_specs=(P("tok", "feat"), P("tok", "feat"), P("tok")),
        check_vma=False,
    )
```

```python
import functools

import jax
import jax.numpy as jnp
from jax import lax
from jax.experimental import pallas as pl
from jax.experimental.pallas import tpu as pltpu
from jax.sharding import PartitionSpec as P

BLOCK = 128
TILE = 128
X_STREAMS = ((0,), (1, 2), (3,))
G_STREAMS = ((0, 1, 2, 3),)
PARAMS = pltpu.CompilerParams(vmem_limit_bytes=56 << 20)
F32 = jnp.float32
BF16 = jnp.bfloat16
LIGHT = pl.CostEstimate(flops=1, bytes_accessed=1, transcendentals=0)


def whole(shape):
    zeros = (0,) * len(shape)
    return pl.BlockSpec(shape, lambda *_: zeros)


def after(value, *others):
    return lax.optimization_barrier((value, others))[0]


def pieces(refs, streams):
    return [refs[a].at[b] for a, stream in enumerate(streams) for b in range(len(stream))]


def cost(rows, depth, feats):
    return pl.CostEstimate(
        flops=2 * rows * depth * feats, bytes_accessed=2 * depth * (rows + feats), transcendentals=0
    )


def enc_body(streams, count, first, last, table, *refs):
    size = len(streams)
    slots = [pieces(refs[q * size:(q + 1) * size], streams) for q in range(count)]
    w_ref, bias_ref, hit_ref = refs[count * size:count * size + 3]
    refs = refs[count * size + 3:]
    carry_ref = None
    if not first:
        carry_ref, refs = refs[0], refs[2:]
    out_ref, own_ref, x_ref = refs[:3]
    total_ref = refs[3] if last else out_ref
    step = pl.program_id(0)
    n_tok, _, width, feats = w_ref.shape
    for q, blocks in enumerate(slots):

        @pl.when(step == q)
        def _():
            for s, x in enumerate(blocks):
                x_ref[:, pl.ds(pl.multiple_of((table[0] ^ s) * width, width), width)] = x[...]

    total = jnp.dot(
        x_ref[...], w_ref[...].reshape(n_tok * width, feats), preferred_element_type=F32
    )

    @pl.when(step == 0)
    def _():
        total_ref[...] = total if first else total + carry_ref[...]

    @pl.when(step > 0)
    def _():
        total_ref[...] += total

    own_ref[0] = x_ref[:, pl.ds(pl.multiple_of(table[1] * width, width), width)]
    if last:

        @pl.when(step == count - 1)
        def _():
            pre = total_ref[...] + bias_ref[...]
            tiles = hit_ref.shape[0]
            shaped = jnp.maximum(pre, 0.0).reshape(tiles, TILE, -1) * hit_ref[...][:, None, :]
            out_ref[...] = shaped.reshape(pre.shape).astype(BF16)


def encode(table, slots, w4, bias, hit, carry, streams, last):
    n_tok, n_feat, width, feats = w4.shape
    rows = slots[0][0].shape[1]
    first = carry is None
    flat = [a for slot in slots for a in slot]
    specs = [whole(a.shape) for a in flat]
    specs += [
        pl.BlockSpec((n_tok, 1, width, feats), lambda q, t: (0, t[2 + q], 0, 0)),
        whole(bias.shape),
        whole(hit.shape),
    ]
    args = [*flat, w4, bias, hit]
    aliases = {}
    if not first:
        specs += [whole(carry[0].shape), pl.BlockSpec(memory_space=pl.ANY)]
        args += carry
        aliases = {len(args): 1}
    count = len(slots)
    scratch = [pltpu.VMEM((rows, n_tok * width), BF16)]
    return pl.pallas_call(
        functools.partial(enc_body, streams, count, first, last),
        grid_spec=pltpu.PrefetchScalarGridSpec(
            num_scalar_prefetch=1,
            grid=(count,),
            in_specs=specs,
            out_specs=[
                whole((rows, feats)),
                pl.BlockSpec((1, rows, width), lambda q, t: (t[2 + q], 0, 0)),
            ],
            scratch_shapes=scratch + ([pltpu.VMEM((rows, feats), F32)] if last else []),
        ),
        out_shape=[
            jax.ShapeDtypeStruct((rows, feats), BF16 if last else F32),
            jax.ShapeDtypeStruct((n_feat, rows, width), BF16),
        ],
        input_output_aliases=aliases,
        compiler_params=PARAMS,
        cost_estimate=LIGHT if last else cost(rows, count * n_tok * width, feats),
        name="encode",
    )(table, *args)


def dec_body(table, acts_ref, w_ref, *out_refs):
    for q, out_ref in enumerate(out_refs):

        @pl.when(pl.program_id(0) == q)
        def _():
            out_ref[...] = jnp.dot(
                acts_ref[...], w_ref[...], preferred_element_type=F32
            ).astype(BF16)


def decode(table, acts, w_dec, share, count):
    rows, feats = acts.shape
    outs = [jax.ShapeDtypeStruct((rows, share), BF16)] * count
    return pl.pallas_call(
        dec_body,
        grid_spec=pltpu.PrefetchScalarGridSpec(
            num_scalar_prefetch=1,
            grid=(count,),
            in_specs=[whole(acts.shape), pl.BlockSpec((feats, share), lambda q, t: (0, t[q]))],
            out_specs=[whole(out.shape) for out in outs],
        ),
        out_shape=outs,
        compiler_params=PARAMS,
        cost_estimate=LIGHT,
        name="decode",
    )(table, acts, w_dec)


def proj_body(count, n_tok, first, last, table, *refs):
    slots, w_refs, acts_ref = refs[:count], refs[count:count + n_tok], refs[count + n_tok]
    refs = refs[count + n_tok + 1:]
    carry_ref = None
    if not first:
        carry_ref, refs = refs[0], refs[2:]
    out_ref, own_ref = refs[:2]
    step = pl.program_id(0)
    for q, g_ref in enumerate(slots):

        @pl.when((step == q) & (table[3 + 2 * q] == 1))
        def _():
            total = lax.dot_general(
                jnp.concatenate([g_ref[s] for s in range(n_tok)], axis=1),
                jnp.concatenate([w_ref[...] for w_ref in w_refs], axis=1),
                (((1,), (1,)), ((), ())),
                preferred_element_type=F32,
            )
            if q > 0:
                total = total + out_ref[...]
            elif not first:
                total = total + carry_ref[...]
            out_ref[...] = total
            own_ref[0] = g_ref[table[1]]

    if last:

        @pl.when(step == count - 1)
        def _():
            attr = acts_ref[...].astype(F32) * out_ref[...]
            out_ref[...] = attr
            refs[2][...] = jnp.sum(attr, axis=1, keepdims=True)


def project(table, slots, w_dec, acts, carry, last, n_feat):
    n_tok, rows, width = slots[0].shape
    feats = w_dec.shape[0]
    first = carry is None
    specs = [whole(a.shape) for a in slots]
    for s in range(n_tok):
        specs.append(
            pl.BlockSpec((feats, width), lambda q, t, s=s: (0, (t[0] ^ s) * n_feat + t[2 + 2 * q]))
        )
    specs.append(whole(acts.shape))
    args = [*slots] + [w_dec] * n_tok + [acts]
    aliases = {}
    if not first:
        specs += [whole(carry[0].shape), pl.BlockSpec(memory_space=pl.ANY)]
        args += carry
        aliases = {len(args): 1}
    out_specs = [
        whole((rows, feats)),
        pl.BlockSpec((1, rows, width), lambda q, t: (t[2 + 2 * q], 0, 0)),
    ]
    out_shape = [
        jax.ShapeDtypeStruct((rows, feats), F32),
        jax.ShapeDtypeStruct((n_feat, rows, width), BF16),
    ]
    if last:
        out_specs.append(whole((rows, 1)))
        out_shape.append(jax.ShapeDtypeStruct((rows, 1), F32))
    count = len(slots)
    return pl.pallas_call(
        functools.partial(proj_body, count, n_tok, first, last),
        grid_spec=pltpu.PrefetchScalarGridSpec(
            num_scalar_prefetch=1, grid=(count,), in_specs=specs, out_specs=out_specs
        ),
        out_shape=out_shape,
        input_output_aliases=aliases,
        compiler_params=PARAMS,
        cost_estimate=LIGHT if last else cost(rows, count * n_tok * width, feats),
        name="project",
    )(table, *args)


def local_body(table, x_ref, g_ref, bias_ref, fa_ref, out_ref):
    total = -fa_ref[...]
    width = x_ref.shape[2]
    for r in range(x_ref.shape[0]):
        term = x_ref[r].astype(F32) - bias_ref[:, r * width:(r + 1) * width]
        total += jnp.sum(term * g_ref[r].astype(F32), axis=1, keepdims=True)
    out_ref[...] = total


def local_terms(table, own_x, own_g, bias, fa_sum):
    _, rows, width = own_x.shape
    picked = pl.BlockSpec((bias.shape[1] // width, rows, width), lambda r, t: (t[0], 0, 0))
    return pl.pallas_call(
        local_body,
        grid_spec=pltpu.PrefetchScalarGridSpec(
            num_scalar_prefetch=1,
            grid=(1,),
            in_specs=[picked, picked, whole(bias.shape), whole((rows, 1))],
            out_specs=whole((rows, 1)),
        ),
        out_shape=jax.ShapeDtypeStruct((rows, 1), F32),
        compiler_params=PARAMS,
        cost_estimate=LIGHT,
        name="local_terms",
    )(table, own_x, own_g, bias, fa_sum)


def error_body(table, x_ref, bias_ref, *refs):
    terms, out_ref = refs[:-1], refs[-1]
    recon = bias_ref[...]
    for term in terms:
        recon = recon + term[...].astype(F32)
    width = x_ref.shape[2]
    for r in range(x_ref.shape[0]):
        cols = slice(r * width, (r + 1) * width)
        out_ref[:, cols] = x_ref[r].astype(F32) - recon[:, cols]


def final_error(table, own_x, bias, terms):
    _, rows, width = own_x.shape
    share = bias.shape[1]
    part = pl.BlockSpec((rows, share // 2), lambda r, t: (0, r))
    return pl.pallas_call(
        error_body,
        grid_spec=pltpu.PrefetchScalarGridSpec(
            num_scalar_prefetch=1,
            grid=(2,),
            in_specs=[
                pl.BlockSpec(
                    (share // width // 2, rows, width), lambda r, t: (2 * t[0] + r, 0, 0)
                ),
                pl.BlockSpec((1, share // 2), lambda r, t: (0, r)),
            ]
            + [part] * len(terms),
            out_specs=part,
        ),
        out_shape=jax.ShapeDtypeStruct((rows, share), F32),
        compiler_params=PARAMS,
        cost_estimate=LIGHT,
        name="final_error",
    )(table, own_x, bias, *terms)


def line_program(resid, resid_grad, active, w_enc, b_enc, w_dec, b_dec):
    n_tok, n_feat = lax.axis_size("tok"), lax.axis_size("feat")
    i, j = lax.axis_index("tok"), lax.axis_index("feat")
    chips = n_feat // 2
    chip, core = j // 2, j % 2
    width = resid.shape[1]
    rows = resid.shape[0] // n_tok
    feats = w_enc.shape[1]
    share = n_tok * width

    def along(pairs):
        return [(2 * a + c, 2 * b + c) for a, b in pairs for c in range(2)]

    def send(array, pairs):
        return lax.ppermute(array, "feat", along(pairs))

    def cross(array):
        return lax.ppermute(array, "feat", [(a, a ^ 1) for a in range(n_feat)])

    def exchange(array, streams):
        def block(s):
            mine = lax.dynamic_slice_in_dim(array, (i ^ s) * rows, rows, 0)
            if s == 0:
                return mine
            return lax.ppermute(mine, "tok", [(a, a ^ s) for a in range(n_tok)])

        blocks = [block(s) for s in range(n_tok)]
        return [jnp.stack([blocks[s] for s in stream]) for stream in streams]

    own_tok = j // (n_feat // n_tok)

    def numbers(*values):
        return jnp.stack([jnp.asarray(v).astype(jnp.int32) for v in values])

    def table(*steps):
        sources = [2 * ((chip + chips - k) % chips) + (core ^ side) for k in steps for side in (0, 1)]
        return numbers(i, own_tok, *sources)

    def line_table(*sources):
        values, seen = [i, i ^ own_tok], 0
        for place, valid in sources:
            seen = jnp.where(valid, place, seen)
            for side in (0, 1):
                values += [2 * seen + (core ^ side), valid]
        return numbers(*values)

    own_start = numbers(j % (n_feat // n_tok))
    blocks = feats // BLOCK
    block_ids = j * blocks + jnp.arange(blocks, dtype=jnp.int32)
    hits = jnp.any(active[:, :, None] == block_ids[None, None, :], axis=1).astype(F32)
    hit = jnp.repeat(hits, BLOCK, axis=1)
    bias = b_enc.reshape(1, feats)
    b_row = b_dec.reshape(1, share)
    w4 = w_enc.reshape(n_tok, n_feat, width, feats)

    shard_x = exchange(resid, X_STREAMS)

    ring = [(a, (a + 1) % chips) for a in range(chips)]
    near_x = [shard_x]
    far_x = [[cross(a) for a in shard_x]]
    for k in range(1, chips):
        held = near_x[-1]
        if k == 3:
            slots = [near_x[0], far_x[0], near_x[1], far_x[1]]
            carry = encode(table(0, 1), slots, w4, bias, hit, None, X_STREAMS, False)
            held = [*held[:-1], after(held[-1], shard_g, carry)]
        near_x.append([send(a, ring) for a in held])
        far_x.append([cross(a) for a in near_x[-1]])
        if k == 2:
            shard_g, = exchange(after(resid_grad, near_x[2][0]), G_STREAMS)

    up_pairs = [(a, a + 1) for a in range(chips - 1)]
    down_pairs = [(a + 1, a) for a in range(chips - 1)]
    shard_g = after(shard_g, near_x[-1])
    up_1, down_1 = send(shard_g, up_pairs), send(shard_g, down_pairs)

    slots = [near_x[2], far_x[2], near_x[3], far_x[3]]
    acts, own_x = encode(table(2, 3), slots, w4, bias, hit, carry, X_STREAMS, True)

    parts = {}
    far_3, near_3 = decode(
        numbers(2 * (chip ^ 3) + 1 - core, 2 * (chip ^ 3) + core), acts, w_dec, share, 2
    )
    up_1, down_1 = after((up_1, down_1), far_3)
    parts[3] = (near_3, cross(far_3))
    acts = after(acts, far_3)
    for k in (2, 1, 0):
        far_out, near_out = [
            jnp.dot(
                acts,
                lax.dynamic_slice_in_dim(w_dec, (2 * (chip ^ k) + place) * share, share, 1),
                preferred_element_type=F32,
            ).astype(BF16)
            for place in (1 - core, core)
        ]
        parts[k] = (near_out, cross(far_out))

    def pair_sum(k):
        return parts[k][0].astype(F32) + parts[k][1].astype(F32)

    sum_3, sum_1 = pair_sum(3), pair_sum(1)
    come = send(sum_3.astype(BF16), [(0, 1), (3, 2)])
    up_2, down_2 = send(up_1, up_pairs[1:]), send(down_1, down_pairs[:-1])
    two_g = up_2 + down_2
    three_g = send(two_g, [(2, 3), (1, 0)])

    going = (pair_sum(2) + come.astype(F32)).astype(BF16)
    up = send(going, up_pairs[:2])
    down = send(going, down_pairs[1:])

    slots = [shard_g, cross(shard_g), up_1, cross(up_1), down_1, cross(down_1)]
    sources = line_table((chip, True), (chip - 1, chip >= 1), (chip + 1, chip <= chips - 2))
    acts = after(acts, going)
    carry = project(sources, slots, w_dec, acts, None, False, n_feat)

    going_up = (jnp.where(chip == 1, sum_3, sum_1) + up.astype(F32)).astype(BF16)
    going_down = (jnp.where(chip == 2, sum_3, sum_1) + down.astype(F32)).astype(BF16)
    going_up, going_down = after((going_up, going_down), carry, parts[0])
    up = send(going_up, up_pairs)
    down = send(going_down, down_pairs)

    slots = [two_g, cross(two_g), three_g, cross(three_g)]
    sources = line_table((chip ^ 2, True), (chip ^ 3, (chip == 0) | (chip == chips - 1)))
    acts = after(acts, going_up, going_down)
    feature_attr, own_g, fa_sum = project(sources, slots, w_dec, acts, carry, True, n_feat)
    attr = local_terms(own_start, own_x, own_g, b_row, fa_sum).reshape(-1, TILE)
    attr = attr + cross(attr)
    others = [send(attr, [(a, a ^ k) for a in range(chips)]) for k in range(1, chips)]
    for other in others:
        attr = attr + other

    error = final_error(own_start, own_x, b_row, [*parts[0], up, down])
    return feature_attr, error, attr.reshape(rows)


def gathered_program(resid, resid_grad, active, w_enc, b_enc, w_dec, b_dec):
    n_tok = lax.axis_size("tok")
    n_feat = lax.axis_size("feat")
    width = resid.shape[1]

    def rows_of(array):
        part = lax.all_to_all(array, "tok", split_axis=0, concat_axis=1, tiled=True)
        part = part.reshape(part.shape[0], n_tok, 1, width)
        part = lax.all_gather(part, "feat", axis=2, tiled=True)
        return part.reshape(part.shape[0], n_tok * n_feat * width)

    rows_x, rows_g = rows_of(resid), rows_of(resid_grad)
    tok_rows = rows_x.shape[0]
    feat_dev = w_enc.shape[1]
    blocks = feat_dev // BLOCK
    tiles_dev = active.shape[0]
    block_ids = lax.axis_index("feat") * blocks + jnp.arange(blocks, dtype=jnp.int32)
    hits = jnp.any(active[:, :, None] == block_ids[None, None, :], axis=1).astype(F32)
    pre = jnp.dot(rows_x, w_enc, preferred_element_type=F32) + b_enc
    shaped = jnp.maximum(pre, 0.0).reshape(tiles_dev, TILE, blocks, BLOCK) * hits[:, None, :, None]
    acts = shaped.reshape(tok_rows, feat_dev).astype(BF16)
    partial_recon = jnp.dot(acts, w_dec, preferred_element_type=F32)
    recon_share = lax.psum_scatter(
        partial_recon.astype(BF16), "feat", scatter_dimension=1, tiled=True
    ).astype(F32)
    share = recon_share.shape[1]
    start = lax.axis_index("feat") * share
    own_x = lax.dynamic_slice_in_dim(rows_x, start, share, 1)
    own_g = lax.dynamic_slice_in_dim(rows_g, start, share, 1)
    recon = recon_share + b_dec
    error = own_x.astype(F32) - recon
    local_sums = jnp.sum(error * own_g.astype(F32), axis=1)
    error_attr = lax.psum(local_sums, "feat")
    proj = lax.dot_general(rows_g, w_dec, (((1,), (1,)), ((), ())), preferred_element_type=F32)
    return acts.astype(F32) * proj, error, error_attr


def per_device(resid, *rest):
    fits = resid.shape[1] % 128 == 0 and lax.axis_size("tok") == 4 and lax.axis_size("feat") == 8
    return (line_program if fits else gathered_program)(resid, *rest)


def solution(mesh):
    placed = (
        P(None, ("tok", "feat")),
        P(None, ("tok", "feat")),
        P("tok", None),
        P(None, "feat"),
        P("feat"),
        P("feat", None),
        P("feat"),
    )
    return jax.shard_map(
        per_device,
        mesh=mesh,
        in_specs=placed,
        out_specs=(P("tok", "feat"), P("tok", "feat"), P("tok")),
        check_vma=False,
    )
```

```python
import functools

import jax
import jax.numpy as jnp
from jax import lax
from jax.experimental import pallas as pl
from jax.experimental.pallas import tpu as pltpu
from jax.sharding import PartitionSpec as P

BLOCK = 128
TILE = 128
X_STREAMS = ((0,), (1, 2), (3,))
PIECES = 8
PARAMS = pltpu.CompilerParams(vmem_limit_bytes=24 << 20)
F32 = jnp.float32
BF16 = jnp.bfloat16
LIGHT = pl.CostEstimate(flops=1, bytes_accessed=1, transcendentals=0)
VMEM = pl.BlockSpec(memory_space=pltpu.VMEM)
SMEM = pl.BlockSpec(memory_space=pltpu.SMEM)


def cost(flops, moved):
    return pl.CostEstimate(flops=flops, bytes_accessed=moved, transcendentals=0)


def after(value, *others):
    return lax.optimization_barrier((value, others))[0]


def kernel_call(body, outs, args, name, hint=LIGHT, scratch=()):
    return pl.pallas_call(
        body,
        in_specs=[SMEM] + [VMEM] * (len(args) - 1),
        out_specs=[VMEM] * len(outs),
        out_shape=[jax.ShapeDtypeStruct(shape, kind) for shape, kind in outs],
        scratch_shapes=list(scratch),
        compiler_params=PARAMS,
        cost_estimate=hint,
        name=name,
    )(*args)


def load_body(w_ref, through_ref, out_ref, same_ref, sems):
    step = w_ref.shape[0] // PIECES
    copies = []
    for n in range(PIECES):
        part = pl.ds(n * step, step)
        copies.append(pltpu.make_async_copy(w_ref.at[part], out_ref.at[part], sems.at[n]))
    for copy in copies:
        copy.start()
    for copy in copies:
        copy.wait()


def load(w, through, room):
    anywhere = pl.BlockSpec(memory_space=pl.ANY)
    return pl.pallas_call(
        load_body,
        in_specs=[anywhere, anywhere],
        out_specs=[VMEM, anywhere],
        out_shape=[
            pltpu.VMEM(w.shape, w.dtype),
            jax.ShapeDtypeStruct(through.shape, through.dtype),
        ],
        scratch_shapes=[pltpu.SemaphoreType.DMA((PIECES,))],
        input_output_aliases={1: 1},
        compiler_params=pltpu.CompilerParams(vmem_limit_bytes=room << 20),
        cost_estimate=cost(0, 2 * w.size),
        name="load",
    )(w, through)


FIXED = 3


def pieces(refs, streams):
    return [refs[a].at[b] for a, stream in enumerate(streams) for b in range(len(stream))]


def aligned(index, width):
    return pl.ds(pl.multiple_of(index * width, width), width)


def enc_body(streams, count, first, last, n_feat, at, table, *refs):
    size = len(streams)
    slots = [pieces(refs[q * size:(q + 1) * size], streams) for q in range(count)]
    w_ref, bias_ref, hit_ref = refs[count * size:count * size + 3]
    refs = refs[count * size + 3:]
    carry_ref = None
    if not first:
        carry_ref, seen_ref, refs = refs[0], refs[1], refs[2:]
    out_ref, own_ref = refs[:2]
    total_ref = refs[2] if last else out_ref
    n_tok, width = len(slots[0]), slots[0][0].shape[1]
    if not first:
        own_ref[...] = seen_ref[...]
    for q, blocks in enumerate(slots):
        source = table[at + q]
        total = carry_ref if q == 0 else total_ref
        total = None if total is None else total[...]
        for s, x in enumerate(blocks):
            w = w_ref[(table[0] ^ s) * n_feat + source]
            term = jnp.dot(x[...], w, preferred_element_type=F32)
            total = term if total is None else total + term
        total_ref[...] = total
        for s, x in enumerate(blocks):

            @pl.when(((table[0] ^ s) == table[1]) & (source // n_tok == table[2]))
            def _():
                own_ref[:, aligned(source % n_tok, width)] = x[...]

    if last:
        pre = total_ref[...] + bias_ref[...]
        tiles = hit_ref.shape[0]
        shaped = jnp.maximum(pre, 0.0).reshape(tiles, TILE, -1) * hit_ref[...][:, None, :]
        out_ref[...] = shaped.reshape(pre.shape).astype(BF16)


def encode(table, at, slots, w, bias, hit, carry, streams, last, n_feat):
    width, feats = w.shape[1:]
    rows = slots[0][0].shape[1]
    n_tok = w.shape[0] // n_feat
    args = [table] + [a for slot in slots for a in slot] + [w, bias, hit]
    if carry is not None:
        args += carry
    return kernel_call(
        functools.partial(enc_body, streams, len(slots), carry is None, last, n_feat, at),
        [((rows, feats), BF16 if last else F32), ((rows, n_tok * width), BF16)],
        args,
        "encode",
        LIGHT if last else cost(2 * len(slots) * rows * n_tok * width * feats, 4 << 20),
        [pltpu.VMEM((rows, feats), F32)] if last else [],
    )


def dec_body(at, table, acts_ref, w_ref, *out_refs):
    share = out_refs[0].shape[1]
    for q, out_ref in enumerate(out_refs):
        w = w_ref[:, aligned(table[at + q], share)]
        out_ref[...] = jnp.dot(acts_ref[...], w, preferred_element_type=F32).astype(BF16)


def decode(table, at, acts, w, share, count, hint):
    outs = [((acts.shape[0], share), BF16)] * count
    return kernel_call(functools.partial(dec_body, at), outs, [table, acts, w], "decode", hint)


def proj_body(count, first, last, n_feat, at, table, *refs):
    slots, refs = refs[:count], refs[count:]
    w_ref, acts_ref, x_ref, bias_ref = refs[:4]
    refs = refs[4:]
    if not first:
        carry_ref, seen_ref, refs = refs[0], refs[1], refs[2:]
    out_ref, sum_ref = refs[:2]
    if last:
        out_ref, line_ref, sum_ref = refs
    if first:
        sum_ref[...] = jnp.zeros_like(sum_ref)
    else:
        sum_ref[...] = seen_ref[...]
    for q, g_ref in enumerate(slots):
        n_tok, _, width = g_ref.shape
        source, held = table[at + 2 * q], table[at + 2 * q + 1] == 1

        @pl.when(held)
        def _():
            total = None if q == 0 and first else (carry_ref if q == 0 else out_ref)[...]
            for s in range(n_tok):
                w = w_ref[:, aligned((table[0] ^ s) * n_feat + source, width)]
                term = lax.dot_general(
                    g_ref[s], w, (((1,), (1,)), ((), ())), preferred_element_type=F32
                )
                total = term if total is None else total + term
            out_ref[...] = total

        @pl.when(held & (source // n_tok == table[2]))
        def _():
            cols = aligned(source % n_tok, width)
            term = x_ref[:, cols].astype(F32) - bias_ref[:, cols]
            term = term * g_ref[table[0] ^ table[1]].astype(F32)
            sum_ref[...] += jnp.sum(term, axis=1, keepdims=True)

    if last:
        attr = acts_ref[...].astype(F32) * out_ref[...]
        out_ref[...] = attr
        total = sum_ref[...] - jnp.sum(attr, axis=1, keepdims=True)
        line_ref[...] = jnp.broadcast_to(total, (total.shape[0], TILE)).T[:8]


def project(table, at, slots, w, acts, own_x, bias, carry, last, n_feat):
    rows, feats = acts.shape
    outs = [((rows, feats), F32), ((8, rows), F32) if last else ((rows, 1), F32)]
    return kernel_call(
        functools.partial(proj_body, len(slots), carry is None, last, n_feat, at),
        outs,
        [table, *slots, w, acts, own_x, bias, *(carry or [])],
        "project",
        LIGHT if last else cost(2 * len(slots) * slots[0].size * feats, 4 << 20),
        [pltpu.VMEM((rows, 1), F32)] if last else [],
    )


def line_program(resid, resid_grad, active, w_enc, b_enc, w_dec, b_dec):
    n_tok, n_feat = lax.axis_size("tok"), lax.axis_size("feat")
    i, j = lax.axis_index("tok"), lax.axis_index("feat")
    chips = n_feat // 2
    chip, core = j // 2, j % 2
    width = resid.shape[1]
    rows = resid.shape[0] // n_tok
    feats = w_enc.shape[1]
    share = n_tok * width

    def along(pairs):
        return [(2 * a + c, 2 * b + c) for a, b in pairs for c in range(2)]

    def send(array, pairs):
        return lax.ppermute(array, "feat", along(pairs))

    def cross(array):
        return lax.ppermute(array, "feat", [(a, a ^ 1) for a in range(n_feat)])

    def exchange(array, streams):
        def block(s):
            mine = lax.dynamic_slice_in_dim(array, (i ^ s) * rows, rows, 0)
            if s == 0:
                return mine
            return lax.ppermute(mine, "tok", [(a, a ^ s) for a in range(n_tok)])

        blocks = [block(s) for s in range(n_tok)]
        return [jnp.stack([blocks[s] for s in stream]) for stream in streams]

    def both_cores(place):
        return [2 * place + core, 2 * place + 1 - core]

    def held_slots(*sources):
        values, seen = [], 0
        for place, valid in sources:
            seen = jnp.where(valid, place, seen)
            for source in both_cores(seen):
                values += [source, valid]
        return values

    numbers = [i, j // (n_feat // n_tok), j % (n_feat // n_tok)]
    at = []
    for values in (
        both_cores(chip) + both_cores((chip + chips - 1) % chips),
        both_cores((chip + chips - 2) % chips) + both_cores((chip + chips - 3) % chips),
        both_cores(chip ^ 3)[::-1],
        both_cores(chip ^ 2)[::-1] + both_cores(chip ^ 1)[::-1] + both_cores(chip)[::-1],
        held_slots((chip, True), (chip - 1, chip >= 1), (chip + 1, chip <= chips - 2)),
        held_slots((chip ^ 2, True), (chip ^ 3, (chip == 0) | (chip == chips - 1))),
    ):
        at.append(len(numbers))
        numbers += values
    table = jnp.stack([jnp.asarray(n).astype(jnp.int32) for n in numbers])

    blocks = feats // BLOCK
    block_ids = j * blocks + jnp.arange(blocks, dtype=jnp.int32)
    hits = jnp.any(active[:, :, None] == block_ids[None, None, :], axis=1).astype(F32)
    hit = jnp.repeat(hits, BLOCK, axis=1)
    bias = b_enc.reshape(1, feats)
    b_row = b_dec.reshape(1, share)

    ring = [(a, (a + 1) % chips) for a in range(chips)]
    near_x = [exchange(resid, X_STREAMS)]
    w_in, near_x[0][2] = load(w_enc.reshape(n_tok * n_feat, width, feats), near_x[0][2], 46)
    far_x = [[cross(a) for a in near_x[0]]]
    carry = None
    for k in range(1, chips):
        held = near_x[-1]
        if k == 2:
            w_out, held[2] = load(w_dec, held[2], 36)
        if k == 3:
            held = [held[0], held[1], after(held[2], shard_g)]
        near_x.append([send(a, ring) for a in held])
        if k == 2:
            shard_g, = exchange(after(resid_grad, near_x[2][0]), ((0, 1, 2, 3),))
        if k == 3:
            slots = [near_x[0], far_x[0], near_x[1], far_x[1]]
            carry = encode(
                table, at[0], slots, w_in, bias, hit, None, X_STREAMS, False, n_feat
            )
            late = after(near_x[3][2], carry)
            far_x.append([cross(near_x[3][0]), cross(near_x[3][1]), cross(late)])
        else:
            far_x.append([cross(a) for a in near_x[-1]])

    up_pairs = [(a, a + 1) for a in range(chips - 1)]
    down_pairs = [(a + 1, a) for a in range(chips - 1)]
    shard_g = after(shard_g, near_x[-1])
    up_1, down_1 = send(shard_g, up_pairs), send(shard_g, down_pairs)

    slots = [near_x[2], far_x[2], near_x[3], far_x[3]]
    acts, own_x = encode(table, at[1], slots, w_in, bias, hit, carry, X_STREAMS, True, n_feat)

    far_3, near_3 = decode(table, at[2], acts, w_out, share, 2, LIGHT)
    up_1, down_1 = after((up_1, down_1), far_3)
    parts = {3: (near_3, cross(far_3))}
    outs = decode(
        table, at[3], after(acts, far_3), w_out, share, 6, cost(12 * rows * feats * share, 4 << 20)
    )
    for n, k in enumerate((2, 1, 0)):
        parts[k] = (outs[2 * n + 1], cross(outs[2 * n]))

    def pair_sum(k):
        return parts[k][0].astype(F32) + parts[k][1].astype(F32)

    sum_3, sum_1 = pair_sum(3), pair_sum(1)
    come = send(sum_3.astype(BF16), [(0, 1), (3, 2)])
    up_2, down_2 = send(up_1, up_pairs[1:]), send(down_1, down_pairs[:-1])
    two_g = up_2 + down_2
    three_g = send(two_g, [(2, 3), (1, 0)])

    going = (pair_sum(2) + come.astype(F32)).astype(BF16)
    up = send(going, up_pairs[:2])
    down = send(going, down_pairs[1:])

    slots = [shard_g, cross(shard_g), up_1, cross(up_1), down_1, cross(down_1)]
    carry = project(
        table, at[4], slots, w_out, after(acts, going), own_x, b_row, None, False, n_feat
    )
    base = own_x.astype(F32) - b_row - pair_sum(0)

    going_up = (jnp.where(chip == 1, sum_3, sum_1) + up.astype(F32)).astype(BF16)
    going_down = (jnp.where(chip == 2, sum_3, sum_1) + down.astype(F32)).astype(BF16)
    going_up, going_down = after((going_up, going_down), carry, base)
    up = send(going_up, up_pairs)
    down = send(going_down, down_pairs)

    slots = [two_g, cross(two_g), three_g, cross(three_g)]
    feature_attr, attr = project(
        table, at[5], slots, w_out, after(acts, going_up, going_down), own_x, b_row, carry, True, n_feat
    )
    attr = attr[:1]
    attr = attr + cross(attr)
    others = [send(attr, [(a, a ^ k) for a in range(chips)]) for k in range(1, chips)]
    for other in others:
        attr = attr + other

    error = base - (up.astype(F32) + down.astype(F32))
    return feature_attr, error, attr.reshape(rows)


def gathered_program(resid, resid_grad, active, w_enc, b_enc, w_dec, b_dec):
    n_tok = lax.axis_size("tok")
    n_feat = lax.axis_size("feat")
    width = resid.shape[1]

    def rows_of(array):
        part = lax.all_to_all(array, "tok", split_axis=0, concat_axis=1, tiled=True)
        part = part.reshape(part.shape[0], n_tok, 1, width)
        part = lax.all_gather(part, "feat", axis=2, tiled=True)
        return part.reshape(part.shape[0], n_tok * n_feat * width)

    rows_x, rows_g = rows_of(resid), rows_of(resid_grad)
    tok_rows = rows_x.shape[0]
    feat_dev = w_enc.shape[1]
    blocks = feat_dev // BLOCK
    tiles_dev = active.shape[0]
    block_ids = lax.axis_index("feat") * blocks + jnp.arange(blocks, dtype=jnp.int32)
    hits = jnp.any(active[:, :, None] == block_ids[None, None, :], axis=1).astype(F32)
    pre = jnp.dot(rows_x, w_enc, preferred_element_type=F32) + b_enc
    shaped = jnp.maximum(pre, 0.0).reshape(tiles_dev, TILE, blocks, BLOCK) * hits[:, None, :, None]
    acts = shaped.reshape(tok_rows, feat_dev).astype(BF16)
    partial_recon = jnp.dot(acts, w_dec, preferred_element_type=F32)
    recon_share = lax.psum_scatter(
        partial_recon.astype(BF16), "feat", scatter_dimension=1, tiled=True
    ).astype(F32)
    share = recon_share.shape[1]
    start = lax.axis_index("feat") * share
    own_x = lax.dynamic_slice_in_dim(rows_x, start, share, 1)
    own_g = lax.dynamic_slice_in_dim(rows_g, start, share, 1)
    recon = recon_share + b_dec
    error = own_x.astype(F32) - recon
    local_sums = jnp.sum(error * own_g.astype(F32), axis=1)
    error_attr = lax.psum(local_sums, "feat")
    proj = lax.dot_general(rows_g, w_dec, (((1,), (1,)), ((), ())), preferred_element_type=F32)
    return acts.astype(F32) * proj, error, error_attr


def per_device(resid, *rest):
    fits = resid.shape[1] % 128 == 0 and lax.axis_size("tok") == 4 and lax.axis_size("feat") == 8
    return (line_program if fits else gathered_program)(resid, *rest)


def solution(mesh):
    placed = (
        P(None, ("tok", "feat")),
        P(None, ("tok", "feat")),
        P("tok", None),
        P(None, "feat"),
        P("feat"),
        P("feat", None),
        P("feat"),
    )
    return jax.shard_map(
        per_device,
        mesh=mesh,
        in_specs=placed,
        out_specs=(P("tok", "feat"), P("tok", "feat"), P("tok")),
        check_vma=False,
    )
```

```python
import functools

import jax
import jax.numpy as jnp
from jax import lax
from jax.experimental import pallas as pl
from jax.experimental.pallas import tpu as pltpu
from jax.sharding import PartitionSpec as P

BLOCK = 128
TILE = 128
X_STREAMS = ((0, 1), (2, 3))
PIECES = 8
PARAMS = pltpu.CompilerParams(vmem_limit_bytes=24 << 20)
F32 = jnp.float32
BF16 = jnp.bfloat16
LIGHT = pl.CostEstimate(flops=1, bytes_accessed=1, transcendentals=0)
VMEM = pl.BlockSpec(memory_space=pltpu.VMEM)
SMEM = pl.BlockSpec(memory_space=pltpu.SMEM)


def cost(flops, moved):
    return pl.CostEstimate(flops=flops, bytes_accessed=moved, transcendentals=0)


def after(value, *others):
    return lax.optimization_barrier((value, others))[0]


def kernel_call(body, outs, args, name, hint=LIGHT, scratch=()):
    return pl.pallas_call(
        body,
        in_specs=[SMEM] + [VMEM] * (len(args) - 1),
        out_specs=[VMEM] * len(outs),
        out_shape=[jax.ShapeDtypeStruct(shape, kind) for shape, kind in outs],
        scratch_shapes=list(scratch),
        compiler_params=PARAMS,
        cost_estimate=hint,
        name=name,
    )(*args)


def load_body(w_ref, through_ref, out_ref, same_ref, sems):
    step = w_ref.shape[0] // PIECES
    copies = []
    for n in range(PIECES):
        part = pl.ds(n * step, step)
        copies.append(pltpu.make_async_copy(w_ref.at[part], out_ref.at[part], sems.at[n]))
    for copy in copies:
        copy.start()
    for copy in copies:
        copy.wait()


def load(w, through, room):
    anywhere = pl.BlockSpec(memory_space=pl.ANY)
    return pl.pallas_call(
        load_body,
        in_specs=[anywhere, anywhere],
        out_specs=[VMEM, anywhere],
        out_shape=[
            pltpu.VMEM(w.shape, w.dtype),
            jax.ShapeDtypeStruct(through.shape, through.dtype),
        ],
        scratch_shapes=[pltpu.SemaphoreType.DMA((PIECES,))],
        input_output_aliases={1: 1},
        compiler_params=pltpu.CompilerParams(vmem_limit_bytes=room << 20),
        cost_estimate=cost(0, 2 * w.size),
        name="load",
    )(w, through)


SLOTS = {"enc_a": 4, "enc_b": 8, "dec_a": 12, "dec_b": 14, "proj_a": 20, "proj_b": 32, "hits": 40}


def table_body(n_tok, n_feat, blocks, ids_ref, active_ref, out_ref):
    i, j = ids_ref[0], ids_ref[1]
    chips, ratio = n_feat // 2, n_feat // n_tok
    chip, core = j // 2, j % 2

    def both_cores(place):
        return [2 * place + core, 2 * place + 1 - core]

    def held_slots(*sources):
        values, seen = [], 0
        for place, valid in sources:
            seen = jnp.where(valid, place, seen)
            for source in both_cores(seen):
                values += [source, jnp.where(valid, 1, 0)]
        return values

    numbers = [i, j // ratio, j % ratio, chip]
    for k in range(chips):
        numbers += both_cores((chip + chips - k) % chips)
    for k in (3, 2, 1, 0):
        numbers += both_cores(chip ^ k)[::-1]
    numbers += held_slots((chip, chip >= 0), (chip - 1, chip >= 1), (chip + 1, chip <= chips - 2))
    numbers += held_slots((chip ^ 2, chip >= 0), (chip ^ 3, (chip == 0) | (chip == chips - 1)))
    for n, number in enumerate(numbers):
        out_ref[n] = number
    tiles, listed = active_ref.shape
    for t in range(tiles):
        for b in range(blocks):
            found = jnp.int32(0)
            for n in range(listed):
                found = jnp.where(active_ref[t, n] == j * blocks + b, 1, found)
            out_ref[SLOTS["hits"] + t * blocks + b] = found


def make_table(ids, active, n_tok, n_feat, blocks):
    size = SLOTS["hits"] + active.shape[0] * blocks
    return pl.pallas_call(
        functools.partial(table_body, n_tok, n_feat, blocks),
        in_specs=[SMEM, SMEM],
        out_specs=SMEM,
        out_shape=jax.ShapeDtypeStruct((size,), jnp.int32),
        compiler_params=PARAMS,
        cost_estimate=LIGHT,
        name="table",
    )(ids, active)


def pick_body(table, array_ref, *refs):
    outs, sems = refs[:-1], refs[-1]
    rows = outs[0].shape[0]
    copies = []
    for s, out_ref in enumerate(outs):
        part = array_ref.at[aligned(table[0] ^ s, rows)]
        copies.append(pltpu.make_async_copy(part, out_ref, sems.at[s]))
    for copy in copies:
        copy.start()
    for copy in copies:
        copy.wait()


def pick(table, array, n_tok):
    shape = (array.shape[0] // n_tok, array.shape[1])
    return pl.pallas_call(
        pick_body,
        in_specs=[SMEM, pl.BlockSpec(memory_space=pl.ANY)],
        out_specs=[VMEM] * n_tok,
        out_shape=[jax.ShapeDtypeStruct(shape, array.dtype)] * n_tok,
        scratch_shapes=[pltpu.SemaphoreType.DMA((n_tok,))],
        compiler_params=PARAMS,
        cost_estimate=LIGHT,
        name="pick",
    )(table, array)


def third_body(chips, table, *refs):
    near_1, far_1, near_3, far_3, up_ref, down_ref, going_up_ref, going_down_ref = refs
    chip = table[3]
    for target, come_ref, turn in ((going_up_ref, up_ref, 1), (going_down_ref, down_ref, chips - 2)):
        for near_ref, far_ref, chosen in ((near_3, far_3, chip == turn), (near_1, far_1, chip != turn)):

            @pl.when(chosen)
            def _():
                total = near_ref[...].astype(F32) + far_ref[...].astype(F32)
                target[...] = (total + come_ref[...].astype(F32)).astype(BF16)


def pieces(refs, streams):
    return [refs[a].at[b] for a, stream in enumerate(streams) for b in range(len(stream))]


def aligned(index, width):
    return pl.ds(pl.multiple_of(index * width, width), width)


def enc_body(streams, count, first, last, n_feat, at, table, *refs):
    size = len(streams)
    slots = [pieces(refs[q * size:(q + 1) * size], streams) for q in range(count)]
    w_ref, bias_ref = refs[count * size:count * size + 2]
    refs = refs[count * size + 2:]
    carry_ref = None
    if not first:
        carry_ref, seen_ref, refs = refs[0], refs[1], refs[2:]
    out_ref, own_ref = refs[:2]
    total_ref = refs[2] if last else out_ref
    n_tok, width = len(slots[0]), slots[0][0].shape[1]
    if not first:
        own_ref[...] = seen_ref[...]
    for q, blocks in enumerate(slots):
        source = table[at + q]
        total = carry_ref if q == 0 else total_ref
        total = None if total is None else total[...]
        for s, x in enumerate(blocks):
            w = w_ref[(table[0] ^ s) * n_feat + source]
            term = jnp.dot(x[...], w, preferred_element_type=F32)
            total = term if total is None else total + term
        total_ref[...] = total
        for s, x in enumerate(blocks):

            @pl.when(((table[0] ^ s) == table[1]) & (source // n_tok == table[2]))
            def _():
                own_ref[:, aligned(source % n_tok, width)] = x[...]

    if last:
        blocks = out_ref.shape[1] // BLOCK
        for t in range(out_ref.shape[0] // TILE):
            for b in range(blocks):
                tile, block = slice(t * TILE, (t + 1) * TILE), slice(b * BLOCK, (b + 1) * BLOCK)
                pre = total_ref[tile, block] + bias_ref[:, block]
                live = table[SLOTS["hits"] + t * blocks + b].astype(F32)
                out_ref[tile, block] = (jnp.maximum(pre, 0.0) * live).astype(BF16)


def encode(table, at, slots, w, bias, carry, streams, last, n_feat):
    width, feats = w.shape[1:]
    rows = slots[0][0].shape[1]
    n_tok = w.shape[0] // n_feat
    args = [table] + [a for slot in slots for a in slot] + [w, bias]
    if carry is not None:
        args += carry
    return kernel_call(
        functools.partial(enc_body, streams, len(slots), carry is None, last, n_feat, at),
        [((rows, feats), BF16 if last else F32), ((rows, n_tok * width), BF16)],
        args,
        "encode",
        LIGHT if last else cost(2 * len(slots) * rows * n_tok * width * feats, 4 << 20),
        [pltpu.VMEM((rows, feats), F32)] if last else [],
    )


def dec_body(at, table, acts_ref, w_ref, *out_refs):
    share = out_refs[0].shape[1]
    for q, out_ref in enumerate(out_refs):
        w = w_ref[:, aligned(table[at + q], share)]
        out_ref[...] = jnp.dot(acts_ref[...], w, preferred_element_type=F32).astype(BF16)


def decode(table, at, acts, w, share, count, hint):
    outs = [((acts.shape[0], share), BF16)] * count
    return kernel_call(functools.partial(dec_body, at), outs, [table, acts, w], "decode", hint)


def proj_body(count, first, last, n_feat, at, table, *refs):
    slots, refs = refs[:count], refs[count:]
    w_ref, acts_ref, x_ref, bias_ref = refs[:4]
    refs = refs[4:]
    if not first:
        carry_ref, seen_ref, refs = refs[0], refs[1], refs[2:]
    out_ref, sum_ref = refs[:2]
    if last:
        out_ref, line_ref, sum_ref = refs
    if first:
        sum_ref[...] = jnp.zeros_like(sum_ref)
    else:
        sum_ref[...] = seen_ref[...]
    for q, g_ref in enumerate(slots):
        n_tok, _, width = g_ref.shape
        source, held = table[at + 2 * q], table[at + 2 * q + 1] == 1

        @pl.when(held)
        def _():
            total = None if q == 0 and first else (carry_ref if q == 0 else out_ref)[...]
            for s in range(n_tok):
                w = w_ref[:, aligned((table[0] ^ s) * n_feat + source, width)]
                term = lax.dot_general(
                    g_ref[s], w, (((1,), (1,)), ((), ())), preferred_element_type=F32
                )
                total = term if total is None else total + term
            out_ref[...] = total

        @pl.when(held & (source // n_tok == table[2]))
        def _():
            cols = aligned(source % n_tok, width)
            term = x_ref[:, cols].astype(F32) - bias_ref[:, cols]
            term = term * g_ref[table[0] ^ table[1]].astype(F32)
            sum_ref[...] += jnp.sum(term, axis=1, keepdims=True)

    if last:
        attr = acts_ref[...].astype(F32) * out_ref[...]
        out_ref[...] = attr
        total = sum_ref[...] - jnp.sum(attr, axis=1, keepdims=True)
        line_ref[...] = jnp.broadcast_to(total, (total.shape[0], TILE)).T[:8]


def project(table, at, slots, w, acts, own_x, bias, carry, last, n_feat):
    rows, feats = acts.shape
    outs = [((rows, feats), F32), ((8, rows), F32) if last else ((rows, 1), F32)]
    return kernel_call(
        functools.partial(proj_body, len(slots), carry is None, last, n_feat, at),
        outs,
        [table, *slots, w, acts, own_x, bias, *(carry or [])],
        "project",
        LIGHT if last else cost(2 * len(slots) * slots[0].size * feats, 4 << 20),
        [pltpu.VMEM((rows, 1), F32)] if last else [],
    )


def line_program(resid, resid_grad, active, w_enc, b_enc, w_dec, b_dec):
    n_tok, n_feat = lax.axis_size("tok"), lax.axis_size("feat")
    i, j = lax.axis_index("tok"), lax.axis_index("feat")
    chips = n_feat // 2
    width = resid.shape[1]
    rows = resid.shape[0] // n_tok
    feats = w_enc.shape[1]
    share = n_tok * width

    def along(pairs):
        return [(2 * a + c, 2 * b + c) for a, b in pairs for c in range(2)]

    def send(array, pairs):
        return lax.ppermute(array, "feat", along(pairs))

    def cross(array):
        return lax.ppermute(array, "feat", [(a, a ^ 1) for a in range(n_feat)])

    def exchange(array, streams):
        blocks = list(pick(table, array, n_tok))
        for s in range(1, n_tok):
            blocks[s] = lax.ppermute(blocks[s], "tok", [(a, a ^ s) for a in range(n_tok)])
        return [jnp.stack([blocks[s] for s in stream]) for stream in streams]

    table = make_table(jnp.stack([i, j]), active, n_tok, n_feat, feats // BLOCK)
    bias = b_enc.reshape(1, feats)
    b_row = b_dec.reshape(1, share)

    ring = [(a, (a + 1) % chips) for a in range(chips)]
    near_x = [exchange(resid, X_STREAMS)]
    far_x = [[cross(a) for a in near_x[0]]]
    for k in range(1, chips):
        first, second = near_x[-1]
        if k == 2:
            w_out, second = load(w_dec, second, 44)
            first = after(first, second)
            w_in, first = load(w_enc.reshape(n_tok * n_feat, width, feats), first, 34)
            near_x[-1] = [first, second]
            far_x.append([cross(a) for a in near_x[-1]])
        near_x.append([send(first, ring), send(second, ring)])
        if k == 2:
            shard_g, = exchange(after(resid_grad, near_x[2][0]), ((0, 1, 2, 3),))
    slots = [near_x[0], far_x[0], near_x[1], far_x[1]]
    carry = encode(table, SLOTS["enc_a"], slots, w_in, bias, None, X_STREAMS, False, n_feat)
    far_x.append([cross(a) for a in near_x[2]])
    far_x.append([cross(near_x[3][0]), cross(after(near_x[3][1], carry))])

    up_pairs = [(a, a + 1) for a in range(chips - 1)]
    down_pairs = [(a + 1, a) for a in range(chips - 1)]
    shard_g = after(shard_g, near_x[-1])
    up_1, down_1 = send(shard_g, up_pairs), send(shard_g, down_pairs)

    slots = [near_x[2], far_x[2], near_x[3], far_x[3]]
    acts, own_x = encode(table, SLOTS["enc_b"], slots, w_in, bias, carry, X_STREAMS, True, n_feat)

    far_3, near_3 = decode(table, SLOTS["dec_a"], acts, w_out, share, 2, LIGHT)
    up_1, down_1 = after((up_1, down_1), far_3)
    parts = {3: (near_3, cross(far_3))}
    outs = decode(
        table, SLOTS["dec_b"], after(acts, far_3), w_out, share, 6, cost(12 * rows * feats * share, 4 << 20)
    )
    for n, k in enumerate((2, 1, 0)):
        parts[k] = (outs[2 * n + 1], cross(outs[2 * n]))

    def pair_sum(k):
        return parts[k][0].astype(F32) + parts[k][1].astype(F32)

    come = send(pair_sum(3).astype(BF16), [(0, 1), (3, 2)])
    up_2, down_2 = send(up_1, up_pairs[1:]), send(down_1, down_pairs[:-1])
    two_g = up_2 + down_2
    three_g = send(two_g, [(2, 3), (1, 0)])

    going = (pair_sum(2) + come.astype(F32)).astype(BF16)
    up = send(going, up_pairs[:2])
    down = send(going, down_pairs[1:])

    slots = [shard_g, cross(shard_g), up_1, cross(up_1), down_1, cross(down_1)]
    carry = project(
        table, SLOTS["proj_a"], slots, w_out, after(acts, going), own_x, b_row, None, False, n_feat
    )
    base = own_x.astype(F32) - b_row - pair_sum(0)

    going_up, going_down = kernel_call(
        functools.partial(third_body, chips),
        [((rows, share), BF16)] * 2,
        [table, *parts[1], *parts[3], up, down],
        "third",
    )
    going_up, going_down = after((going_up, going_down), carry, base)
    up = send(going_up, up_pairs)
    down = send(going_down, down_pairs)

    slots = [two_g, cross(two_g), three_g, cross(three_g)]
    feature_attr, attr = project(
        table, SLOTS["proj_b"], slots, w_out, after(acts, going_up, going_down), own_x, b_row, carry, True, n_feat
    )
    attr = attr[:1]
    attr = attr + cross(attr)
    others = [send(attr, [(a, a ^ k) for a in range(chips)]) for k in range(1, chips)]
    for other in others:
        attr = attr + other

    error = base - (up.astype(F32) + down.astype(F32))
    return feature_attr, error, attr.reshape(rows)


def gathered_program(resid, resid_grad, active, w_enc, b_enc, w_dec, b_dec):
    n_tok = lax.axis_size("tok")
    n_feat = lax.axis_size("feat")
    width = resid.shape[1]

    def rows_of(array):
        part = lax.all_to_all(array, "tok", split_axis=0, concat_axis=1, tiled=True)
        part = part.reshape(part.shape[0], n_tok, 1, width)
        part = lax.all_gather(part, "feat", axis=2, tiled=True)
        return part.reshape(part.shape[0], n_tok * n_feat * width)

    rows_x, rows_g = rows_of(resid), rows_of(resid_grad)
    tok_rows = rows_x.shape[0]
    feat_dev = w_enc.shape[1]
    blocks = feat_dev // BLOCK
    tiles_dev = active.shape[0]
    block_ids = lax.axis_index("feat") * blocks + jnp.arange(blocks, dtype=jnp.int32)
    hits = jnp.any(active[:, :, None] == block_ids[None, None, :], axis=1).astype(F32)
    pre = jnp.dot(rows_x, w_enc, preferred_element_type=F32) + b_enc
    shaped = jnp.maximum(pre, 0.0).reshape(tiles_dev, TILE, blocks, BLOCK) * hits[:, None, :, None]
    acts = shaped.reshape(tok_rows, feat_dev).astype(BF16)
    partial_recon = jnp.dot(acts, w_dec, preferred_element_type=F32)
    recon_share = lax.psum_scatter(
        partial_recon.astype(BF16), "feat", scatter_dimension=1, tiled=True
    ).astype(F32)
    share = recon_share.shape[1]
    start = lax.axis_index("feat") * share
    own_x = lax.dynamic_slice_in_dim(rows_x, start, share, 1)
    own_g = lax.dynamic_slice_in_dim(rows_g, start, share, 1)
    recon = recon_share + b_dec
    error = own_x.astype(F32) - recon
    local_sums = jnp.sum(error * own_g.astype(F32), axis=1)
    error_attr = lax.psum(local_sums, "feat")
    proj = lax.dot_general(rows_g, w_dec, (((1,), (1,)), ((), ())), preferred_element_type=F32)
    return acts.astype(F32) * proj, error, error_attr


def per_device(resid, *rest):
    fits = resid.shape[1] % 128 == 0 and lax.axis_size("tok") == 4 and lax.axis_size("feat") == 8
    return (line_program if fits else gathered_program)(resid, *rest)


def solution(mesh):
    placed = (
        P(None, ("tok", "feat")),
        P(None, ("tok", "feat")),
        P("tok", None),
        P(None, "feat"),
        P("feat"),
        P("feat", None),
        P("feat"),
    )
    return jax.shard_map(
        per_device,
        mesh=mesh,
        in_specs=placed,
        out_specs=(P("tok", "feat"), P("tok", "feat"), P("tok")),
        check_vma=False,
    )
```

```python
import functools

import jax
import jax.numpy as jnp
from jax import lax
from jax.experimental import pallas as pl
from jax.experimental.pallas import tpu as pltpu
from jax.sharding import PartitionSpec as P

BLOCK = 128
TILE = 128
X_STREAMS = ((0, 1), (2, 3))
PIECES = 8
PARAMS = pltpu.CompilerParams(vmem_limit_bytes=20 << 20)
F32 = jnp.float32
BF16 = jnp.bfloat16
LIGHT = pl.CostEstimate(flops=1, bytes_accessed=1, transcendentals=0)
VMEM = pl.BlockSpec(memory_space=pltpu.VMEM)
SMEM = pl.BlockSpec(memory_space=pltpu.SMEM)


def cost(flops, moved):
    return pl.CostEstimate(flops=flops, bytes_accessed=moved, transcendentals=0)


def after(value, *others):
    return lax.optimization_barrier((value, others))[0]


def kernel_call(body, outs, args, name, hint=LIGHT, scratch=()):
    return pl.pallas_call(
        body,
        in_specs=[SMEM] + [VMEM] * (len(args) - 1),
        out_specs=[VMEM] * len(outs),
        out_shape=[jax.ShapeDtypeStruct(shape, kind) for shape, kind in outs],
        scratch_shapes=list(scratch),
        compiler_params=PARAMS,
        cost_estimate=hint,
        name=name,
    )(*args)


def load_body(w_ref, through_ref, out_ref, same_ref, sems):
    step = w_ref.shape[0] // PIECES
    copies = []
    for n in range(PIECES):
        part = pl.ds(n * step, step)
        copies.append(pltpu.make_async_copy(w_ref.at[part], out_ref.at[part], sems.at[n]))
    for copy in copies:
        copy.start()
    for copy in copies:
        copy.wait()


def load(w, through, room):
    anywhere = pl.BlockSpec(memory_space=pl.ANY)
    return pl.pallas_call(
        load_body,
        in_specs=[anywhere, anywhere],
        out_specs=[VMEM, anywhere],
        out_shape=[
            pltpu.VMEM(w.shape, w.dtype),
            jax.ShapeDtypeStruct(through.shape, through.dtype),
        ],
        scratch_shapes=[pltpu.SemaphoreType.DMA((PIECES,))],
        input_output_aliases={1: 1},
        compiler_params=pltpu.CompilerParams(vmem_limit_bytes=room << 20),
        cost_estimate=cost(0, 2 * w.size),
        name="load",
    )(w, through)


SLOTS = {"enc_a": 4, "enc_b": 8, "dec_a": 12, "dec_b": 14, "proj_a": 20, "proj_b": 32, "hits": 40}


def table_body(n_tok, n_feat, blocks, ids_ref, active_ref, out_ref):
    i, j = ids_ref[0], ids_ref[1]
    chips, ratio = n_feat // 2, n_feat // n_tok
    chip, core = j // 2, j % 2

    def both_cores(place):
        return [2 * place + core, 2 * place + 1 - core]

    def held_slots(*sources):
        values, seen = [], 0
        for place, valid in sources:
            seen = jnp.where(valid, place, seen)
            for source in both_cores(seen):
                values += [source, jnp.where(valid, 1, 0)]
        return values

    numbers = [i, j // ratio, j % ratio, chip]
    for k in range(chips):
        numbers += both_cores((chip + chips - k) % chips)
    for k in (3, 2, 1, 0):
        numbers += both_cores(chip ^ k)[::-1]
    numbers += held_slots((chip, chip >= 0), (chip - 1, chip >= 1), (chip + 1, chip <= chips - 2))
    numbers += held_slots((chip ^ 2, chip >= 0), (chip ^ 3, (chip == 0) | (chip == chips - 1)))
    for n, number in enumerate(numbers):
        out_ref[n] = number
    tiles, listed = active_ref.shape
    for t in range(tiles):
        for b in range(blocks):
            found = jnp.int32(0)
            for n in range(listed):
                found = jnp.where(active_ref[t, n] == j * blocks + b, 1, found)
            out_ref[SLOTS["hits"] + t * blocks + b] = found


def make_table(ids, active, n_tok, n_feat, blocks):
    size = SLOTS["hits"] + active.shape[0] * blocks
    return pl.pallas_call(
        functools.partial(table_body, n_tok, n_feat, blocks),
        in_specs=[SMEM, SMEM],
        out_specs=SMEM,
        out_shape=jax.ShapeDtypeStruct((size,), jnp.int32),
        compiler_params=PARAMS,
        cost_estimate=LIGHT,
        name="table",
    )(ids, active)


def pick_body(table, array_ref, *refs):
    outs, sems = refs[:-1], refs[-1]
    rows = outs[0].shape[0]
    copies = []
    for s, out_ref in enumerate(outs):
        part = array_ref.at[aligned(table[0] ^ s, rows)]
        copies.append(pltpu.make_async_copy(part, out_ref, sems.at[s]))
    for copy in copies:
        copy.start()
    for copy in copies:
        copy.wait()


def pick(table, array, n_tok):
    shape = (array.shape[0] // n_tok, array.shape[1])
    return pl.pallas_call(
        pick_body,
        in_specs=[SMEM, pl.BlockSpec(memory_space=pl.ANY)],
        out_specs=[VMEM] * n_tok,
        out_shape=[jax.ShapeDtypeStruct(shape, array.dtype)] * n_tok,
        scratch_shapes=[pltpu.SemaphoreType.DMA((n_tok,))],
        compiler_params=PARAMS,
        cost_estimate=LIGHT,
        name="pick",
    )(table, array)


def third_body(chips, table, *refs):
    near_1, far_1, near_3, far_3, up_ref, down_ref, going_up_ref, going_down_ref = refs
    chip = table[3]
    for target, come_ref, turn in ((going_up_ref, up_ref, 1), (going_down_ref, down_ref, chips - 2)):
        for near_ref, far_ref, chosen in ((near_3, far_3, chip == turn), (near_1, far_1, chip != turn)):

            @pl.when(chosen)
            def _():
                total = near_ref[...].astype(F32) + far_ref[...].astype(F32)
                target[...] = (total + come_ref[...].astype(F32)).astype(BF16)


def pieces(refs, streams):
    return [refs[a].at[b] for a, stream in enumerate(streams) for b in range(len(stream))]


def aligned(index, width):
    return pl.ds(pl.multiple_of(index * width, width), width)


def enc_body(streams, count, first, last, n_feat, at, table, *refs):
    size = len(streams)
    slots = [pieces(refs[q * size:(q + 1) * size], streams) for q in range(count)]
    w_ref, bias_ref = refs[count * size:count * size + 2]
    refs = refs[count * size + 2:]
    carry_ref = None
    if not first:
        carry_ref, seen_ref, refs = refs[0], refs[1], refs[2:]
    out_ref, own_ref = refs[:2]
    total_ref = refs[2] if last else out_ref
    n_tok, width = len(slots[0]), slots[0][0].shape[1]
    if not first:
        own_ref[...] = seen_ref[...]
    for q, blocks in enumerate(slots):
        source = table[at + q]
        total = carry_ref if q == 0 else total_ref
        total = None if total is None else total[...]
        for s, x in enumerate(blocks):
            w = w_ref[(table[0] ^ s) * n_feat + source]
            term = jnp.dot(x[...], w, preferred_element_type=F32)
            total = term if total is None else total + term
        total_ref[...] = total
        for s, x in enumerate(blocks):

            @pl.when(((table[0] ^ s) == table[1]) & (source // n_tok == table[2]))
            def _():
                own_ref[:, aligned(source % n_tok, width)] = x[...]

    if last:
        blocks = out_ref.shape[1] // BLOCK
        for t in range(out_ref.shape[0] // TILE):
            for b in range(blocks):
                tile, block = slice(t * TILE, (t + 1) * TILE), slice(b * BLOCK, (b + 1) * BLOCK)
                pre = total_ref[tile, block] + bias_ref[:, block]
                live = table[SLOTS["hits"] + t * blocks + b].astype(F32)
                out_ref[tile, block] = (jnp.maximum(pre, 0.0) * live).astype(BF16)


def encode(table, at, slots, w, bias, carry, streams, last, n_feat):
    width, feats = w.shape[1:]
    rows = slots[0][0].shape[1]
    n_tok = w.shape[0] // n_feat
    args = [table] + [a for slot in slots for a in slot] + [w, bias]
    if carry is not None:
        args += carry
    return kernel_call(
        functools.partial(enc_body, streams, len(slots), carry is None, last, n_feat, at),
        [((rows, feats), BF16 if last else F32), ((rows, n_tok * width), BF16)],
        args,
        "encode",
        LIGHT if last else cost(2 * len(slots) * rows * n_tok * width * feats, 4 << 20),
        [pltpu.VMEM((rows, feats), F32)] if last else [],
    )


def dec_body(at, table, acts_ref, w_ref, *out_refs):
    share = out_refs[0].shape[1]
    for q, out_ref in enumerate(out_refs):
        w = w_ref[:, aligned(table[at + q], share)]
        out_ref[...] = jnp.dot(acts_ref[...], w, preferred_element_type=F32).astype(BF16)


def decode(table, at, acts, w, share, count, hint):
    outs = [((acts.shape[0], share), BF16)] * count
    return kernel_call(functools.partial(dec_body, at), outs, [table, acts, w], "decode", hint)


def proj_body(count, first, last, n_feat, at, table, *refs):
    slots, refs = refs[:count], refs[count:]
    w_ref, acts_ref, x_ref, bias_ref = refs[:4]
    refs = refs[4:]
    if not first:
        carry_ref, seen_ref, refs = refs[0], refs[1], refs[2:]
    out_ref, sum_ref = refs[:2]
    if last:
        out_ref, line_ref, sum_ref = refs
    if first:
        sum_ref[...] = jnp.zeros_like(sum_ref)
    else:
        sum_ref[...] = seen_ref[...]
    for q, g_ref in enumerate(slots):
        n_tok, _, width = g_ref.shape
        source, held = table[at + 2 * q], table[at + 2 * q + 1] == 1

        @pl.when(held)
        def _():
            total = None if q == 0 and first else (carry_ref if q == 0 else out_ref)[...]
            for s in range(n_tok):
                w = w_ref[:, aligned((table[0] ^ s) * n_feat + source, width)]
                term = lax.dot_general(
                    g_ref[s], w, (((1,), (1,)), ((), ())), preferred_element_type=F32
                )
                total = term if total is None else total + term
            out_ref[...] = total

        @pl.when(held & (source // n_tok == table[2]))
        def _():
            cols = aligned(source % n_tok, width)
            term = x_ref[:, cols].astype(F32) - bias_ref[:, cols]
            term = term * g_ref[table[0] ^ table[1]].astype(F32)
            sum_ref[...] += jnp.sum(term, axis=1, keepdims=True)

    if last:
        attr = acts_ref[...].astype(F32) * out_ref[...]
        out_ref[...] = attr
        total = sum_ref[...] - jnp.sum(attr, axis=1, keepdims=True)
        line_ref[...] = jnp.broadcast_to(total, (total.shape[0], TILE)).T[:8]


def project(table, at, slots, w, acts, own_x, bias, carry, last, n_feat):
    rows, feats = acts.shape
    outs = [((rows, feats), F32), ((8, rows), F32) if last else ((rows, 1), F32)]
    return kernel_call(
        functools.partial(proj_body, len(slots), carry is None, last, n_feat, at),
        outs,
        [table, *slots, w, acts, own_x, bias, *(carry or [])],
        "project",
        LIGHT if last else cost(2 * len(slots) * slots[0].size * feats, 4 << 20),
        [pltpu.VMEM((rows, 1), F32)] if last else [],
    )


def line_program(resid, resid_grad, active, w_enc, b_enc, w_dec, b_dec):
    n_tok, n_feat = lax.axis_size("tok"), lax.axis_size("feat")
    i, j = lax.axis_index("tok"), lax.axis_index("feat")
    chips = n_feat // 2
    width = resid.shape[1]
    rows = resid.shape[0] // n_tok
    feats = w_enc.shape[1]
    share = n_tok * width

    def along(pairs):
        return [(2 * a + c, 2 * b + c) for a, b in pairs for c in range(2)]

    def send(array, pairs):
        return lax.ppermute(array, "feat", along(pairs))

    def cross(array):
        return lax.ppermute(array, "feat", [(a, a ^ 1) for a in range(n_feat)])

    def exchange(blocks, streams):
        blocks = list(blocks)
        for s in range(1, n_tok):
            blocks[s] = lax.ppermute(blocks[s], "tok", [(a, a ^ s) for a in range(n_tok)])
        return [jnp.stack([blocks[s] for s in stream]) for stream in streams]

    table = make_table(jnp.stack([i, j]), active, n_tok, n_feat, feats // BLOCK)
    bias = b_enc.reshape(1, feats)
    b_row = b_dec.reshape(1, share)

    ring = [(a, (a + 1) % chips) for a in range(chips)]
    cut_x = [lax.dynamic_slice_in_dim(resid, (i ^ s) * rows, rows, 0) for s in range(n_tok)]
    near_x = [exchange(cut_x, X_STREAMS)]
    far_x = [[cross(a) for a in near_x[0]]]
    for k in range(1, chips):
        first, second = near_x[-1]
        if k == 1:
            second = after(second, table)
        if k == 2:
            w_out, first = load(w_dec, first, 44)
            shard_g, = exchange(pick(table, after(resid_grad, first), n_tok), ((0, 1, 2, 3),))
        if k == 3:
            w_in, first = load(w_enc.reshape(n_tok * n_feat, width, feats), first, 36)
            second = after(second, shard_g)
        near_x[-1] = [first, second]
        if k > 1:
            far_x.append([cross(a) for a in near_x[-1]])
        near_x.append([send(first, ring), send(second, ring)])
    slots = [near_x[0], far_x[0], near_x[1], far_x[1]]
    carry = encode(table, SLOTS["enc_a"], slots, w_in, bias, None, X_STREAMS, False, n_feat)
    far_x.append([cross(near_x[3][0]), cross(after(near_x[3][1], carry))])

    up_pairs = [(a, a + 1) for a in range(chips - 1)]
    down_pairs = [(a + 1, a) for a in range(chips - 1)]
    shard_g = after(shard_g, near_x[-1])
    up_1, down_1 = send(shard_g, up_pairs), send(shard_g, down_pairs)

    slots = [near_x[2], far_x[2], near_x[3], far_x[3]]
    acts, own_x = encode(table, SLOTS["enc_b"], slots, w_in, bias, carry, X_STREAMS, True, n_feat)

    far_3, near_3 = decode(table, SLOTS["dec_a"], acts, w_out, share, 2, LIGHT)
    up_1, down_1 = after((up_1, down_1), far_3)
    parts = {3: (near_3, cross(far_3))}
    outs = decode(
        table, SLOTS["dec_b"], after(acts, far_3), w_out, share, 6, cost(12 * rows * feats * share, 4 << 20)
    )
    for n, k in enumerate((2, 1, 0)):
        parts[k] = (outs[2 * n + 1], cross(outs[2 * n]))

    def pair_sum(k):
        return parts[k][0].astype(F32) + parts[k][1].astype(F32)

    come = send(pair_sum(3).astype(BF16), [(0, 1), (3, 2)])
    up_2, down_2 = send(up_1, up_pairs[1:]), send(down_1, down_pairs[:-1])
    two_g = up_2 + down_2
    three_g = send(two_g, [(2, 3), (1, 0)])

    going = (pair_sum(2) + come.astype(F32)).astype(BF16)
    up = send(going, up_pairs[:2])
    down = send(going, down_pairs[1:])

    slots = [shard_g, cross(shard_g), up_1, cross(up_1), down_1, cross(down_1)]
    carry = project(
        table, SLOTS["proj_a"], slots, w_out, after(acts, going), own_x, b_row, None, False, n_feat
    )
    base = own_x.astype(F32) - b_row - pair_sum(0)

    going_up, going_down = kernel_call(
        functools.partial(third_body, chips),
        [((rows, share), BF16)] * 2,
        [table, *parts[1], *parts[3], up, down],
        "third",
    )
    going_up, going_down = after((going_up, going_down), carry, base)
    up = send(going_up, up_pairs)
    down = send(going_down, down_pairs)

    slots = [two_g, cross(two_g), three_g, cross(three_g)]
    feature_attr, attr = project(
        table, SLOTS["proj_b"], slots, w_out, after(acts, going_up, going_down), own_x, b_row, carry, True, n_feat
    )
    attr = attr[:1]
    attr = attr + cross(attr)
    others = [send(attr, [(a, a ^ k) for a in range(chips)]) for k in range(1, chips)]
    for other in others:
        attr = attr + other

    error = base - (up.astype(F32) + down.astype(F32))
    return feature_attr, error, attr.reshape(rows)


def gathered_program(resid, resid_grad, active, w_enc, b_enc, w_dec, b_dec):
    n_tok = lax.axis_size("tok")
    n_feat = lax.axis_size("feat")
    width = resid.shape[1]

    def rows_of(array):
        part = lax.all_to_all(array, "tok", split_axis=0, concat_axis=1, tiled=True)
        part = part.reshape(part.shape[0], n_tok, 1, width)
        part = lax.all_gather(part, "feat", axis=2, tiled=True)
        return part.reshape(part.shape[0], n_tok * n_feat * width)

    rows_x, rows_g = rows_of(resid), rows_of(resid_grad)
    tok_rows = rows_x.shape[0]
    feat_dev = w_enc.shape[1]
    blocks = feat_dev // BLOCK
    tiles_dev = active.shape[0]
    block_ids = lax.axis_index("feat") * blocks + jnp.arange(blocks, dtype=jnp.int32)
    hits = jnp.any(active[:, :, None] == block_ids[None, None, :], axis=1).astype(F32)
    pre = jnp.dot(rows_x, w_enc, preferred_element_type=F32) + b_enc
    shaped = jnp.maximum(pre, 0.0).reshape(tiles_dev, TILE, blocks, BLOCK) * hits[:, None, :, None]
    acts = shaped.reshape(tok_rows, feat_dev).astype(BF16)
    partial_recon = jnp.dot(acts, w_dec, preferred_element_type=F32)
    recon_share = lax.psum_scatter(
        partial_recon.astype(BF16), "feat", scatter_dimension=1, tiled=True
    ).astype(F32)
    share = recon_share.shape[1]
    start = lax.axis_index("feat") * share
    own_x = lax.dynamic_slice_in_dim(rows_x, start, share, 1)
    own_g = lax.dynamic_slice_in_dim(rows_g, start, share, 1)
    recon = recon_share + b_dec
    error = own_x.astype(F32) - recon
    local_sums = jnp.sum(error * own_g.astype(F32), axis=1)
    error_attr = lax.psum(local_sums, "feat")
    proj = lax.dot_general(rows_g, w_dec, (((1,), (1,)), ((), ())), preferred_element_type=F32)
    return acts.astype(F32) * proj, error, error_attr


def per_device(resid, *rest):
    fits = resid.shape[1] % 128 == 0 and lax.axis_size("tok") == 4 and lax.axis_size("feat") == 8
    return (line_program if fits else gathered_program)(resid, *rest)


def solution(mesh):
    placed = (
        P(None, ("tok", "feat")),
        P(None, ("tok", "feat")),
        P("tok", None),
        P(None, "feat"),
        P("feat"),
        P("feat", None),
        P("feat"),
    )
    return jax.shard_map(
        per_device,
        mesh=mesh,
        in_specs=placed,
        out_specs=(P("tok", "feat"), P("tok", "feat"), P("tok")),
        check_vma=False,
    )
```

```python
import functools

import jax
import jax.numpy as jnp
from jax import lax
from jax.experimental import pallas as pl
from jax.experimental.pallas import tpu as pltpu
from jax.sharding import PartitionSpec as P

BLOCK = 128
TILE = 128
X_STREAMS = ((0, 1), (2, 3))
PIECES = 8
PARAMS = pltpu.CompilerParams(vmem_limit_bytes=20 << 20)
F32 = jnp.float32
BF16 = jnp.bfloat16
LIGHT = pl.CostEstimate(flops=1, bytes_accessed=1, transcendentals=0)
VMEM = pl.BlockSpec(memory_space=pltpu.VMEM)
SMEM = pl.BlockSpec(memory_space=pltpu.SMEM)


def cost(flops, moved):
    return pl.CostEstimate(flops=flops, bytes_accessed=moved, transcendentals=0)


def after(value, *others):
    return lax.optimization_barrier((value, others))[0]


def kernel_call(body, outs, args, name, hint=LIGHT, scratch=()):
    return pl.pallas_call(
        body,
        in_specs=[SMEM] + [VMEM] * (len(args) - 1),
        out_specs=[VMEM] * len(outs),
        out_shape=[jax.ShapeDtypeStruct(shape, kind) for shape, kind in outs],
        scratch_shapes=list(scratch),
        compiler_params=PARAMS,
        cost_estimate=hint,
        name=name,
    )(*args)


def load_body(w_ref, through_ref, out_ref, same_ref, sems):
    step = w_ref.shape[0] // PIECES
    copies = []
    for n in range(PIECES):
        part = pl.ds(n * step, step)
        copies.append(pltpu.make_async_copy(w_ref.at[part], out_ref.at[part], sems.at[n]))
    for copy in copies:
        copy.start()
    for copy in copies:
        copy.wait()


def load(w, through, room):
    anywhere = pl.BlockSpec(memory_space=pl.ANY)
    return pl.pallas_call(
        load_body,
        in_specs=[anywhere, anywhere],
        out_specs=[VMEM, anywhere],
        out_shape=[
            pltpu.VMEM(w.shape, w.dtype),
            jax.ShapeDtypeStruct(through.shape, through.dtype),
        ],
        scratch_shapes=[pltpu.SemaphoreType.DMA((PIECES,))],
        input_output_aliases={1: 1},
        compiler_params=pltpu.CompilerParams(vmem_limit_bytes=room << 20),
        cost_estimate=cost(0, 2 * w.size),
        name="load",
    )(w, through)


SLOTS = {"enc_a": 4, "enc_b": 8, "dec_a": 12, "dec_b": 14, "proj_a": 20, "proj_b": 32, "hits": 40}


def table_body(n_tok, n_feat, blocks, ids_ref, active_ref, out_ref):
    i, j = ids_ref[0], ids_ref[1]
    chips, ratio = n_feat // 2, n_feat // n_tok
    chip, core = j // 2, j % 2

    def both_cores(place):
        return [2 * place + core, 2 * place + 1 - core]

    def held_slots(*sources):
        values, seen = [], 0
        for place, valid in sources:
            seen = jnp.where(valid, place, seen)
            for source in both_cores(seen):
                values += [source, jnp.where(valid, 1, 0)]
        return values

    numbers = [i, j // ratio, j % ratio, chip]
    for k in range(chips):
        numbers += both_cores((chip + chips - k) % chips)
    for k in (3, 2, 1, 0):
        numbers += both_cores(chip ^ k)[::-1]
    numbers += held_slots((chip, chip >= 0), (chip - 1, chip >= 1), (chip + 1, chip <= chips - 2))
    numbers += held_slots((chip ^ 2, chip >= 0), (chip ^ 3, (chip == 0) | (chip == chips - 1)))
    for n, number in enumerate(numbers):
        out_ref[n] = number
    tiles, listed = active_ref.shape
    for t in range(tiles):
        for b in range(blocks):
            found = jnp.int32(0)
            for n in range(listed):
                found = jnp.where(active_ref[t, n] == j * blocks + b, 1, found)
            out_ref[SLOTS["hits"] + t * blocks + b] = found


def make_table(ids, active, n_tok, n_feat, blocks):
    size = SLOTS["hits"] + active.shape[0] * blocks
    return pl.pallas_call(
        functools.partial(table_body, n_tok, n_feat, blocks),
        in_specs=[SMEM, SMEM],
        out_specs=SMEM,
        out_shape=jax.ShapeDtypeStruct((size,), jnp.int32),
        compiler_params=PARAMS,
        cost_estimate=LIGHT,
        name="table",
    )(ids, active)


def pick_body(table, array_ref, *refs):
    outs, sems = refs[:-1], refs[-1]
    rows = outs[0].shape[0]
    copies = []
    for s, out_ref in enumerate(outs):
        part = array_ref.at[aligned(table[0] ^ s, rows)]
        copies.append(pltpu.make_async_copy(part, out_ref, sems.at[s]))
    for copy in copies:
        copy.start()
    for copy in copies:
        copy.wait()


def pick(table, array, n_tok):
    shape = (array.shape[0] // n_tok, array.shape[1])
    return pl.pallas_call(
        pick_body,
        in_specs=[SMEM, pl.BlockSpec(memory_space=pl.ANY)],
        out_specs=[VMEM] * n_tok,
        out_shape=[jax.ShapeDtypeStruct(shape, array.dtype)] * n_tok,
        scratch_shapes=[pltpu.SemaphoreType.DMA((n_tok,))],
        compiler_params=PARAMS,
        cost_estimate=LIGHT,
        name="pick",
    )(table, array)


def third_body(chips, table, *refs):
    near_1, far_1, near_3, far_3, up_ref, down_ref = refs[:3] + (refs[3:-4],) + refs[-4:-2]
    chip = table[3]
    for target, come_ref, turn in ((refs[-2], up_ref, 1), (refs[-1], down_ref, chips - 2)):

        @pl.when(chip == turn)
        def _():
            rows = far_3[0].shape[0]
            for h, far_ref in enumerate(far_3):
                part = slice(h * rows, (h + 1) * rows)
                total = near_3[part].astype(F32) + far_ref[...].astype(F32)
                target[part] = (total + come_ref[part].astype(F32)).astype(BF16)

        @pl.when(chip != turn)
        def _():
            total = near_1[...].astype(F32) + far_1[...].astype(F32)
            target[...] = (total + come_ref[...].astype(F32)).astype(BF16)


def pieces(refs, streams):
    return [refs[a].at[b] for a, stream in enumerate(streams) for b in range(len(stream))]


def aligned(index, width):
    return pl.ds(pl.multiple_of(index * width, width), width)


def enc_body(streams, count, first, last, n_feat, at, table, *refs):
    size = len(streams)
    slots = [pieces(refs[q * size:(q + 1) * size], streams) for q in range(count)]
    w_ref, bias_ref = refs[count * size:count * size + 2]
    refs = refs[count * size + 2:]
    carry_ref = None
    if not first:
        carry_ref, seen_ref, refs = refs[0], refs[1], refs[2:]
    out_ref, own_ref = refs[:2]
    total_ref = refs[2] if last else out_ref
    n_tok, width = len(slots[0]), slots[0][0].shape[1]
    if not first:
        own_ref[...] = seen_ref[...]
    for q, blocks in enumerate(slots):
        source = table[at + q]
        total = carry_ref if q == 0 else total_ref
        total = None if total is None else total[...]
        for s, x in enumerate(blocks):
            w = w_ref[(table[0] ^ s) * n_feat + source]
            term = jnp.dot(x[...], w, preferred_element_type=F32)
            total = term if total is None else total + term
        total_ref[...] = total
        for s, x in enumerate(blocks):

            @pl.when(((table[0] ^ s) == table[1]) & (source // n_tok == table[2]))
            def _():
                own_ref[:, aligned(source % n_tok, width)] = x[...]

    if last:
        blocks = out_ref.shape[1] // BLOCK
        for t in range(out_ref.shape[0] // TILE):
            for b in range(blocks):
                tile, block = slice(t * TILE, (t + 1) * TILE), slice(b * BLOCK, (b + 1) * BLOCK)
                pre = total_ref[tile, block] + bias_ref[:, block]
                live = table[SLOTS["hits"] + t * blocks + b].astype(F32)
                out_ref[tile, block] = (jnp.maximum(pre, 0.0) * live).astype(BF16)


def encode(table, at, slots, w, bias, carry, streams, last, n_feat):
    width, feats = w.shape[1:]
    rows = slots[0][0].shape[1]
    n_tok = w.shape[0] // n_feat
    args = [table] + [a for slot in slots for a in slot] + [w, bias]
    if carry is not None:
        args += carry
    return kernel_call(
        functools.partial(enc_body, streams, len(slots), carry is None, last, n_feat, at),
        [((rows, feats), BF16 if last else F32), ((rows, n_tok * width), BF16)],
        args,
        "encode",
        LIGHT if last else cost(2 * len(slots) * rows * n_tok * width * feats, 4 << 20),
        [pltpu.VMEM((rows, feats), F32)] if last else [],
    )


def dec_body(at, table, acts_ref, w_ref, *out_refs):
    share = out_refs[0].shape[1]
    for q, out_ref in enumerate(out_refs):
        w = w_ref[:, aligned(table[at + q], share)]
        out_ref[...] = jnp.dot(acts_ref[...], w, preferred_element_type=F32).astype(BF16)


def decode(table, at, acts, w, share, count):
    outs = [((acts.shape[0], share), BF16)] * count
    hint = cost(2 * count * acts.size * share, 4 << 20)
    return kernel_call(functools.partial(dec_body, at), outs, [table, acts, w], "decode", hint)


def first_body(at, table, acts_ref, w_ref, *out_refs):
    share = out_refs[0].shape[1]
    for q, targets in enumerate((out_refs[:-1], out_refs[-1:])):
        w = w_ref[:, aligned(table[at + q], share)]
        part = jnp.dot(acts_ref[...], w, preferred_element_type=F32).astype(BF16)
        rows = part.shape[0] // len(targets)
        for h, out_ref in enumerate(targets):
            out_ref[...] = part[h * rows:(h + 1) * rows]


def sum_body(table, near_ref, *refs):
    far_refs, out_ref = refs[:-1], refs[-1]
    rows = far_refs[0].shape[0]
    for h, far_ref in enumerate(far_refs):
        part = slice(h * rows, (h + 1) * rows)
        out_ref[part] = (near_ref[part].astype(F32) + far_ref[...].astype(F32)).astype(BF16)


def proj_body(count, first, last, n_feat, at, table, *refs):
    slots, refs = refs[:count], refs[count:]
    w_ref, acts_ref, x_ref, bias_ref = refs[:4]
    refs = refs[4:]
    if not first:
        carry_ref, seen_ref, refs = refs[0], refs[1], refs[2:]
    out_ref, sum_ref = refs[:2]
    if last:
        out_ref, line_ref, sum_ref = refs
    if first:
        sum_ref[...] = jnp.zeros_like(sum_ref)
    else:
        sum_ref[...] = seen_ref[...]
    for q, g_ref in enumerate(slots):
        n_tok, _, width = g_ref.shape
        source, held = table[at + 2 * q], table[at + 2 * q + 1] == 1

        @pl.when(held)
        def _():
            total = None if q == 0 and first else (carry_ref if q == 0 else out_ref)[...]
            for s in range(n_tok):
                w = w_ref[:, aligned((table[0] ^ s) * n_feat + source, width)]
                term = lax.dot_general(
                    g_ref[s], w, (((1,), (1,)), ((), ())), preferred_element_type=F32
                )
                total = term if total is None else total + term
            out_ref[...] = total

        @pl.when(held & (source // n_tok == table[2]))
        def _():
            cols = aligned(source % n_tok, width)
            term = x_ref[:, cols].astype(F32) - bias_ref[:, cols]
            term = term * g_ref[table[0] ^ table[1]].astype(F32)
            sum_ref[...] += jnp.sum(term, axis=1, keepdims=True)

    if last:
        attr = acts_ref[...].astype(F32) * out_ref[...]
        out_ref[...] = attr
        total = sum_ref[...] - jnp.sum(attr, axis=1, keepdims=True)
        line_ref[...] = jnp.broadcast_to(total, (total.shape[0], TILE)).T[:8]


def project(table, at, slots, w, acts, own_x, bias, carry, last, n_feat):
    rows, feats = acts.shape
    outs = [((rows, feats), F32), ((8, rows), F32) if last else ((rows, 1), F32)]
    return kernel_call(
        functools.partial(proj_body, len(slots), carry is None, last, n_feat, at),
        outs,
        [table, *slots, w, acts, own_x, bias, *(carry or [])],
        "project",
        LIGHT if last else cost(2 * len(slots) * slots[0].size * feats, 4 << 20),
        [pltpu.VMEM((rows, 1), F32)] if last else [],
    )


def line_program(resid, resid_grad, active, w_enc, b_enc, w_dec, b_dec):
    n_tok, n_feat = lax.axis_size("tok"), lax.axis_size("feat")
    i, j = lax.axis_index("tok"), lax.axis_index("feat")
    chips = n_feat // 2
    width = resid.shape[1]
    rows = resid.shape[0] // n_tok
    feats = w_enc.shape[1]
    share = n_tok * width

    def along(pairs):
        return [(2 * a + c, 2 * b + c) for a, b in pairs for c in range(2)]

    def send(array, pairs):
        return lax.ppermute(array, "feat", along(pairs))

    def cross(array):
        return lax.ppermute(array, "feat", [(a, a ^ 1) for a in range(n_feat)])

    def exchange(blocks, streams):
        blocks = list(blocks)
        for s in range(1, n_tok):
            blocks[s] = lax.ppermute(blocks[s], "tok", [(a, a ^ s) for a in range(n_tok)])
        return [jnp.stack([blocks[s] for s in stream]) for stream in streams]

    table = make_table(jnp.stack([i, j]), active, n_tok, n_feat, feats // BLOCK)
    bias = b_enc.reshape(1, feats)
    b_row = b_dec.reshape(1, share)

    ring = [(a, (a + 1) % chips) for a in range(chips)]
    cut_x = [lax.dynamic_slice_in_dim(resid, (i ^ s) * rows, rows, 0) for s in range(n_tok)]
    near_x = [exchange(cut_x, X_STREAMS)]
    far_x = [[cross(a) for a in near_x[0]]]
    for k in range(1, chips):
        first, second = near_x[-1]
        if k == 1:
            second = after(second, table)
        if k == 2:
            w_out, far_x[0][0] = load(w_dec, far_x[0][0], 44)
            first = after(first, far_x[0][0])
            shard_g, = exchange(pick(table, after(resid_grad, first), n_tok), ((0, 1, 2, 3),))
        if k == 3:
            far_x[0][1] = after(far_x[0][1], far_x[1][0])
            w_in, far_x[0][1] = load(w_enc.reshape(n_tok * n_feat, width, feats), far_x[0][1], 36)
            first = after(first, far_x[0][1])
            second = after(second, shard_g)
        near_x[-1] = [first, second]
        if k > 1:
            far_x.append([cross(a) for a in near_x[-1]])
        near_x.append([send(first, ring), send(second, ring)])
    slots = [near_x[0], far_x[0], near_x[1], far_x[1]]
    carry = encode(table, SLOTS["enc_a"], slots, w_in, bias, None, X_STREAMS, False, n_feat)
    far_x.append([cross(near_x[3][0]), cross(after(near_x[3][1], carry))])

    up_pairs = [(a, a + 1) for a in range(chips - 1)]
    down_pairs = [(a + 1, a) for a in range(chips - 1)]
    shard_g = after(shard_g, near_x[-1], carry)
    up_1, down_1 = send(shard_g, up_pairs), send(shard_g, down_pairs)

    slots = [near_x[2], far_x[2], near_x[3], far_x[3]]
    acts, own_x = encode(table, SLOTS["enc_b"], slots, w_in, bias, carry, X_STREAMS, True, n_feat)

    *far_3, near_3 = kernel_call(
        functools.partial(first_body, SLOTS["dec_a"]),
        [((rows // 2, share), BF16)] * 2 + [((rows, share), BF16)],
        [table, acts, w_out],
        "decode",
    )
    up_1, down_1 = after((up_1, down_1), far_3)
    far_in = [cross(a) for a in far_3]
    start, = kernel_call(sum_body, [((rows, share), BF16)], [table, near_3, *far_in], "sum")
    parts = {}
    outs = decode(table, SLOTS["dec_b"], after(acts, start), w_out, share, 6)
    for n, k in enumerate((2, 1, 0)):
        parts[k] = (outs[2 * n + 1], cross(outs[2 * n]))

    def pair_sum(k):
        return parts[k][0].astype(F32) + parts[k][1].astype(F32)

    come = send(start, [(0, 1), (3, 2)])
    up_2, down_2 = send(up_1, up_pairs[1:]), send(down_1, down_pairs[:-1])
    going = (pair_sum(2) + come.astype(F32)).astype(BF16)
    two_g = up_2 + down_2
    three_g = send(two_g, [(2, 3), (1, 0)])

    up = send(going, up_pairs[:2])
    down = send(going, down_pairs[1:])

    slots = [shard_g, cross(shard_g), up_1, cross(up_1), down_1, cross(down_1)]
    carry = project(
        table, SLOTS["proj_a"], slots, w_out, after(acts, going), own_x, b_row, None, False, n_feat
    )
    base = own_x.astype(F32) - b_row - pair_sum(0)

    going_up, going_down = kernel_call(
        functools.partial(third_body, chips),
        [((rows, share), BF16)] * 2,
        [table, *parts[1], near_3, *far_in, up, down],
        "third",
    )
    going_up, going_down = after((going_up, going_down), carry, base)
    up = send(going_up, up_pairs)
    down = send(going_down, down_pairs)

    slots = [two_g, cross(two_g), three_g, cross(three_g)]
    feature_attr, attr = project(
        table, SLOTS["proj_b"], slots, w_out, after(acts, going_up, going_down), own_x, b_row, carry, True, n_feat
    )
    attr = attr[:1]
    attr = attr + cross(attr)
    others = [send(attr, [(a, a ^ k) for a in range(chips)]) for k in range(1, chips)]
    for other in others:
        attr = attr + other

    error = base - (up.astype(F32) + down.astype(F32))
    return feature_attr, error, attr.reshape(rows)


def gathered_program(resid, resid_grad, active, w_enc, b_enc, w_dec, b_dec):
    n_tok = lax.axis_size("tok")
    n_feat = lax.axis_size("feat")
    width = resid.shape[1]

    def rows_of(array):
        part = lax.all_to_all(array, "tok", split_axis=0, concat_axis=1, tiled=True)
        part = part.reshape(part.shape[0], n_tok, 1, width)
        part = lax.all_gather(part, "feat", axis=2, tiled=True)
        return part.reshape(part.shape[0], n_tok * n_feat * width)

    rows_x, rows_g = rows_of(resid), rows_of(resid_grad)
    tok_rows = rows_x.shape[0]
    feat_dev = w_enc.shape[1]
    blocks = feat_dev // BLOCK
    tiles_dev = active.shape[0]
    block_ids = lax.axis_index("feat") * blocks + jnp.arange(blocks, dtype=jnp.int32)
    hits = jnp.any(active[:, :, None] == block_ids[None, None, :], axis=1).astype(F32)
    pre = jnp.dot(rows_x, w_enc, preferred_element_type=F32) + b_enc
    shaped = jnp.maximum(pre, 0.0).reshape(tiles_dev, TILE, blocks, BLOCK) * hits[:, None, :, None]
    acts = shaped.reshape(tok_rows, feat_dev).astype(BF16)
    partial_recon = jnp.dot(acts, w_dec, preferred_element_type=F32)
    recon_share = lax.psum_scatter(
        partial_recon.astype(BF16), "feat", scatter_dimension=1, tiled=True
    ).astype(F32)
    share = recon_share.shape[1]
    start = lax.axis_index("feat") * share
    own_x = lax.dynamic_slice_in_dim(rows_x, start, share, 1)
    own_g = lax.dynamic_slice_in_dim(rows_g, start, share, 1)
    recon = recon_share + b_dec
    error = own_x.astype(F32) - recon
    local_sums = jnp.sum(error * own_g.astype(F32), axis=1)
    error_attr = lax.psum(local_sums, "feat")
    proj = lax.dot_general(rows_g, w_dec, (((1,), (1,)), ((), ())), preferred_element_type=F32)
    return acts.astype(F32) * proj, error, error_attr


def per_device(resid, *rest):
    fits = resid.shape[1] % 128 == 0 and lax.axis_size("tok") == 4 and lax.axis_size("feat") == 8
    return (line_program if fits else gathered_program)(resid, *rest)


def solution(mesh):
    placed = (
        P(None, ("tok", "feat")),
        P(None, ("tok", "feat")),
        P("tok", None),
        P(None, "feat"),
        P("feat"),
        P("feat", None),
        P("feat"),
    )
    return jax.shard_map(
        per_device,
        mesh=mesh,
        in_specs=placed,
        out_specs=(P("tok", "feat"), P("tok", "feat"), P("tok")),
        check_vma=False,
    )
```

```python
import functools

import jax
import jax.numpy as jnp
from jax import lax
from jax.experimental import pallas as pl
from jax.experimental.pallas import tpu as pltpu
from jax.sharding import PartitionSpec as P

BLOCK = 128
TILE = 128
X_STREAMS = ((0, 1), (2, 3))
PIECES = 8
PARAMS = pltpu.CompilerParams(vmem_limit_bytes=20 << 20)
F32 = jnp.float32
BF16 = jnp.bfloat16
LIGHT = pl.CostEstimate(flops=1, bytes_accessed=1, transcendentals=0)
VMEM = pl.BlockSpec(memory_space=pltpu.VMEM)
SMEM = pl.BlockSpec(memory_space=pltpu.SMEM)


def cost(flops, moved):
    return pl.CostEstimate(flops=flops, bytes_accessed=moved, transcendentals=0)


def after(value, *others):
    return lax.optimization_barrier((value, others))[0]


def kernel_call(body, outs, args, name, hint=LIGHT, scratch=()):
    return pl.pallas_call(
        body,
        in_specs=[SMEM] + [VMEM] * (len(args) - 1),
        out_specs=[VMEM] * len(outs),
        out_shape=[jax.ShapeDtypeStruct(shape, kind) for shape, kind in outs],
        scratch_shapes=list(scratch),
        compiler_params=PARAMS,
        cost_estimate=hint,
        name=name,
    )(*args)


def load_body(w_ref, through_ref, out_ref, same_ref, sems):
    step = w_ref.shape[0] // PIECES
    copies = []
    for n in range(PIECES):
        part = pl.ds(n * step, step)
        copies.append(pltpu.make_async_copy(w_ref.at[part], out_ref.at[part], sems.at[n]))
    for copy in copies:
        copy.start()
    for copy in copies:
        copy.wait()


def load(w, through, room):
    anywhere = pl.BlockSpec(memory_space=pl.ANY)
    return pl.pallas_call(
        load_body,
        in_specs=[anywhere, anywhere],
        out_specs=[VMEM, anywhere],
        out_shape=[
            pltpu.VMEM(w.shape, w.dtype),
            jax.ShapeDtypeStruct(through.shape, through.dtype),
        ],
        scratch_shapes=[pltpu.SemaphoreType.DMA((PIECES,))],
        input_output_aliases={1: 1},
        compiler_params=pltpu.CompilerParams(vmem_limit_bytes=room << 20),
        cost_estimate=cost(0, 2 * w.size),
        name="load",
    )(w, through)


SLOTS = {"enc_a": 4, "enc_b": 8, "dec": 12, "proj_a": 20, "proj_b": 32, "hits": 40}


def table_body(n_tok, n_feat, blocks, ids_ref, active_ref, out_ref):
    i, j = ids_ref[0], ids_ref[1]
    chips, ratio = n_feat // 2, n_feat // n_tok
    chip, core = j // 2, j % 2

    def both_cores(place):
        return [2 * place + core, 2 * place + 1 - core]

    def held_slots(*sources):
        values, seen = [], 0
        for place, valid in sources:
            seen = jnp.where(valid, place, seen)
            for source in both_cores(seen):
                values += [source, jnp.where(valid, 1, 0)]
        return values

    numbers = [i, j // ratio, j % ratio, chip]
    for k in range(chips):
        numbers += both_cores((chip + chips - k) % chips)
    for k in (3, 2, 1, 0):
        numbers += both_cores(chip ^ k)[::-1]
    numbers += held_slots((chip, chip >= 0), (chip - 1, chip >= 1), (chip + 1, chip <= chips - 2))
    numbers += held_slots((chip ^ 2, chip >= 0), (chip ^ 3, (chip == 0) | (chip == chips - 1)))
    for n, number in enumerate(numbers):
        out_ref[n] = number
    tiles, listed = active_ref.shape
    for t in range(tiles):
        for b in range(blocks):
            found = jnp.int32(0)
            for n in range(listed):
                found = jnp.where(active_ref[t, n] == j * blocks + b, 1, found)
            out_ref[SLOTS["hits"] + t * blocks + b] = found


def make_table(ids, active, n_tok, n_feat, blocks):
    size = SLOTS["hits"] + active.shape[0] * blocks
    return pl.pallas_call(
        functools.partial(table_body, n_tok, n_feat, blocks),
        in_specs=[SMEM, SMEM],
        out_specs=SMEM,
        out_shape=jax.ShapeDtypeStruct((size,), jnp.int32),
        compiler_params=PARAMS,
        cost_estimate=LIGHT,
        name="table",
    )(ids, active)


def pick_body(table, array_ref, *refs):
    outs, sems = refs[:-1], refs[-1]
    rows = outs[0].shape[0]
    copies = []
    for s, out_ref in enumerate(outs):
        part = array_ref.at[aligned(table[0] ^ s, rows)]
        copies.append(pltpu.make_async_copy(part, out_ref, sems.at[s]))
    for copy in copies:
        copy.start()
    for copy in copies:
        copy.wait()


def pick(table, array, n_tok):
    shape = (array.shape[0] // n_tok, array.shape[1])
    return pl.pallas_call(
        pick_body,
        in_specs=[SMEM, pl.BlockSpec(memory_space=pl.ANY)],
        out_specs=[VMEM] * n_tok,
        out_shape=[jax.ShapeDtypeStruct(shape, array.dtype)] * n_tok,
        scratch_shapes=[pltpu.SemaphoreType.DMA((n_tok,))],
        compiler_params=PARAMS,
        cost_estimate=LIGHT,
        name="pick",
    )(table, array)


def third_body(chips, table, *refs):
    near_1, far_1, near_3, far_3, up_ref, down_ref = refs[:3] + (refs[3:-4],) + refs[-4:-2]
    chip = table[3]
    for target, come_ref, turn in ((refs[-2], up_ref, 1), (refs[-1], down_ref, chips - 2)):

        @pl.when(chip == turn)
        def _():
            rows = far_3[0].shape[0]
            for h, far_ref in enumerate(far_3):
                part = slice(h * rows, (h + 1) * rows)
                total = near_3[part].astype(F32) + far_ref[...].astype(F32)
                target[part] = (total + come_ref[part].astype(F32)).astype(BF16)

        @pl.when(chip != turn)
        def _():
            total = near_1[...].astype(F32) + far_1[...].astype(F32)
            target[...] = (total + come_ref[...].astype(F32)).astype(BF16)


def pieces(refs, streams):
    return [refs[a].at[b] for a, stream in enumerate(streams) for b in range(len(stream))]


def aligned(index, width):
    return pl.ds(pl.multiple_of(index * width, width), width)


def enc_body(streams, count, first, last, n_feat, at, table, *refs):
    size = len(streams)
    slots = [pieces(refs[q * size:(q + 1) * size], streams) for q in range(count)]
    w_ref, bias_ref = refs[count * size:count * size + 2]
    refs = refs[count * size + 2:]
    carry_ref = None
    if not first:
        carry_ref, seen_ref, refs = refs[0], refs[1], refs[2:]
    out_ref, own_ref = refs[:2]
    total_ref = refs[2] if last else out_ref
    n_tok, width = len(slots[0]), slots[0][0].shape[1]
    if not first:
        own_ref[...] = seen_ref[...]
    for q, blocks in enumerate(slots):
        source = table[at + q]
        total = carry_ref if q == 0 else total_ref
        total = None if total is None else total[...]
        for s, x in enumerate(blocks):
            w = w_ref[(table[0] ^ s) * n_feat + source]
            term = jnp.dot(x[...], w, preferred_element_type=F32)
            total = term if total is None else total + term
        total_ref[...] = total
        for s, x in enumerate(blocks):

            @pl.when(((table[0] ^ s) == table[1]) & (source // n_tok == table[2]))
            def _():
                own_ref[:, aligned(source % n_tok, width)] = x[...]

    if last:
        blocks = out_ref.shape[1] // BLOCK
        for t in range(out_ref.shape[0] // TILE):
            for b in range(blocks):
                tile, block = slice(t * TILE, (t + 1) * TILE), slice(b * BLOCK, (b + 1) * BLOCK)
                pre = total_ref[tile, block] + bias_ref[:, block]
                live = table[SLOTS["hits"] + t * blocks + b].astype(F32)
                out_ref[tile, block] = (jnp.maximum(pre, 0.0) * live).astype(BF16)


def encode(table, at, slots, w, bias, carry, streams, last, n_feat):
    width, feats = w.shape[1:]
    rows = slots[0][0].shape[1]
    n_tok = w.shape[0] // n_feat
    args = [table] + [a for slot in slots for a in slot] + [w, bias]
    if carry is not None:
        args += carry
    return kernel_call(
        functools.partial(enc_body, streams, len(slots), carry is None, last, n_feat, at),
        [((rows, feats), BF16 if last else F32), ((rows, n_tok * width), BF16)],
        args,
        "encode",
        LIGHT if last else cost(2 * len(slots) * rows * n_tok * width * feats, 4 << 20),
        [pltpu.VMEM((rows, feats), F32)] if last else [],
    )


def dec_body(at, table, acts_ref, w_ref, *out_refs):
    share = out_refs[0].shape[1]
    for q, targets in enumerate([out_refs[:2]] + [(out_ref,) for out_ref in out_refs[2:]]):
        w = w_ref[:, aligned(table[at + q], share)]
        part = jnp.dot(acts_ref[...], w, preferred_element_type=F32).astype(BF16)
        rows = part.shape[0] // len(targets)
        for h, out_ref in enumerate(targets):
            out_ref[...] = part[h * rows:(h + 1) * rows]


def sum_body(table, near_ref, *refs):
    far_refs, out_ref = refs[:-1], refs[-1]
    rows = far_refs[0].shape[0]
    for h, far_ref in enumerate(far_refs):
        part = slice(h * rows, (h + 1) * rows)
        out_ref[part] = (near_ref[part].astype(F32) + far_ref[...].astype(F32)).astype(BF16)


def proj_body(count, first, last, n_feat, at, table, *refs):
    slots, refs = refs[:count], refs[count:]
    w_ref, acts_ref, x_ref, bias_ref = refs[:4]
    refs = refs[4:]
    if not first:
        carry_ref, seen_ref, refs = refs[0], refs[1], refs[2:]
    out_ref, sum_ref = refs[:2]
    if last:
        out_ref, line_ref, sum_ref = refs
    if first:
        sum_ref[...] = jnp.zeros_like(sum_ref)
    else:
        sum_ref[...] = seen_ref[...]
    for q, g_ref in enumerate(slots):
        n_tok, _, width = g_ref.shape
        source, held = table[at + 2 * q], table[at + 2 * q + 1] == 1

        @pl.when(held)
        def _():
            total = None if q == 0 and first else (carry_ref if q == 0 else out_ref)[...]
            for s in range(n_tok):
                w = w_ref[:, aligned((table[0] ^ s) * n_feat + source, width)]
                term = lax.dot_general(
                    g_ref[s], w, (((1,), (1,)), ((), ())), preferred_element_type=F32
                )
                total = term if total is None else total + term
            out_ref[...] = total

        @pl.when(held & (source // n_tok == table[2]))
        def _():
            cols = aligned(source % n_tok, width)
            term = x_ref[:, cols].astype(F32) - bias_ref[:, cols]
            term = term * g_ref[table[0] ^ table[1]].astype(F32)
            sum_ref[...] += jnp.sum(term, axis=1, keepdims=True)

    if last:
        attr = acts_ref[...].astype(F32) * out_ref[...]
        out_ref[...] = attr
        total = sum_ref[...] - jnp.sum(attr, axis=1, keepdims=True)
        line_ref[...] = jnp.broadcast_to(total, (total.shape[0], TILE)).T[:8]


def project(table, at, slots, w, acts, own_x, bias, carry, last, n_feat):
    rows, feats = acts.shape
    outs = [((rows, feats), F32), ((8, rows), F32) if last else ((rows, 1), F32)]
    return kernel_call(
        functools.partial(proj_body, len(slots), carry is None, last, n_feat, at),
        outs,
        [table, *slots, w, acts, own_x, bias, *(carry or [])],
        "project",
        LIGHT if last else cost(2 * len(slots) * slots[0].size * feats, 4 << 20),
        [pltpu.VMEM((rows, 1), F32)] if last else [],
    )


def line_program(resid, resid_grad, active, w_enc, b_enc, w_dec, b_dec):
    n_tok, n_feat = lax.axis_size("tok"), lax.axis_size("feat")
    i, j = lax.axis_index("tok"), lax.axis_index("feat")
    chips = n_feat // 2
    width = resid.shape[1]
    rows = resid.shape[0] // n_tok
    feats = w_enc.shape[1]
    share = n_tok * width

    def along(pairs):
        return [(2 * a + c, 2 * b + c) for a, b in pairs for c in range(2)]

    def send(array, pairs):
        return lax.ppermute(array, "feat", along(pairs))

    def cross(array):
        return lax.ppermute(array, "feat", [(a, a ^ 1) for a in range(n_feat)])

    def exchange(blocks, streams):
        blocks = list(blocks)
        for s in range(1, n_tok):
            blocks[s] = lax.ppermute(blocks[s], "tok", [(a, a ^ s) for a in range(n_tok)])
        return [jnp.stack([blocks[s] for s in stream]) for stream in streams]

    table = make_table(jnp.stack([i, j]), active, n_tok, n_feat, feats // BLOCK)
    bias = b_enc.reshape(1, feats)
    b_row = b_dec.reshape(1, share)

    ring = [(a, (a + 1) % chips) for a in range(chips)]
    cut_x = [lax.dynamic_slice_in_dim(resid, (i ^ s) * rows, rows, 0) for s in range(n_tok)]
    near_x = [exchange(cut_x, X_STREAMS)]
    far_x = [[cross(a) for a in near_x[0]]]
    for k in range(1, chips):
        first, second = near_x[-1]
        if k == 1:
            second = after(second, table)
        if k == 2:
            w_out, far_x[0][0] = load(w_dec, far_x[0][0], 44)
            first = after(first, far_x[0][0])
        if k == 3:
            far_x[0][1] = after(far_x[0][1], far_x[1][0])
            w_in, far_x[0][1] = load(w_enc.reshape(n_tok * n_feat, width, feats), far_x[0][1], 36)
            first = after(first, far_x[0][1])
            shard_g, = exchange(pick(table, after(resid_grad, first), n_tok), ((0, 1, 2, 3),))
        near_x[-1] = [first, second]
        if k > 1:
            far_x.append([cross(a) for a in near_x[-1]])
        near_x.append([send(first, ring), send(second, ring)])
    slots = [near_x[0], far_x[0], near_x[1], far_x[1]]
    carry = encode(
        after(table, shard_g), SLOTS["enc_a"], slots, w_in, bias, None, X_STREAMS, False, n_feat
    )
    far_x.append([cross(near_x[3][0]), cross(after(near_x[3][1], carry))])

    up_pairs = [(a, a + 1) for a in range(chips - 1)]
    down_pairs = [(a + 1, a) for a in range(chips - 1)]
    shard_g = after(shard_g, near_x[-1], carry)
    up_1, down_1 = send(shard_g, up_pairs), send(shard_g, down_pairs)

    slots = [near_x[2], far_x[2], near_x[3], far_x[3]]
    acts, own_x = encode(table, SLOTS["enc_b"], slots, w_in, bias, carry, X_STREAMS, True, n_feat)

    far_3_a, far_3_b, near_3, *outs = kernel_call(
        functools.partial(dec_body, SLOTS["dec"]),
        [((rows // 2, share), BF16)] * 2 + [((rows, share), BF16)] * (2 * chips - 1),
        [table, acts, w_out],
        "decode",
    )
    up_1, down_1 = after((up_1, down_1), far_3_a)
    far_in = [cross(far_3_a), cross(far_3_b)]
    start, = kernel_call(sum_body, [((rows, share), BF16)], [table, near_3, *far_in], "sum")
    outs = after(outs, start)
    parts = {k: (outs[2 * n + 1], cross(outs[2 * n])) for n, k in enumerate((2, 1, 0))}

    def pair_sum(k):
        return parts[k][0].astype(F32) + parts[k][1].astype(F32)

    come = send(start, [(0, 1), (3, 2)])
    up_2, down_2 = send(up_1, up_pairs[1:]), send(down_1, down_pairs[:-1])
    going = (pair_sum(2) + come.astype(F32)).astype(BF16)
    two_g = up_2 + down_2
    three_g = send(two_g, [(2, 3), (1, 0)])

    up = send(going, up_pairs[:2])
    down = send(going, down_pairs[1:])

    slots = [shard_g, cross(shard_g), up_1, cross(up_1), down_1, cross(down_1)]
    carry = project(
        table, SLOTS["proj_a"], slots, w_out, after(acts, going), own_x, b_row, None, False, n_feat
    )
    base = own_x.astype(F32) - b_row - pair_sum(0)

    going_up, going_down = kernel_call(
        functools.partial(third_body, chips),
        [((rows, share), BF16)] * 2,
        [table, *parts[1], near_3, *far_in, up, down],
        "third",
    )
    going_up, going_down = after((going_up, going_down), carry, base)
    up = send(going_up, up_pairs)
    down = send(going_down, down_pairs)

    slots = [two_g, cross(two_g), three_g, cross(three_g)]
    feature_attr, attr = project(
        table, SLOTS["proj_b"], slots, w_out, after(acts, going_up, going_down), own_x, b_row, carry, True, n_feat
    )
    attr = attr[:1]
    attr = attr + cross(attr)
    others = [send(attr, [(a, a ^ k) for a in range(chips)]) for k in range(1, chips)]
    for other in others:
        attr = attr + other

    error = base - (up.astype(F32) + down.astype(F32))
    return feature_attr, error, attr.reshape(rows)


def gathered_program(resid, resid_grad, active, w_enc, b_enc, w_dec, b_dec):
    n_tok = lax.axis_size("tok")
    n_feat = lax.axis_size("feat")
    width = resid.shape[1]

    def rows_of(array):
        part = lax.all_to_all(array, "tok", split_axis=0, concat_axis=1, tiled=True)
        part = part.reshape(part.shape[0], n_tok, 1, width)
        part = lax.all_gather(part, "feat", axis=2, tiled=True)
        return part.reshape(part.shape[0], n_tok * n_feat * width)

    rows_x, rows_g = rows_of(resid), rows_of(resid_grad)
    tok_rows = rows_x.shape[0]
    feat_dev = w_enc.shape[1]
    blocks = feat_dev // BLOCK
    tiles_dev = active.shape[0]
    block_ids = lax.axis_index("feat") * blocks + jnp.arange(blocks, dtype=jnp.int32)
    hits = jnp.any(active[:, :, None] == block_ids[None, None, :], axis=1).astype(F32)
    pre = jnp.dot(rows_x, w_enc, preferred_element_type=F32) + b_enc
    shaped = jnp.maximum(pre, 0.0).reshape(tiles_dev, TILE, blocks, BLOCK) * hits[:, None, :, None]
    acts = shaped.reshape(tok_rows, feat_dev).astype(BF16)
    partial_recon = jnp.dot(acts, w_dec, preferred_element_type=F32)
    recon_share = lax.psum_scatter(
        partial_recon.astype(BF16), "feat", scatter_dimension=1, tiled=True
    ).astype(F32)
    share = recon_share.shape[1]
    start = lax.axis_index("feat") * share
    own_x = lax.dynamic_slice_in_dim(rows_x, start, share, 1)
    own_g = lax.dynamic_slice_in_dim(rows_g, start, share, 1)
    recon = recon_share + b_dec
    error = own_x.astype(F32) - recon
    local_sums = jnp.sum(error * own_g.astype(F32), axis=1)
    error_attr = lax.psum(local_sums, "feat")
    proj = lax.dot_general(rows_g, w_dec, (((1,), (1,)), ((), ())), preferred_element_type=F32)
    return acts.astype(F32) * proj, error, error_attr


def per_device(resid, *rest):
    fits = resid.shape[1] % 128 == 0 and lax.axis_size("tok") == 4 and lax.axis_size("feat") == 8
    return (line_program if fits else gathered_program)(resid, *rest)


def solution(mesh):
    placed = (
        P(None, ("tok", "feat")),
        P(None, ("tok", "feat")),
        P("tok", None),
        P(None, "feat"),
        P("feat"),
        P("feat", None),
        P("feat"),
    )
    return jax.shard_map(
        per_device,
        mesh=mesh,
        in_specs=placed,
        out_specs=(P("tok", "feat"), P("tok", "feat"), P("tok")),
        check_vma=False,
    )
```

```python
import functools

import jax
import jax.numpy as jnp
from jax import lax
from jax.experimental import pallas as pl
from jax.experimental.pallas import tpu as pltpu
from jax.sharding import PartitionSpec as P

BLOCK = 128
TILE = 128
X_STREAMS = ((0, 1), (2, 3))
PIECES = 8
PARAMS = pltpu.CompilerParams(vmem_limit_bytes=20 << 20)
F32 = jnp.float32
BF16 = jnp.bfloat16
LIGHT = pl.CostEstimate(flops=1, bytes_accessed=1, transcendentals=0)
VMEM = pl.BlockSpec(memory_space=pltpu.VMEM)
SMEM = pl.BlockSpec(memory_space=pltpu.SMEM)


def cost(flops, moved):
    return pl.CostEstimate(flops=flops, bytes_accessed=moved, transcendentals=0)


def after(value, *others):
    return lax.optimization_barrier((value, others))[0]


def kernel_call(body, outs, args, name, hint=LIGHT, scratch=()):
    return pl.pallas_call(
        body,
        in_specs=[SMEM] + [VMEM] * (len(args) - 1),
        out_specs=[VMEM] * len(outs),
        out_shape=[jax.ShapeDtypeStruct(shape, kind) for shape, kind in outs],
        scratch_shapes=list(scratch),
        compiler_params=PARAMS,
        cost_estimate=hint,
        name=name,
    )(*args)


def load_body(w_ref, through_ref, out_ref, same_ref, sems):
    step = w_ref.shape[0] // PIECES
    copies = []
    for n in range(PIECES):
        part = pl.ds(n * step, step)
        copies.append(pltpu.make_async_copy(w_ref.at[part], out_ref.at[part], sems.at[n]))
    for copy in copies:
        copy.start()
    for copy in copies:
        copy.wait()


def load(w, through, room):
    anywhere = pl.BlockSpec(memory_space=pl.ANY)
    return pl.pallas_call(
        load_body,
        in_specs=[anywhere, anywhere],
        out_specs=[VMEM, anywhere],
        out_shape=[
            pltpu.VMEM(w.shape, w.dtype),
            jax.ShapeDtypeStruct(through.shape, through.dtype),
        ],
        scratch_shapes=[pltpu.SemaphoreType.DMA((PIECES,))],
        input_output_aliases={1: 1},
        compiler_params=pltpu.CompilerParams(vmem_limit_bytes=room << 20),
        cost_estimate=cost(0, 2 * w.size),
        name="load",
    )(w, through)


SLOTS = {"enc_a": 4, "enc_b": 8, "dec": 12, "proj_a": 20, "proj_b": 32, "hits": 40}


def table_body(n_tok, n_feat, blocks, ids_ref, active_ref, out_ref):
    i, j = ids_ref[0], ids_ref[1]
    chips, ratio = n_feat // 2, n_feat // n_tok
    chip, core = j // 2, j % 2

    def both_cores(place):
        return [2 * place + core, 2 * place + 1 - core]

    def held_slots(*sources):
        values, seen = [], 0
        for place, valid in sources:
            seen = jnp.where(valid, place, seen)
            for source in both_cores(seen):
                values += [source, jnp.where(valid, 1, 0)]
        return values

    numbers = [i, j // ratio, j % ratio, chip]
    for k in range(chips):
        numbers += both_cores((chip + chips - k) % chips)
    for k in (3, 2, 1, 0):
        numbers += both_cores(chip ^ k)[::-1]
    numbers += held_slots((chip, chip >= 0), (chip - 1, chip >= 1), (chip + 1, chip <= chips - 2))
    numbers += held_slots((chip ^ 2, chip >= 0), (chip ^ 3, (chip == 0) | (chip == chips - 1)))
    for n, number in enumerate(numbers):
        out_ref[n] = number
    tiles, listed = active_ref.shape
    for t in range(tiles):
        for b in range(blocks):
            found = jnp.int32(0)
            for n in range(listed):
                found = jnp.where(active_ref[t, n] == j * blocks + b, 1, found)
            out_ref[SLOTS["hits"] + t * blocks + b] = found


def make_table(ids, active, n_tok, n_feat, blocks):
    size = SLOTS["hits"] + active.shape[0] * blocks
    return pl.pallas_call(
        functools.partial(table_body, n_tok, n_feat, blocks),
        in_specs=[SMEM, SMEM],
        out_specs=SMEM,
        out_shape=jax.ShapeDtypeStruct((size,), jnp.int32),
        compiler_params=PARAMS,
        cost_estimate=LIGHT,
        name="table",
    )(ids, active)


def pick_body(table, array_ref, *refs):
    outs, sems = refs[:-1], refs[-1]
    rows = outs[0].shape[0]
    copies = []
    for s, out_ref in enumerate(outs):
        part = array_ref.at[aligned(table[0] ^ s, rows)]
        copies.append(pltpu.make_async_copy(part, out_ref, sems.at[s]))
    for copy in copies:
        copy.start()
    for copy in copies:
        copy.wait()


def pick(table, array, n_tok):
    shape = (array.shape[0] // n_tok, array.shape[1])
    return pl.pallas_call(
        pick_body,
        in_specs=[SMEM, pl.BlockSpec(memory_space=pl.ANY)],
        out_specs=[VMEM] * n_tok,
        out_shape=[jax.ShapeDtypeStruct(shape, array.dtype)] * n_tok,
        scratch_shapes=[pltpu.SemaphoreType.DMA((n_tok,))],
        compiler_params=PARAMS,
        cost_estimate=LIGHT,
        name="pick",
    )(table, array)


def third_body(chips, table, *refs):
    near_1, far_1, near_3, far_3, up_ref, down_ref = refs[:3] + (refs[3:-4],) + refs[-4:-2]
    chip = table[3]
    for target, come_ref, turn in ((refs[-2], up_ref, 1), (refs[-1], down_ref, chips - 2)):

        @pl.when(chip == turn)
        def _():
            rows = far_3[0].shape[0]
            for h, far_ref in enumerate(far_3):
                part = slice(h * rows, (h + 1) * rows)
                total = near_3[part].astype(F32) + far_ref[...].astype(F32)
                target[part] = (total + come_ref[part].astype(F32)).astype(BF16)

        @pl.when(chip != turn)
        def _():
            total = near_1[...].astype(F32) + far_1[...].astype(F32)
            target[...] = (total + come_ref[...].astype(F32)).astype(BF16)


def pieces(refs, streams):
    return [refs[a].at[b] for a, stream in enumerate(streams) for b in range(len(stream))]


def aligned(index, width):
    return pl.ds(pl.multiple_of(index * width, width), width)


def enc_body(streams, count, first, last, n_feat, at, table, *refs):
    size = len(streams)
    slots = [pieces(refs[q * size:(q + 1) * size], streams) for q in range(count)]
    w_ref, bias_ref = refs[count * size:count * size + 2]
    refs = refs[count * size + 2:]
    carry_ref = None
    if not first:
        carry_ref, seen_ref, refs = refs[0], refs[1], refs[2:]
    out_ref, own_ref = refs[:2]
    total_ref = refs[2] if last else out_ref
    n_tok, width = len(slots[0]), slots[0][0].shape[1]
    if not first:
        own_ref[...] = seen_ref[...]
    for q, blocks in enumerate(slots):
        source = table[at + q]
        total = carry_ref if q == 0 else total_ref
        total = None if total is None else total[...]
        for s, x in enumerate(blocks):
            w = w_ref[(table[0] ^ s) * n_feat + source]
            term = jnp.dot(x[...], w, preferred_element_type=F32)
            total = term if total is None else total + term
        total_ref[...] = total
        for s, x in enumerate(blocks):

            @pl.when(((table[0] ^ s) == table[1]) & (source // n_tok == table[2]))
            def _():
                own_ref[:, aligned(source % n_tok, width)] = x[...]

    if last:
        blocks = out_ref.shape[1] // BLOCK
        for t in range(out_ref.shape[0] // TILE):
            for b in range(blocks):
                tile, block = slice(t * TILE, (t + 1) * TILE), slice(b * BLOCK, (b + 1) * BLOCK)
                pre = total_ref[tile, block] + bias_ref[:, block]
                live = table[SLOTS["hits"] + t * blocks + b].astype(F32)
                out_ref[tile, block] = (jnp.maximum(pre, 0.0) * live).astype(BF16)


def encode(table, at, slots, w, bias, carry, streams, last, n_feat):
    width, feats = w.shape[1:]
    rows = slots[0][0].shape[1]
    n_tok = w.shape[0] // n_feat
    args = [table] + [a for slot in slots for a in slot] + [w, bias]
    if carry is not None:
        args += carry
    return kernel_call(
        functools.partial(enc_body, streams, len(slots), carry is None, last, n_feat, at),
        [((rows, feats), BF16 if last else F32), ((rows, n_tok * width), BF16)],
        args,
        "encode",
        LIGHT if last else cost(2 * len(slots) * rows * n_tok * width * feats, 4 << 20),
        [pltpu.VMEM((rows, feats), F32)] if last else [],
    )


def dec_body(at, table, acts_ref, w_ref, *out_refs):
    share = out_refs[0].shape[1]
    for q, targets in enumerate([out_refs[:2]] + [(out_ref,) for out_ref in out_refs[2:]]):
        w = w_ref[:, aligned(table[at + q], share)]
        part = jnp.dot(acts_ref[...], w, preferred_element_type=F32).astype(BF16)
        rows = part.shape[0] // len(targets)
        for h, out_ref in enumerate(targets):
            out_ref[...] = part[h * rows:(h + 1) * rows]


def sum_body(table, near_ref, *refs):
    far_refs, out_ref = refs[:-1], refs[-1]
    rows = far_refs[0].shape[0]
    for h, far_ref in enumerate(far_refs):
        part = slice(h * rows, (h + 1) * rows)
        out_ref[part] = (near_ref[part].astype(F32) + far_ref[...].astype(F32)).astype(BF16)


def proj_body(count, first, last, n_feat, at, table, *refs):
    slots, refs = refs[:count], refs[count:]
    w_ref, acts_ref, x_ref, bias_ref = refs[:4]
    refs = refs[4:]
    if not first:
        carry_ref, seen_ref, refs = refs[0], refs[1], refs[2:]
    out_ref, sum_ref = refs[:2]
    if last:
        out_ref, line_ref, sum_ref = refs
    if first:
        sum_ref[...] = jnp.zeros_like(sum_ref)
    else:
        sum_ref[...] = seen_ref[...]
    for q, g_ref in enumerate(slots):
        n_tok, _, width = g_ref.shape
        source, held = table[at + 2 * q], table[at + 2 * q + 1] == 1

        @pl.when(held)
        def _():
            total = None if q == 0 and first else (carry_ref if q == 0 else out_ref)[...]
            for s in range(n_tok):
                w = w_ref[:, aligned((table[0] ^ s) * n_feat + source, width)]
                term = lax.dot_general(
                    g_ref[s], w, (((1,), (1,)), ((), ())), preferred_element_type=F32
                )
                total = term if total is None else total + term
            out_ref[...] = total

        @pl.when(held & (source // n_tok == table[2]))
        def _():
            cols = aligned(source % n_tok, width)
            term = x_ref[:, cols].astype(F32) - bias_ref[:, cols]
            term = term * g_ref[table[0] ^ table[1]].astype(F32)
            sum_ref[...] += jnp.sum(term, axis=1, keepdims=True)

    if last:
        attr = acts_ref[...].astype(F32) * out_ref[...]
        out_ref[...] = attr
        total = sum_ref[...] - jnp.sum(attr, axis=1, keepdims=True)
        line_ref[...] = jnp.broadcast_to(total, (total.shape[0], TILE)).T[:8]


def project(table, at, slots, w, acts, own_x, bias, carry, last, n_feat):
    rows, feats = acts.shape
    outs = [((rows, feats), F32), ((8, rows), F32) if last else ((rows, 1), F32)]
    return kernel_call(
        functools.partial(proj_body, len(slots), carry is None, last, n_feat, at),
        outs,
        [table, *slots, w, acts, own_x, bias, *(carry or [])],
        "project",
        LIGHT if last else cost(2 * len(slots) * slots[0].size * feats, 4 << 20),
        [pltpu.VMEM((rows, 1), F32)] if last else [],
    )


def line_program(resid, resid_grad, active, w_enc, b_enc, w_dec, b_dec):
    n_tok, n_feat = lax.axis_size("tok"), lax.axis_size("feat")
    i, j = lax.axis_index("tok"), lax.axis_index("feat")
    chips = n_feat // 2
    width = resid.shape[1]
    rows = resid.shape[0] // n_tok
    feats = w_enc.shape[1]
    share = n_tok * width

    def along(pairs):
        return [(2 * a + c, 2 * b + c) for a, b in pairs for c in range(2)]

    def send(array, pairs):
        return lax.ppermute(array, "feat", along(pairs))

    def cross(array):
        return lax.ppermute(array, "feat", [(a, a ^ 1) for a in range(n_feat)])

    def exchange(blocks, streams):
        blocks = list(blocks)
        for s in range(1, n_tok):
            blocks[s] = lax.ppermute(blocks[s], "tok", [(a, a ^ s) for a in range(n_tok)])
        return [jnp.stack([blocks[s] for s in stream]) for stream in streams]

    table = make_table(jnp.stack([i, j]), active, n_tok, n_feat, feats // BLOCK)
    bias = b_enc.reshape(1, feats)
    b_row = b_dec.reshape(1, share)

    ring = [(a, (a + 1) % chips) for a in range(chips)]
    cut_x = [lax.dynamic_slice_in_dim(resid, (i ^ s) * rows, rows, 0) for s in range(n_tok)]
    near_x = [exchange(cut_x, X_STREAMS)]
    far_x = [[cross(a) for a in near_x[0]]]
    for k in range(1, chips):
        first, second = near_x[-1]
        if k == 1:
            second = after(second, table)
        if k == 2:
            w_out, far_x[0][0] = load(w_dec, far_x[0][0], 44)
            first = after(first, far_x[0][0])
        if k == 3:
            far_x[0][1] = after(far_x[0][1], far_x[1][0])
            w_in, far_x[0][1] = load(w_enc.reshape(n_tok * n_feat, width, feats), far_x[0][1], 36)
            first = after(first, far_x[0][1])
            shard_g, = exchange(pick(table, after(resid_grad, first), n_tok), ((0, 1, 2, 3),))
        near_x[-1] = [first, second]
        if k > 1:
            far_x.append([cross(a) for a in near_x[-1]])
        near_x.append([send(first, ring), send(second, ring)])
    slots = [near_x[0], far_x[0], near_x[1], far_x[1]]
    carry = encode(
        table, SLOTS["enc_a"], slots, w_in, bias, None, X_STREAMS, False, n_feat
    )
    far_x.append([cross(after(near_x[3][0], shard_g)), cross(after(near_x[3][1], carry))])

    up_pairs = [(a, a + 1) for a in range(chips - 1)]
    down_pairs = [(a + 1, a) for a in range(chips - 1)]
    shard_g = after(shard_g, near_x[-1], carry)
    up_1, down_1 = send(shard_g, up_pairs), send(shard_g, down_pairs)

    slots = [near_x[2], far_x[2], near_x[3], far_x[3]]
    acts, own_x = encode(table, SLOTS["enc_b"], slots, w_in, bias, carry, X_STREAMS, True, n_feat)

    far_3_a, far_3_b, near_3, *outs = kernel_call(
        functools.partial(dec_body, SLOTS["dec"]),
        [((rows // 2, share), BF16)] * 2 + [((rows, share), BF16)] * (2 * chips - 1),
        [table, acts, w_out],
        "decode",
    )
    up_1, down_1 = after((up_1, down_1), far_3_a)
    far_in = [cross(far_3_a), cross(far_3_b)]
    start, = kernel_call(sum_body, [((rows, share), BF16)], [table, near_3, *far_in], "sum")
    outs = after(outs, start)
    parts = {k: (outs[2 * n + 1], cross(outs[2 * n])) for n, k in enumerate((2, 1, 0))}

    def pair_sum(k):
        return parts[k][0].astype(F32) + parts[k][1].astype(F32)

    come = send(start, [(0, 1), (3, 2)])
    up_2, down_2 = send(up_1, up_pairs[1:]), send(down_1, down_pairs[:-1])
    going = (pair_sum(2) + come.astype(F32)).astype(BF16)
    two_g = up_2 + down_2
    three_g = send(two_g, [(2, 3), (1, 0)])

    up = send(going, up_pairs[:2])
    down = send(going, down_pairs[1:])

    slots = [shard_g, cross(shard_g), up_1, cross(up_1), down_1, cross(down_1)]
    carry = project(
        table, SLOTS["proj_a"], slots, w_out, after(acts, going), own_x, b_row, None, False, n_feat
    )
    base = own_x.astype(F32) - b_row - pair_sum(0)

    going_up, going_down = kernel_call(
        functools.partial(third_body, chips),
        [((rows, share), BF16)] * 2,
        [table, *parts[1], near_3, *far_in, up, down],
        "third",
    )
    going_up, going_down = after((going_up, going_down), carry, base)
    up = send(going_up, up_pairs)
    down = send(going_down, down_pairs)

    slots = [two_g, cross(two_g), three_g, cross(three_g)]
    feature_attr, attr = project(
        table, SLOTS["proj_b"], slots, w_out, after(acts, going_up, going_down), own_x, b_row, carry, True, n_feat
    )
    attr = attr[:1]
    attr = attr + cross(attr)
    others = [send(attr, [(a, a ^ k) for a in range(chips)]) for k in range(1, chips)]
    for other in others:
        attr = attr + other

    error = base - (up.astype(F32) + down.astype(F32))
    return feature_attr, error, attr.reshape(rows)


def gathered_program(resid, resid_grad, active, w_enc, b_enc, w_dec, b_dec):
    n_tok = lax.axis_size("tok")
    n_feat = lax.axis_size("feat")
    width = resid.shape[1]

    def rows_of(array):
        part = lax.all_to_all(array, "tok", split_axis=0, concat_axis=1, tiled=True)
        part = part.reshape(part.shape[0], n_tok, 1, width)
        part = lax.all_gather(part, "feat", axis=2, tiled=True)
        return part.reshape(part.shape[0], n_tok * n_feat * width)

    rows_x, rows_g = rows_of(resid), rows_of(resid_grad)
    tok_rows = rows_x.shape[0]
    feat_dev = w_enc.shape[1]
    blocks = feat_dev // BLOCK
    tiles_dev = active.shape[0]
    block_ids = lax.axis_index("feat") * blocks + jnp.arange(blocks, dtype=jnp.int32)
    hits = jnp.any(active[:, :, None] == block_ids[None, None, :], axis=1).astype(F32)
    pre = jnp.dot(rows_x, w_enc, preferred_element_type=F32) + b_enc
    shaped = jnp.maximum(pre, 0.0).reshape(tiles_dev, TILE, blocks, BLOCK) * hits[:, None, :, None]
    acts = shaped.reshape(tok_rows, feat_dev).astype(BF16)
    partial_recon = jnp.dot(acts, w_dec, preferred_element_type=F32)
    recon_share = lax.psum_scatter(
        partial_recon.astype(BF16), "feat", scatter_dimension=1, tiled=True
    ).astype(F32)
    share = recon_share.shape[1]
    start = lax.axis_index("feat") * share
    own_x = lax.dynamic_slice_in_dim(rows_x, start, share, 1)
    own_g = lax.dynamic_slice_in_dim(rows_g, start, share, 1)
    recon = recon_share + b_dec
    error = own_x.astype(F32) - recon
    local_sums = jnp.sum(error * own_g.astype(F32), axis=1)
    error_attr = lax.psum(local_sums, "feat")
    proj = lax.dot_general(rows_g, w_dec, (((1,), (1,)), ((), ())), preferred_element_type=F32)
    return acts.astype(F32) * proj, error, error_attr


def per_device(resid, *rest):
    fits = resid.shape[1] % 128 == 0 and lax.axis_size("tok") == 4 and lax.axis_size("feat") == 8
    return (line_program if fits else gathered_program)(resid, *rest)


def solution(mesh):
    placed = (
        P(None, ("tok", "feat")),
        P(None, ("tok", "feat")),
        P("tok", None),
        P(None, "feat"),
        P("feat"),
        P("feat", None),
        P("feat"),
    )
    return jax.shard_map(
        per_device,
        mesh=mesh,
        in_specs=placed,
        out_specs=(P("tok", "feat"), P("tok", "feat"), P("tok")),
        check_vma=False,
    )
```

```python
import functools

import jax
import jax.numpy as jnp
from jax import lax
from jax.experimental import pallas as pl
from jax.experimental.pallas import tpu as pltpu
from jax.sharding import PartitionSpec as P

BLOCK = 128
TILE = 128
X_STREAMS = ((0, 1), (2, 3))
PIECES = 8
PARAMS = pltpu.CompilerParams(vmem_limit_bytes=20 << 20)
F32 = jnp.float32
BF16 = jnp.bfloat16
LIGHT = pl.CostEstimate(flops=1, bytes_accessed=1, transcendentals=0)
VMEM = pl.BlockSpec(memory_space=pltpu.VMEM)
SMEM = pl.BlockSpec(memory_space=pltpu.SMEM)


def cost(flops, moved):
    return pl.CostEstimate(flops=flops, bytes_accessed=moved, transcendentals=0)


def after(value, *others):
    return lax.optimization_barrier((value, others))[0]


def kernel_call(body, outs, args, name, hint=LIGHT, scratch=()):
    return pl.pallas_call(
        body,
        in_specs=[SMEM] + [VMEM] * (len(args) - 1),
        out_specs=[VMEM] * len(outs),
        out_shape=[jax.ShapeDtypeStruct(shape, kind) for shape, kind in outs],
        scratch_shapes=list(scratch),
        compiler_params=PARAMS,
        cost_estimate=hint,
        name=name,
    )(*args)


def load_body(w_ref, through_ref, out_ref, same_ref, sems):
    step = w_ref.shape[0] // PIECES
    copies = []
    for n in range(PIECES):
        part = pl.ds(n * step, step)
        copies.append(pltpu.make_async_copy(w_ref.at[part], out_ref.at[part], sems.at[n]))
    for copy in copies:
        copy.start()
    for copy in copies:
        copy.wait()


def load(w, through, room):
    anywhere = pl.BlockSpec(memory_space=pl.ANY)
    return pl.pallas_call(
        load_body,
        in_specs=[anywhere, anywhere],
        out_specs=[VMEM, anywhere],
        out_shape=[
            pltpu.VMEM(w.shape, w.dtype),
            jax.ShapeDtypeStruct(through.shape, through.dtype),
        ],
        scratch_shapes=[pltpu.SemaphoreType.DMA((PIECES,))],
        input_output_aliases={1: 1},
        compiler_params=pltpu.CompilerParams(vmem_limit_bytes=room << 20),
        cost_estimate=cost(0, 2 * w.size),
        name="load",
    )(w, through)


SLOTS = {"enc_a": 4, "enc_b": 8, "dec": 12, "proj_a": 20, "proj_b": 32, "hits": 40}


def table_body(n_tok, n_feat, blocks, ids_ref, active_ref, out_ref):
    i, j = ids_ref[0], ids_ref[1]
    chips, ratio = n_feat // 2, n_feat // n_tok
    chip, core = j // 2, j % 2

    def both_cores(place):
        return [2 * place + core, 2 * place + 1 - core]

    def held_slots(*sources):
        values, seen = [], 0
        for place, valid in sources:
            seen = jnp.where(valid, place, seen)
            for source in both_cores(seen):
                values += [source, jnp.where(valid, 1, 0)]
        return values

    numbers = [i, j // ratio, j % ratio, chip]
    for k in range(chips):
        numbers += both_cores((chip + chips - k) % chips)
    for k in (3, 2, 1, 0):
        numbers += both_cores(chip ^ k)[::-1]
    numbers += held_slots((chip, chip >= 0), (chip - 1, chip >= 1), (chip + 1, chip <= chips - 2))
    numbers += held_slots((chip ^ 2, chip >= 0), (chip ^ 3, (chip == 0) | (chip == chips - 1)))
    for n, number in enumerate(numbers):
        out_ref[n] = number
    tiles, listed = active_ref.shape
    for t in range(tiles):
        for b in range(blocks):
            found = jnp.int32(0)
            for n in range(listed):
                found = jnp.where(active_ref[t, n] == j * blocks + b, 1, found)
            out_ref[SLOTS["hits"] + t * blocks + b] = found


def make_table(ids, active, n_tok, n_feat, blocks):
    size = SLOTS["hits"] + active.shape[0] * blocks
    return pl.pallas_call(
        functools.partial(table_body, n_tok, n_feat, blocks),
        in_specs=[SMEM, SMEM],
        out_specs=SMEM,
        out_shape=jax.ShapeDtypeStruct((size,), jnp.int32),
        compiler_params=PARAMS,
        cost_estimate=LIGHT,
        name="table",
    )(ids, active)


def pick_body(table, array_ref, *refs):
    outs, sems = refs[:-1], refs[-1]
    rows = outs[0].shape[0]
    copies = []
    for s, out_ref in enumerate(outs):
        part = array_ref.at[aligned(table[0] ^ s, rows)]
        copies.append(pltpu.make_async_copy(part, out_ref, sems.at[s]))
    for copy in copies:
        copy.start()
    for copy in copies:
        copy.wait()


def pick(table, array, n_tok):
    shape = (array.shape[0] // n_tok, array.shape[1])
    return pl.pallas_call(
        pick_body,
        in_specs=[SMEM, pl.BlockSpec(memory_space=pl.ANY)],
        out_specs=[VMEM] * n_tok,
        out_shape=[jax.ShapeDtypeStruct(shape, array.dtype)] * n_tok,
        scratch_shapes=[pltpu.SemaphoreType.DMA((n_tok,))],
        compiler_params=PARAMS,
        cost_estimate=LIGHT,
        name="pick",
    )(table, array)


def third_body(chips, table, *refs):
    near_1, far_1, near_3, far_3, up_ref, down_ref = refs[:3] + (refs[3:-4],) + refs[-4:-2]
    chip = table[3]
    for target, come_ref, turn in ((refs[-2], up_ref, 1), (refs[-1], down_ref, chips - 2)):

        @pl.when(chip == turn)
        def _():
            rows = far_3[0].shape[0]
            for h, far_ref in enumerate(far_3):
                part = slice(h * rows, (h + 1) * rows)
                total = near_3[part].astype(F32) + far_ref[...].astype(F32)
                target[part] = (total + come_ref[part].astype(F32)).astype(BF16)

        @pl.when(chip != turn)
        def _():
            total = near_1[...].astype(F32) + far_1[...].astype(F32)
            target[...] = (total + come_ref[...].astype(F32)).astype(BF16)


def pieces(refs, streams):
    return [refs[a].at[b] for a, stream in enumerate(streams) for b in range(len(stream))]


def aligned(index, width):
    return pl.ds(pl.multiple_of(index * width, width), width)


def enc_body(streams, count, first, last, n_feat, at, table, *refs):
    size = len(streams)
    slots = [pieces(refs[q * size:(q + 1) * size], streams) for q in range(count)]
    w_ref, bias_ref = refs[count * size:count * size + 2]
    refs = refs[count * size + 2:]
    carry_ref = None
    if not first:
        carry_ref, seen_ref, refs = refs[0], refs[1], refs[2:]
    out_ref, own_ref = refs[:2]
    total_ref = refs[2] if last else out_ref
    n_tok, width = len(slots[0]), slots[0][0].shape[1]
    if not first:
        own_ref[...] = seen_ref[...]
    for q, blocks in enumerate(slots):
        source = table[at + q]
        total = carry_ref if q == 0 else total_ref
        total = None if total is None else total[...]
        for s, x in enumerate(blocks):
            w = w_ref[(table[0] ^ s) * n_feat + source]
            term = jnp.dot(x[...], w, preferred_element_type=F32)
            total = term if total is None else total + term
        total_ref[...] = total
        for s, x in enumerate(blocks):

            @pl.when(((table[0] ^ s) == table[1]) & (source // n_tok == table[2]))
            def _():
                own_ref[:, aligned(source % n_tok, width)] = x[...]

    if last:
        blocks = out_ref.shape[1] // BLOCK
        for t in range(out_ref.shape[0] // TILE):
            for b in range(blocks):
                tile, block = slice(t * TILE, (t + 1) * TILE), slice(b * BLOCK, (b + 1) * BLOCK)
                pre = total_ref[tile, block] + bias_ref[:, block]
                live = table[SLOTS["hits"] + t * blocks + b].astype(F32)
                out_ref[tile, block] = (jnp.maximum(pre, 0.0) * live).astype(BF16)


def encode(table, at, slots, w, bias, carry, streams, last, n_feat):
    width, feats = w.shape[1:]
    rows = slots[0][0].shape[1]
    n_tok = w.shape[0] // n_feat
    args = [table] + [a for slot in slots for a in slot] + [w, bias]
    if carry is not None:
        args += carry
    return kernel_call(
        functools.partial(enc_body, streams, len(slots), carry is None, last, n_feat, at),
        [((rows, feats), BF16 if last else F32), ((rows, n_tok * width), BF16)],
        args,
        "encode",
        LIGHT if last else cost(2 * len(slots) * rows * n_tok * width * feats, 4 << 20),
        [pltpu.VMEM((rows, feats), F32)] if last else [],
    )


def dec_body(at, table, acts_ref, w_ref, *out_refs):
    share = out_refs[0].shape[1]
    for q, targets in enumerate([out_refs[:2]] + [(out_ref,) for out_ref in out_refs[2:]]):
        w = w_ref[:, aligned(table[at + q], share)]
        part = jnp.dot(acts_ref[...], w, preferred_element_type=F32).astype(BF16)
        rows = part.shape[0] // len(targets)
        for h, out_ref in enumerate(targets):
            out_ref[...] = part[h * rows:(h + 1) * rows]


def sum_body(table, near_ref, *refs):
    far_refs, out_ref = refs[:-1], refs[-1]
    rows = far_refs[0].shape[0]
    for h, far_ref in enumerate(far_refs):
        part = slice(h * rows, (h + 1) * rows)
        out_ref[part] = (near_ref[part].astype(F32) + far_ref[...].astype(F32)).astype(BF16)


def proj_body(count, first, last, n_feat, at, table, *refs):
    slots, refs = refs[:count], refs[count:]
    w_ref, acts_ref, x_ref, bias_ref = refs[:4]
    refs = refs[4:]
    if not first:
        carry_ref, seen_ref, refs = refs[0], refs[1], refs[2:]
    out_ref, sum_ref = refs[:2]
    if last:
        out_ref, line_ref, sum_ref = refs
    if first:
        sum_ref[...] = jnp.zeros_like(sum_ref)
    else:
        sum_ref[...] = seen_ref[...]
    for q, g_ref in enumerate(slots):
        n_tok, _, width = g_ref.shape
        source, held = table[at + 2 * q], table[at + 2 * q + 1] == 1

        @pl.when(held)
        def _():
            total = None if q == 0 and first else (carry_ref if q == 0 else out_ref)[...]
            for s in range(n_tok):
                w = w_ref[:, aligned((table[0] ^ s) * n_feat + source, width)]
                term = lax.dot_general(
                    g_ref[s], w, (((1,), (1,)), ((), ())), preferred_element_type=F32
                )
                total = term if total is None else total + term
            out_ref[...] = total

        @pl.when(held & (source // n_tok == table[2]))
        def _():
            cols = aligned(source % n_tok, width)
            term = x_ref[:, cols].astype(F32) - bias_ref[:, cols]
            term = term * g_ref[table[0] ^ table[1]].astype(F32)
            sum_ref[...] += jnp.sum(term, axis=1, keepdims=True)

    if last:
        attr = acts_ref[...].astype(F32) * out_ref[...]
        out_ref[...] = attr
        total = sum_ref[...] - jnp.sum(attr, axis=1, keepdims=True)
        line_ref[...] = jnp.broadcast_to(total, (total.shape[0], TILE)).T[:8]


def project(table, at, slots, w, acts, own_x, bias, carry, last, n_feat):
    rows, feats = acts.shape
    outs = [((rows, feats), F32), ((8, rows), F32) if last else ((rows, 1), F32)]
    return kernel_call(
        functools.partial(proj_body, len(slots), carry is None, last, n_feat, at),
        outs,
        [table, *slots, w, acts, own_x, bias, *(carry or [])],
        "project",
        LIGHT if last else cost(2 * len(slots) * slots[0].size * feats, 4 << 20),
        [pltpu.VMEM((rows, 1), F32)] if last else [],
    )


def line_program(resid, resid_grad, active, w_enc, b_enc, w_dec, b_dec):
    n_tok, n_feat = lax.axis_size("tok"), lax.axis_size("feat")
    i, j = lax.axis_index("tok"), lax.axis_index("feat")
    chips = n_feat // 2
    width = resid.shape[1]
    rows = resid.shape[0] // n_tok
    feats = w_enc.shape[1]
    share = n_tok * width

    def along(pairs):
        return [(2 * a + c, 2 * b + c) for a, b in pairs for c in range(2)]

    def send(array, pairs):
        return lax.ppermute(array, "feat", along(pairs))

    def cross(array):
        return lax.ppermute(array, "feat", [(a, a ^ 1) for a in range(n_feat)])

    def exchange(blocks, streams):
        blocks = list(blocks)
        for s in range(1, n_tok):
            blocks[s] = lax.ppermute(blocks[s], "tok", [(a, a ^ s) for a in range(n_tok)])
        return [jnp.stack([blocks[s] for s in stream]) for stream in streams]

    table = make_table(jnp.stack([i, j]), active, n_tok, n_feat, feats // BLOCK)
    bias = b_enc.reshape(1, feats)
    b_row = b_dec.reshape(1, share)

    ring = [(a, (a + 1) % chips) for a in range(chips)]
    cut_x = [lax.dynamic_slice_in_dim(resid, (i ^ s) * rows, rows, 0) for s in range(n_tok)]
    near_x = [exchange(cut_x, X_STREAMS)]
    cut_g = [lax.dynamic_slice_in_dim(resid_grad, (i ^ s) * rows, rows, 0) for s in range(n_tok)]
    shard_g, = exchange(cut_g, ((0, 1, 2, 3),))
    far_x = [[cross(a) for a in near_x[0]]]
    for k in range(1, chips):
        first, second = near_x[-1]
        if k == 1:
            second = after(second, table)
        if k == 2:
            second = after(second, shard_g)
            w_out, far_x[0][0] = load(w_dec, far_x[0][0], 44)
            first = after(first, far_x[0][0])
        if k == 3:
            far_x[0][1] = after(far_x[0][1], far_x[1][0])
            w_in, far_x[0][1] = load(w_enc.reshape(n_tok * n_feat, width, feats), far_x[0][1], 36)
            first = after(first, far_x[0][1])
            far_x.append([cross(first), cross(second)])
            slots = [near_x[0], far_x[0], near_x[1], far_x[1]]
            carry = encode(
                table, SLOTS["enc_a"], slots, w_in, bias, None, X_STREAMS, False, n_feat
            )
            second = after(second, carry)
        near_x[-1] = [first, second]
        if k == 2:
            far_x.append([cross(a) for a in near_x[-1]])
        near_x.append([send(first, ring), send(second, ring)])
    far_x.append([cross(near_x[3][0]), cross(after(near_x[3][1], carry))])

    up_pairs = [(a, a + 1) for a in range(chips - 1)]
    down_pairs = [(a + 1, a) for a in range(chips - 1)]
    shard_g = after(shard_g, near_x[-1], carry)
    up_1, down_1 = send(shard_g, up_pairs), send(shard_g, down_pairs)

    slots = [near_x[2], far_x[2], near_x[3], far_x[3]]
    acts, own_x = encode(table, SLOTS["enc_b"], slots, w_in, bias, carry, X_STREAMS, True, n_feat)

    far_3_a, far_3_b, near_3, *outs = kernel_call(
        functools.partial(dec_body, SLOTS["dec"]),
        [((rows // 2, share), BF16)] * 2 + [((rows, share), BF16)] * (2 * chips - 1),
        [table, acts, w_out],
        "decode",
    )
    up_1, down_1 = after((up_1, down_1), far_3_a)
    far_in = [cross(far_3_a), cross(far_3_b)]
    start, = kernel_call(sum_body, [((rows, share), BF16)], [table, near_3, *far_in], "sum")
    outs = after(outs, start)
    parts = {k: (outs[2 * n + 1], cross(outs[2 * n])) for n, k in enumerate((2, 1, 0))}

    def pair_sum(k):
        return parts[k][0].astype(F32) + parts[k][1].astype(F32)

    come = send(start, [(0, 1), (3, 2)])
    up_2, down_2 = send(up_1, up_pairs[1:]), send(down_1, down_pairs[:-1])
    going = (pair_sum(2) + come.astype(F32)).astype(BF16)
    two_g = up_2 + down_2
    three_g = send(two_g, [(2, 3), (1, 0)])

    up = send(going, up_pairs[:2])
    down = send(going, down_pairs[1:])

    slots = [shard_g, cross(shard_g), up_1, cross(up_1), down_1, cross(down_1)]
    carry = project(
        table, SLOTS["proj_a"], slots, w_out, after(acts, going), own_x, b_row, None, False, n_feat
    )
    base = own_x.astype(F32) - b_row - pair_sum(0)

    going_up, going_down = kernel_call(
        functools.partial(third_body, chips),
        [((rows, share), BF16)] * 2,
        [table, *parts[1], near_3, *far_in, up, down],
        "third",
    )
    going_up, going_down = after((going_up, going_down), carry, base)
    up = send(going_up, up_pairs)
    down = send(going_down, down_pairs)

    slots = [two_g, cross(two_g), three_g, cross(three_g)]
    feature_attr, attr = project(
        table, SLOTS["proj_b"], slots, w_out, after(acts, going_up, going_down), own_x, b_row, carry, True, n_feat
    )
    attr = attr[:1]
    attr = attr + cross(attr)
    others = [send(attr, [(a, a ^ k) for a in range(chips)]) for k in range(1, chips)]
    for other in others:
        attr = attr + other

    error = base - (up.astype(F32) + down.astype(F32))
    return feature_attr, error, attr.reshape(rows)


def gathered_program(resid, resid_grad, active, w_enc, b_enc, w_dec, b_dec):
    n_tok = lax.axis_size("tok")
    n_feat = lax.axis_size("feat")
    width = resid.shape[1]

    def rows_of(array):
        part = lax.all_to_all(array, "tok", split_axis=0, concat_axis=1, tiled=True)
        part = part.reshape(part.shape[0], n_tok, 1, width)
        part = lax.all_gather(part, "feat", axis=2, tiled=True)
        return part.reshape(part.shape[0], n_tok * n_feat * width)

    rows_x, rows_g = rows_of(resid), rows_of(resid_grad)
    tok_rows = rows_x.shape[0]
    feat_dev = w_enc.shape[1]
    blocks = feat_dev // BLOCK
    tiles_dev = active.shape[0]
    block_ids = lax.axis_index("feat") * blocks + jnp.arange(blocks, dtype=jnp.int32)
    hits = jnp.any(active[:, :, None] == block_ids[None, None, :], axis=1).astype(F32)
    pre = jnp.dot(rows_x, w_enc, preferred_element_type=F32) + b_enc
    shaped = jnp.maximum(pre, 0.0).reshape(tiles_dev, TILE, blocks, BLOCK) * hits[:, None, :, None]
    acts = shaped.reshape(tok_rows, feat_dev).astype(BF16)
    partial_recon = jnp.dot(acts, w_dec, preferred_element_type=F32)
    recon_share = lax.psum_scatter(
        partial_recon.astype(BF16), "feat", scatter_dimension=1, tiled=True
    ).astype(F32)
    share = recon_share.shape[1]
    start = lax.axis_index("feat") * share
    own_x = lax.dynamic_slice_in_dim(rows_x, start, share, 1)
    own_g = lax.dynamic_slice_in_dim(rows_g, start, share, 1)
    recon = recon_share + b_dec
    error = own_x.astype(F32) - recon
    local_sums = jnp.sum(error * own_g.astype(F32), axis=1)
    error_attr = lax.psum(local_sums, "feat")
    proj = lax.dot_general(rows_g, w_dec, (((1,), (1,)), ((), ())), preferred_element_type=F32)
    return acts.astype(F32) * proj, error, error_attr


def per_device(resid, *rest):
    fits = resid.shape[1] % 128 == 0 and lax.axis_size("tok") == 4 and lax.axis_size("feat") == 8
    return (line_program if fits else gathered_program)(resid, *rest)


def solution(mesh):
    placed = (
        P(None, ("tok", "feat")),
        P(None, ("tok", "feat")),
        P("tok", None),
        P(None, "feat"),
        P("feat"),
        P("feat", None),
        P("feat"),
    )
    return jax.shard_map(
        per_device,
        mesh=mesh,
        in_specs=placed,
        out_specs=(P("tok", "feat"), P("tok", "feat"), P("tok")),
        check_vma=False,
    )
```

```python
import functools

import jax
import jax.numpy as jnp
from jax import lax
from jax.experimental import pallas as pl
from jax.experimental.pallas import tpu as pltpu
from jax.sharding import PartitionSpec as P

BLOCK = 128
TILE = 128
X_STREAMS = ((0, 1), (2, 3))
PIECES = 8
PARAMS = pltpu.CompilerParams(vmem_limit_bytes=20 << 20)
F32 = jnp.float32
BF16 = jnp.bfloat16
LIGHT = pl.CostEstimate(flops=1, bytes_accessed=1, transcendentals=0)
VMEM = pl.BlockSpec(memory_space=pltpu.VMEM)
SMEM = pl.BlockSpec(memory_space=pltpu.SMEM)


def cost(flops, moved):
    return pl.CostEstimate(flops=flops, bytes_accessed=moved, transcendentals=0)


def after(value, *others):
    return lax.optimization_barrier((value, others))[0]


def kernel_call(body, outs, args, name, hint=LIGHT, scratch=()):
    return pl.pallas_call(
        body,
        in_specs=[SMEM] + [VMEM] * (len(args) - 1),
        out_specs=[VMEM] * len(outs),
        out_shape=[jax.ShapeDtypeStruct(shape, kind) for shape, kind in outs],
        scratch_shapes=list(scratch),
        compiler_params=PARAMS,
        cost_estimate=hint,
        name=name,
    )(*args)


def load_body(w_ref, through_ref, out_ref, same_ref, sems):
    step = w_ref.shape[0] // PIECES
    copies = []
    for n in range(PIECES):
        part = pl.ds(n * step, step)
        copies.append(pltpu.make_async_copy(w_ref.at[part], out_ref.at[part], sems.at[n]))
    for copy in copies:
        copy.start()
    for copy in copies:
        copy.wait()


def load(w, through, room):
    anywhere = pl.BlockSpec(memory_space=pl.ANY)
    return pl.pallas_call(
        load_body,
        in_specs=[anywhere, anywhere],
        out_specs=[VMEM, anywhere],
        out_shape=[
            pltpu.VMEM(w.shape, w.dtype),
            jax.ShapeDtypeStruct(through.shape, through.dtype),
        ],
        scratch_shapes=[pltpu.SemaphoreType.DMA((PIECES,))],
        input_output_aliases={1: 1},
        compiler_params=pltpu.CompilerParams(vmem_limit_bytes=room << 20),
        cost_estimate=cost(0, 2 * w.size),
        name="load",
    )(w, through)


SLOTS = {"enc_a": 4, "enc_b": 8, "dec": 12, "proj_a": 20, "proj_b": 32, "hits": 40}


def table_body(n_tok, n_feat, blocks, ids_ref, active_ref, out_ref):
    i, j = ids_ref[0], ids_ref[1]
    chips, ratio = n_feat // 2, n_feat // n_tok
    chip, core = j // 2, j % 2

    def both_cores(place):
        return [2 * place + core, 2 * place + 1 - core]

    def held_slots(*sources):
        values, seen = [], 0
        for place, valid in sources:
            seen = jnp.where(valid, place, seen)
            for source in both_cores(seen):
                values += [source, jnp.where(valid, 1, 0)]
        return values

    numbers = [i, j // ratio, j % ratio, chip]
    for k in range(chips):
        numbers += both_cores((chip + chips - k) % chips)
    for k in (3, 2, 1, 0):
        numbers += both_cores(chip ^ k)[::-1]
    numbers += held_slots((chip, chip >= 0), (chip - 1, chip >= 1), (chip + 1, chip <= chips - 2))
    numbers += held_slots((chip ^ 2, chip >= 0), (chip ^ 3, (chip == 0) | (chip == chips - 1)))
    for n, number in enumerate(numbers):
        out_ref[n] = number
    tiles, listed = active_ref.shape
    for t in range(tiles):
        for b in range(blocks):
            found = jnp.int32(0)
            for n in range(listed):
                found = jnp.where(active_ref[t, n] == j * blocks + b, 1, found)
            out_ref[SLOTS["hits"] + t * blocks + b] = found


def make_table(ids, active, n_tok, n_feat, blocks):
    size = SLOTS["hits"] + active.shape[0] * blocks
    return pl.pallas_call(
        functools.partial(table_body, n_tok, n_feat, blocks),
        in_specs=[SMEM, SMEM],
        out_specs=SMEM,
        out_shape=jax.ShapeDtypeStruct((size,), jnp.int32),
        compiler_params=PARAMS,
        cost_estimate=LIGHT,
        name="table",
    )(ids, active)


def pick_body(table, array_ref, *refs):
    outs, sems = refs[:-1], refs[-1]
    rows = outs[0].shape[0]
    copies = []
    for s, out_ref in enumerate(outs):
        part = array_ref.at[aligned(table[0] ^ s, rows)]
        copies.append(pltpu.make_async_copy(part, out_ref, sems.at[s]))
    for copy in copies:
        copy.start()
    for copy in copies:
        copy.wait()


def pick(table, array, n_tok):
    shape = (array.shape[0] // n_tok, array.shape[1])
    return pl.pallas_call(
        pick_body,
        in_specs=[SMEM, pl.BlockSpec(memory_space=pl.ANY)],
        out_specs=[VMEM] * n_tok,
        out_shape=[jax.ShapeDtypeStruct(shape, array.dtype)] * n_tok,
        scratch_shapes=[pltpu.SemaphoreType.DMA((n_tok,))],
        compiler_params=PARAMS,
        cost_estimate=LIGHT,
        name="pick",
    )(table, array)


def third_body(chips, table, *refs):
    near_1, far_1, near_3, far_3, up_ref, down_ref = refs[:3] + (refs[3:-4],) + refs[-4:-2]
    chip = table[3]
    for target, come_ref, turn in ((refs[-2], up_ref, 1), (refs[-1], down_ref, chips - 2)):

        @pl.when(chip == turn)
        def _():
            rows = far_3[0].shape[0]
            for h, far_ref in enumerate(far_3):
                part = slice(h * rows, (h + 1) * rows)
                total = near_3[part].astype(F32) + far_ref[...].astype(F32)
                target[part] = (total + come_ref[part].astype(F32)).astype(BF16)

        @pl.when(chip != turn)
        def _():
            total = near_1[...].astype(F32) + far_1[...].astype(F32)
            target[...] = (total + come_ref[...].astype(F32)).astype(BF16)


def pieces(refs, streams):
    return [refs[a].at[b] for a, stream in enumerate(streams) for b in range(len(stream))]


def aligned(index, width):
    return pl.ds(pl.multiple_of(index * width, width), width)


def enc_body(streams, count, first, last, n_feat, at, table, *refs):
    size = len(streams)
    slots = [pieces(refs[q * size:(q + 1) * size], streams) for q in range(count)]
    w_ref, bias_ref = refs[count * size:count * size + 2]
    refs = refs[count * size + 2:]
    carry_ref = None
    if not first:
        carry_ref, seen_ref, refs = refs[0], refs[1], refs[2:]
    out_ref, own_ref = refs[:2]
    total_ref = refs[2] if last else out_ref
    n_tok, width = len(slots[0]), slots[0][0].shape[1]
    if not first:
        own_ref[...] = seen_ref[...]
    for q, blocks in enumerate(slots):
        source = table[at + q]
        total = carry_ref if q == 0 else total_ref
        total = None if total is None else total[...]
        for s, x in enumerate(blocks):
            w = w_ref[(table[0] ^ s) * n_feat + source]
            term = jnp.dot(x[...], w, preferred_element_type=F32)
            total = term if total is None else total + term
        total_ref[...] = total
        for s, x in enumerate(blocks):

            @pl.when(((table[0] ^ s) == table[1]) & (source // n_tok == table[2]))
            def _():
                own_ref[:, aligned(source % n_tok, width)] = x[...]

    if last:
        blocks = out_ref.shape[1] // BLOCK
        for t in range(out_ref.shape[0] // TILE):
            for b in range(blocks):
                tile, block = slice(t * TILE, (t + 1) * TILE), slice(b * BLOCK, (b + 1) * BLOCK)
                pre = total_ref[tile, block] + bias_ref[:, block]
                live = table[SLOTS["hits"] + t * blocks + b].astype(F32)
                out_ref[tile, block] = (jnp.maximum(pre, 0.0) * live).astype(BF16)


def encode(table, at, slots, w, bias, carry, streams, last, n_feat):
    width, feats = w.shape[1:]
    rows = slots[0][0].shape[1]
    n_tok = w.shape[0] // n_feat
    args = [table] + [a for slot in slots for a in slot] + [w, bias]
    if carry is not None:
        args += carry
    return kernel_call(
        functools.partial(enc_body, streams, len(slots), carry is None, last, n_feat, at),
        [((rows, feats), BF16 if last else F32), ((rows, n_tok * width), BF16)],
        args,
        "encode",
        LIGHT if last else cost(2 * len(slots) * rows * n_tok * width * feats, 4 << 20),
        [pltpu.VMEM((rows, feats), F32)] if last else [],
    )


def dec_body(at, table, acts_ref, w_ref, *out_refs):
    share = out_refs[0].shape[1]
    for q, targets in enumerate([out_refs[:2]] + [(out_ref,) for out_ref in out_refs[2:]]):
        w = w_ref[:, aligned(table[at + q], share)]
        part = jnp.dot(acts_ref[...], w, preferred_element_type=F32).astype(BF16)
        rows = part.shape[0] // len(targets)
        for h, out_ref in enumerate(targets):
            out_ref[...] = part[h * rows:(h + 1) * rows]


def sum_body(table, near_ref, *refs):
    far_refs, out_ref = refs[:-1], refs[-1]
    rows = far_refs[0].shape[0]
    for h, far_ref in enumerate(far_refs):
        part = slice(h * rows, (h + 1) * rows)
        out_ref[part] = (near_ref[part].astype(F32) + far_ref[...].astype(F32)).astype(BF16)


def proj_body(count, first, last, n_feat, at, table, *refs):
    slots, refs = refs[:count], refs[count:]
    w_ref, acts_ref, x_ref, bias_ref = refs[:4]
    refs = refs[4:]
    if not first:
        carry_ref, seen_ref, refs = refs[0], refs[1], refs[2:]
    out_ref, sum_ref = refs[:2]
    if last:
        out_ref, line_ref, sum_ref = refs
    if first:
        sum_ref[...] = jnp.zeros_like(sum_ref)
    else:
        sum_ref[...] = seen_ref[...]
    for q, g_ref in enumerate(slots):
        n_tok, _, width = g_ref.shape
        source, held = table[at + 2 * q], table[at + 2 * q + 1] == 1

        @pl.when(held)
        def _():
            total = None if q == 0 and first else (carry_ref if q == 0 else out_ref)[...]
            for s in range(n_tok):
                w = w_ref[:, aligned((table[0] ^ s) * n_feat + source, width)]
                term = lax.dot_general(
                    g_ref[s], w, (((1,), (1,)), ((), ())), preferred_element_type=F32
                )
                total = term if total is None else total + term
            out_ref[...] = total

        @pl.when(held & (source // n_tok == table[2]))
        def _():
            cols = aligned(source % n_tok, width)
            term = x_ref[:, cols].astype(F32) - bias_ref[:, cols]
            term = term * g_ref[table[0] ^ table[1]].astype(F32)
            sum_ref[...] += jnp.sum(term, axis=1, keepdims=True)

    if last:
        attr = acts_ref[...].astype(F32) * out_ref[...]
        out_ref[...] = attr
        total = sum_ref[...] - jnp.sum(attr, axis=1, keepdims=True)
        line_ref[...] = jnp.broadcast_to(total, (total.shape[0], TILE)).T[:8]


def project(table, at, slots, w, acts, own_x, bias, carry, last, n_feat):
    rows, feats = acts.shape
    outs = [((rows, feats), F32), ((8, rows), F32) if last else ((rows, 1), F32)]
    return kernel_call(
        functools.partial(proj_body, len(slots), carry is None, last, n_feat, at),
        outs,
        [table, *slots, w, acts, own_x, bias, *(carry or [])],
        "project",
        LIGHT if last else cost(2 * len(slots) * slots[0].size * feats, 4 << 20),
        [pltpu.VMEM((rows, 1), F32)] if last else [],
    )


def line_program(resid, resid_grad, active, w_enc, b_enc, w_dec, b_dec):
    n_tok, n_feat = lax.axis_size("tok"), lax.axis_size("feat")
    i, j = lax.axis_index("tok"), lax.axis_index("feat")
    chips = n_feat // 2
    width = resid.shape[1]
    rows = resid.shape[0] // n_tok
    feats = w_enc.shape[1]
    share = n_tok * width

    def along(pairs):
        return [(2 * a + c, 2 * b + c) for a, b in pairs for c in range(2)]

    def send(array, pairs):
        return lax.ppermute(array, "feat", along(pairs))

    def cross(array):
        return lax.ppermute(array, "feat", [(a, a ^ 1) for a in range(n_feat)])

    def exchange(blocks, streams):
        blocks = list(blocks)
        for s in range(1, n_tok):
            blocks[s] = lax.ppermute(blocks[s], "tok", [(a, a ^ s) for a in range(n_tok)])
        return [jnp.stack([blocks[s] for s in stream]) for stream in streams]

    table = make_table(jnp.stack([i, j]), active, n_tok, n_feat, feats // BLOCK)
    bias = b_enc.reshape(1, feats)
    b_row = b_dec.reshape(1, share)

    ring = [(a, (a + 1) % chips) for a in range(chips)]
    cut_x = [lax.dynamic_slice_in_dim(resid, (i ^ s) * rows, rows, 0) for s in range(n_tok)]
    near_x = [exchange(cut_x, X_STREAMS)]
    cut_g = [lax.dynamic_slice_in_dim(resid_grad, (i ^ s) * rows, rows, 0) for s in range(n_tok)]
    shard_g, = exchange(cut_g, ((0, 1, 2, 3),))
    far_x = [[cross(a) for a in near_x[0]]]
    for k in range(1, chips):
        first, second = near_x[-1]
        if k == 1:
            second = after(second, table)
        if k == 2:
            second = after(second, shard_g)
            w_out, far_x[0][0] = load(w_dec, far_x[0][0], 44)
            first = after(first, far_x[0][0])
        if k == 3:
            far_x[0][1] = after(far_x[0][1], far_x[1][0])
            w_in, far_x[0][1] = load(w_enc.reshape(n_tok * n_feat, width, feats), far_x[0][1], 36)
            first = after(first, far_x[0][1])
        near_x[-1] = [first, second]
        if k > 1:
            far_x.append([cross(a) for a in near_x[-1]])
        near_x.append([send(first, ring), send(second, ring)])
    slots = [near_x[0], far_x[0], near_x[1], far_x[1]]
    carry = encode(
        after(table, near_x[3][0]), SLOTS["enc_a"], slots, w_in, bias, None, X_STREAMS, False, n_feat
    )
    far_x.append([cross(near_x[3][0]), cross(after(near_x[3][1], carry))])

    up_pairs = [(a, a + 1) for a in range(chips - 1)]
    down_pairs = [(a + 1, a) for a in range(chips - 1)]
    shard_g = after(shard_g, near_x[-1], carry)
    up_1, down_1 = send(shard_g, up_pairs), send(shard_g, down_pairs)

    slots = [near_x[2], far_x[2], near_x[3], far_x[3]]
    acts, own_x = encode(table, SLOTS["enc_b"], slots, w_in, bias, carry, X_STREAMS, True, n_feat)

    far_3_a, far_3_b, near_3, *outs = kernel_call(
        functools.partial(dec_body, SLOTS["dec"]),
        [((rows // 2, share), BF16)] * 2 + [((rows, share), BF16)] * (2 * chips - 1),
        [table, acts, w_out],
        "decode",
    )
    up_1, down_1 = after((up_1, down_1), far_3_a)
    far_in = [cross(far_3_a), cross(far_3_b)]
    start, = kernel_call(sum_body, [((rows, share), BF16)], [table, near_3, *far_in], "sum")
    outs = after(outs, start)
    parts = {k: (outs[2 * n + 1], cross(outs[2 * n])) for n, k in enumerate((2, 1, 0))}

    def pair_sum(k):
        return parts[k][0].astype(F32) + parts[k][1].astype(F32)

    come = send(start, [(0, 1), (3, 2)])
    up_2, down_2 = send(up_1, up_pairs[1:]), send(down_1, down_pairs[:-1])
    going = (pair_sum(2) + come.astype(F32)).astype(BF16)
    two_g = up_2 + down_2
    three_g = send(two_g, [(2, 3), (1, 0)])

    up = send(going, up_pairs[:2])
    down = send(going, down_pairs[1:])

    slots = [shard_g, cross(shard_g), up_1, cross(up_1), down_1, cross(down_1)]
    carry = project(
        table, SLOTS["proj_a"], slots, w_out, after(acts, going), own_x, b_row, None, False, n_feat
    )
    base = own_x.astype(F32) - b_row - pair_sum(0)

    going_up, going_down = kernel_call(
        functools.partial(third_body, chips),
        [((rows, share), BF16)] * 2,
        [table, *parts[1], near_3, *far_in, up, down],
        "third",
    )
    going_up, going_down = after((going_up, going_down), carry, base)
    up = send(going_up, up_pairs)
    down = send(going_down, down_pairs)

    slots = [two_g, cross(two_g), three_g, cross(three_g)]
    feature_attr, attr = project(
        table, SLOTS["proj_b"], slots, w_out, after(acts, going_up, going_down), own_x, b_row, carry, True, n_feat
    )
    attr = attr[:1]
    attr = attr + cross(attr)
    others = [send(attr, [(a, a ^ k) for a in range(chips)]) for k in range(1, chips)]
    for other in others:
        attr = attr + other

    error = base - (up.astype(F32) + down.astype(F32))
    return feature_attr, error, attr.reshape(rows)


def gathered_program(resid, resid_grad, active, w_enc, b_enc, w_dec, b_dec):
    n_tok = lax.axis_size("tok")
    n_feat = lax.axis_size("feat")
    width = resid.shape[1]

    def rows_of(array):
        part = lax.all_to_all(array, "tok", split_axis=0, concat_axis=1, tiled=True)
        part = part.reshape(part.shape[0], n_tok, 1, width)
        part = lax.all_gather(part, "feat", axis=2, tiled=True)
        return part.reshape(part.shape[0], n_tok * n_feat * width)

    rows_x, rows_g = rows_of(resid), rows_of(resid_grad)
    tok_rows = rows_x.shape[0]
    feat_dev = w_enc.shape[1]
    blocks = feat_dev // BLOCK
    tiles_dev = active.shape[0]
    block_ids = lax.axis_index("feat") * blocks + jnp.arange(blocks, dtype=jnp.int32)
    hits = jnp.any(active[:, :, None] == block_ids[None, None, :], axis=1).astype(F32)
    pre = jnp.dot(rows_x, w_enc, preferred_element_type=F32) + b_enc
    shaped = jnp.maximum(pre, 0.0).reshape(tiles_dev, TILE, blocks, BLOCK) * hits[:, None, :, None]
    acts = shaped.reshape(tok_rows, feat_dev).astype(BF16)
    partial_recon = jnp.dot(acts, w_dec, preferred_element_type=F32)
    recon_share = lax.psum_scatter(
        partial_recon.astype(BF16), "feat", scatter_dimension=1, tiled=True
    ).astype(F32)
    share = recon_share.shape[1]
    start = lax.axis_index("feat") * share
    own_x = lax.dynamic_slice_in_dim(rows_x, start, share, 1)
    own_g = lax.dynamic_slice_in_dim(rows_g, start, share, 1)
    recon = recon_share + b_dec
    error = own_x.astype(F32) - recon
    local_sums = jnp.sum(error * own_g.astype(F32), axis=1)
    error_attr = lax.psum(local_sums, "feat")
    proj = lax.dot_general(rows_g, w_dec, (((1,), (1,)), ((), ())), preferred_element_type=F32)
    return acts.astype(F32) * proj, error, error_attr


def per_device(resid, *rest):
    fits = resid.shape[1] % 128 == 0 and lax.axis_size("tok") == 4 and lax.axis_size("feat") == 8
    return (line_program if fits else gathered_program)(resid, *rest)


def solution(mesh):
    placed = (
        P(None, ("tok", "feat")),
        P(None, ("tok", "feat")),
        P("tok", None),
        P(None, "feat"),
        P("feat"),
        P("feat", None),
        P("feat"),
    )
    return jax.shard_map(
        per_device,
        mesh=mesh,
        in_specs=placed,
        out_specs=(P("tok", "feat"), P("tok", "feat"), P("tok")),
        check_vma=False,
    )
```

```python
import functools

import jax
import jax.numpy as jnp
from jax import lax
from jax.experimental import pallas as pl
from jax.experimental.pallas import tpu as pltpu
from jax.sharding import PartitionSpec as P

BLOCK = 128
TILE = 128
X_STREAMS = ((0, 1), (2, 3))
PIECES = 8
PARAMS = pltpu.CompilerParams(vmem_limit_bytes=20 << 20)
F32 = jnp.float32
BF16 = jnp.bfloat16
LIGHT = pl.CostEstimate(flops=1, bytes_accessed=1, transcendentals=0)
VMEM = pl.BlockSpec(memory_space=pltpu.VMEM)
SMEM = pl.BlockSpec(memory_space=pltpu.SMEM)


def cost(flops, moved):
    return pl.CostEstimate(flops=flops, bytes_accessed=moved, transcendentals=0)


def after(value, *others):
    return lax.optimization_barrier((value, others))[0]


def kernel_call(body, outs, args, name, hint=LIGHT, scratch=()):
    return pl.pallas_call(
        body,
        in_specs=[SMEM] + [VMEM] * (len(args) - 1),
        out_specs=[VMEM] * len(outs),
        out_shape=[jax.ShapeDtypeStruct(shape, kind) for shape, kind in outs],
        scratch_shapes=list(scratch),
        compiler_params=PARAMS,
        cost_estimate=hint,
        name=name,
    )(*args)


def load_body(w_ref, through_ref, out_ref, same_ref, sems):
    step = w_ref.shape[0] // PIECES
    copies = []
    for n in range(PIECES):
        part = pl.ds(n * step, step)
        copies.append(pltpu.make_async_copy(w_ref.at[part], out_ref.at[part], sems.at[n]))
    for copy in copies:
        copy.start()
    for copy in copies:
        copy.wait()


def load(w, through, room):
    anywhere = pl.BlockSpec(memory_space=pl.ANY)
    return pl.pallas_call(
        load_body,
        in_specs=[anywhere, anywhere],
        out_specs=[VMEM, anywhere],
        out_shape=[
            pltpu.VMEM(w.shape, w.dtype),
            jax.ShapeDtypeStruct(through.shape, through.dtype),
        ],
        scratch_shapes=[pltpu.SemaphoreType.DMA((PIECES,))],
        input_output_aliases={1: 1},
        compiler_params=pltpu.CompilerParams(vmem_limit_bytes=room << 20),
        cost_estimate=cost(0, 2 * w.size),
        name="load",
    )(w, through)


SLOTS = {"enc_a": 4, "enc_b": 8, "dec": 12, "proj_a": 20, "proj_b": 32, "hits": 40}


def table_body(n_tok, n_feat, blocks, ids_ref, active_ref, out_ref):
    i, j = ids_ref[0], ids_ref[1]
    chips, ratio = n_feat // 2, n_feat // n_tok
    chip, core = j // 2, j % 2

    def both_cores(place):
        return [2 * place + core, 2 * place + 1 - core]

    def held_slots(*sources):
        values, seen = [], 0
        for place, valid in sources:
            seen = jnp.where(valid, place, seen)
            for source in both_cores(seen):
                values += [source, jnp.where(valid, 1, 0)]
        return values

    numbers = [i, j // ratio, j % ratio, chip]
    for k in range(chips):
        numbers += both_cores((chip + chips - k) % chips)
    for k in (3, 2, 1, 0):
        numbers += both_cores(chip ^ k)[::-1]
    numbers += held_slots((chip, chip >= 0), (chip - 1, chip >= 1), (chip + 1, chip <= chips - 2))
    numbers += held_slots((chip ^ 2, chip >= 0), (chip ^ 3, (chip == 0) | (chip == chips - 1)))
    for n, number in enumerate(numbers):
        out_ref[n] = number
    tiles, listed = active_ref.shape
    for t in range(tiles):
        for b in range(blocks):
            found = jnp.int32(0)
            for n in range(listed):
                found = jnp.where(active_ref[t, n] == j * blocks + b, 1, found)
            out_ref[SLOTS["hits"] + t * blocks + b] = found


def make_table(ids, active, n_tok, n_feat, blocks):
    size = SLOTS["hits"] + active.shape[0] * blocks
    return pl.pallas_call(
        functools.partial(table_body, n_tok, n_feat, blocks),
        in_specs=[SMEM, SMEM],
        out_specs=SMEM,
        out_shape=jax.ShapeDtypeStruct((size,), jnp.int32),
        compiler_params=PARAMS,
        cost_estimate=LIGHT,
        name="table",
    )(ids, active)


def pick_body(table, array_ref, *refs):
    outs, sems = refs[:-1], refs[-1]
    rows = outs[0].shape[0]
    copies = []
    for s, out_ref in enumerate(outs):
        part = array_ref.at[aligned(table[0] ^ s, rows)]
        copies.append(pltpu.make_async_copy(part, out_ref, sems.at[s]))
    for copy in copies:
        copy.start()
    for copy in copies:
        copy.wait()


def pick(table, array, n_tok):
    shape = (array.shape[0] // n_tok, array.shape[1])
    return pl.pallas_call(
        pick_body,
        in_specs=[SMEM, pl.BlockSpec(memory_space=pl.ANY)],
        out_specs=[VMEM] * n_tok,
        out_shape=[jax.ShapeDtypeStruct(shape, array.dtype)] * n_tok,
        scratch_shapes=[pltpu.SemaphoreType.DMA((n_tok,))],
        compiler_params=PARAMS,
        cost_estimate=LIGHT,
        name="pick",
    )(table, array)


def third_body(chips, table, *refs):
    near_1, far_1, near_3, far_3, up_ref, down_ref = refs[:3] + (refs[3:-4],) + refs[-4:-2]
    chip = table[3]
    for target, come_ref, turn in ((refs[-2], up_ref, 1), (refs[-1], down_ref, chips - 2)):

        @pl.when(chip == turn)
        def _():
            rows = far_3[0].shape[0]
            for h, far_ref in enumerate(far_3):
                part = slice(h * rows, (h + 1) * rows)
                total = near_3[part].astype(F32) + far_ref[...].astype(F32)
                target[part] = (total + come_ref[part].astype(F32)).astype(BF16)

        @pl.when(chip != turn)
        def _():
            total = near_1[...].astype(F32) + far_1[...].astype(F32)
            target[...] = (total + come_ref[...].astype(F32)).astype(BF16)


def pieces(refs, streams):
    return [refs[a].at[b] for a, stream in enumerate(streams) for b in range(len(stream))]


def aligned(index, width):
    return pl.ds(pl.multiple_of(index * width, width), width)


def enc_body(streams, count, first, last, n_feat, at, table, *refs):
    size = len(streams)
    slots = [pieces(refs[q * size:(q + 1) * size], streams) for q in range(count)]
    w_ref, bias_ref = refs[count * size:count * size + 2]
    refs = refs[count * size + 2:]
    carry_ref = None
    if not first:
        carry_ref, seen_ref, refs = refs[0], refs[1], refs[2:]
    out_ref, own_ref = refs[:2]
    total_ref = refs[2] if last else out_ref
    n_tok, width = len(slots[0]), slots[0][0].shape[1]
    if not first:
        own_ref[...] = seen_ref[...]
    for q, blocks in enumerate(slots):
        source = table[at + q]
        total = carry_ref if q == 0 else total_ref
        total = None if total is None else total[...]
        for s, x in enumerate(blocks):
            w = w_ref[(table[0] ^ s) * n_feat + source]
            term = jnp.dot(x[...], w, preferred_element_type=F32)
            total = term if total is None else total + term
        total_ref[...] = total
        for s, x in enumerate(blocks):

            @pl.when(((table[0] ^ s) == table[1]) & (source // n_tok == table[2]))
            def _():
                own_ref[:, aligned(source % n_tok, width)] = x[...]

    if last:
        blocks = out_ref.shape[1] // BLOCK
        for t in range(out_ref.shape[0] // TILE):
            for b in range(blocks):
                tile, block = slice(t * TILE, (t + 1) * TILE), slice(b * BLOCK, (b + 1) * BLOCK)
                pre = total_ref[tile, block] + bias_ref[:, block]
                live = table[SLOTS["hits"] + t * blocks + b].astype(F32)
                out_ref[tile, block] = (jnp.maximum(pre, 0.0) * live).astype(BF16)


def encode(table, at, slots, w, bias, carry, streams, last, n_feat):
    width, feats = w.shape[1:]
    rows = slots[0][0].shape[1]
    n_tok = w.shape[0] // n_feat
    args = [table] + [a for slot in slots for a in slot] + [w, bias]
    if carry is not None:
        args += carry
    return kernel_call(
        functools.partial(enc_body, streams, len(slots), carry is None, last, n_feat, at),
        [((rows, feats), BF16 if last else F32), ((rows, n_tok * width), BF16)],
        args,
        "encode",
        LIGHT if last else cost(2 * len(slots) * rows * n_tok * width * feats, 4 << 20),
        [pltpu.VMEM((rows, feats), F32)] if last else [],
    )


def dec_body(at, table, acts_ref, w_ref, *out_refs):
    share = out_refs[0].shape[1]
    for q, targets in enumerate([out_refs[:2]] + [(out_ref,) for out_ref in out_refs[2:]]):
        w = w_ref[:, aligned(table[at + q], share)]
        part = jnp.dot(acts_ref[...], w, preferred_element_type=F32).astype(BF16)
        rows = part.shape[0] // len(targets)
        for h, out_ref in enumerate(targets):
            out_ref[...] = part[h * rows:(h + 1) * rows]


def sum_body(table, near_ref, *refs):
    far_refs, out_ref = refs[:-1], refs[-1]
    rows = far_refs[0].shape[0]
    for h, far_ref in enumerate(far_refs):
        part = slice(h * rows, (h + 1) * rows)
        out_ref[part] = (near_ref[part].astype(F32) + far_ref[...].astype(F32)).astype(BF16)


def proj_body(count, first, last, n_feat, at, table, *refs):
    slots, refs = refs[:count], refs[count:]
    w_ref, acts_ref, x_ref, bias_ref = refs[:4]
    refs = refs[4:]
    if not first:
        carry_ref, seen_ref, refs = refs[0], refs[1], refs[2:]
    out_ref, sum_ref = refs[:2]
    if last:
        out_ref, line_ref, sum_ref = refs
    if first:
        sum_ref[...] = jnp.zeros_like(sum_ref)
    else:
        sum_ref[...] = seen_ref[...]
    for q, g_ref in enumerate(slots):
        n_tok, _, width = g_ref.shape
        source, held = table[at + 2 * q], table[at + 2 * q + 1] == 1

        @pl.when(held)
        def _():
            total = None if q == 0 and first else (carry_ref if q == 0 else out_ref)[...]
            for s in range(n_tok):
                w = w_ref[:, aligned((table[0] ^ s) * n_feat + source, width)]
                term = lax.dot_general(
                    g_ref[s], w, (((1,), (1,)), ((), ())), preferred_element_type=F32
                )
                total = term if total is None else total + term
            out_ref[...] = total

        @pl.when(held & (source // n_tok == table[2]))
        def _():
            cols = aligned(source % n_tok, width)
            term = x_ref[:, cols].astype(F32) - bias_ref[:, cols]
            term = term * g_ref[table[0] ^ table[1]].astype(F32)
            sum_ref[...] += jnp.sum(term, axis=1, keepdims=True)

    if last:
        attr = acts_ref[...].astype(F32) * out_ref[...]
        out_ref[...] = attr
        total = sum_ref[...] - jnp.sum(attr, axis=1, keepdims=True)
        line_ref[...] = jnp.broadcast_to(total, (total.shape[0], TILE)).T[:8]


def project(table, at, slots, w, acts, own_x, bias, carry, last, n_feat):
    rows, feats = acts.shape
    outs = [((rows, feats), F32), ((8, rows), F32) if last else ((rows, 1), F32)]
    return kernel_call(
        functools.partial(proj_body, len(slots), carry is None, last, n_feat, at),
        outs,
        [table, *slots, w, acts, own_x, bias, *(carry or [])],
        "project",
        LIGHT if last else cost(2 * len(slots) * slots[0].size * feats, 4 << 20),
        [pltpu.VMEM((rows, 1), F32)] if last else [],
    )


def line_program(resid, resid_grad, active, w_enc, b_enc, w_dec, b_dec):
    n_tok, n_feat = lax.axis_size("tok"), lax.axis_size("feat")
    i, j = lax.axis_index("tok"), lax.axis_index("feat")
    chips = n_feat // 2
    width = resid.shape[1]
    rows = resid.shape[0] // n_tok
    feats = w_enc.shape[1]
    share = n_tok * width

    def along(pairs):
        return [(2 * a + c, 2 * b + c) for a, b in pairs for c in range(2)]

    def send(array, pairs):
        return lax.ppermute(array, "feat", along(pairs))

    def cross(array):
        return lax.ppermute(array, "feat", [(a, a ^ 1) for a in range(n_feat)])

    def exchange(blocks, streams):
        blocks = list(blocks)
        for s in range(1, n_tok):
            blocks[s] = lax.ppermute(blocks[s], "tok", [(a, a ^ s) for a in range(n_tok)])
        return [jnp.stack([blocks[s] for s in stream]) for stream in streams]

    table = make_table(jnp.stack([i, j]), active, n_tok, n_feat, feats // BLOCK)
    bias = b_enc.reshape(1, feats)
    b_row = b_dec.reshape(1, share)

    ring = [(a, (a + 1) % chips) for a in range(chips)]
    cut_x = [lax.dynamic_slice_in_dim(resid, (i ^ s) * rows, rows, 0) for s in range(n_tok)]
    near_x = [exchange(cut_x, X_STREAMS)]
    cut_g = [lax.dynamic_slice_in_dim(resid_grad, (i ^ s) * rows, rows, 0) for s in range(n_tok)]
    shard_g, = exchange(cut_g, ((0, 1, 2, 3),))
    far_x = [[cross(a) for a in near_x[0]]]
    for k in range(1, chips):
        first, second = near_x[-1]
        if k == 1:
            second = after(second, table)
        if k == 2:
            w_out, far_x[0][0] = load(w_dec, far_x[0][0], 44)
            second = after(second, shard_g, far_x[0][0])
        if k == 3:
            far_x[0][1] = after(far_x[0][1], far_x[1][0])
            w_in, far_x[0][1] = load(w_enc.reshape(n_tok * n_feat, width, feats), far_x[0][1], 36)
            first = after(first, far_x[0][1])
        near_x[-1] = [first, second]
        if k > 1:
            far_x.append([cross(a) for a in near_x[-1]])
        near_x.append([send(first, ring), send(second, ring)])
    slots = [near_x[0], far_x[0], near_x[1], far_x[1]]
    carry = encode(
        after(table, near_x[3][0]), SLOTS["enc_a"], slots, w_in, bias, None, X_STREAMS, False, n_feat
    )
    far_x.append([cross(near_x[3][0]), cross(after(near_x[3][1], carry))])

    up_pairs = [(a, a + 1) for a in range(chips - 1)]
    down_pairs = [(a + 1, a) for a in range(chips - 1)]
    shard_g = after(shard_g, near_x[-1], carry)
    up_1, down_1 = send(shard_g, up_pairs), send(shard_g, down_pairs)

    slots = [near_x[2], far_x[2], near_x[3], far_x[3]]
    acts, own_x = encode(table, SLOTS["enc_b"], slots, w_in, bias, carry, X_STREAMS, True, n_feat)

    far_3_a, far_3_b, near_3, *outs = kernel_call(
        functools.partial(dec_body, SLOTS["dec"]),
        [((rows // 2, share), BF16)] * 2 + [((rows, share), BF16)] * (2 * chips - 1),
        [table, acts, w_out],
        "decode",
    )
    up_1, down_1 = after((up_1, down_1), far_3_a)
    far_in = [cross(far_3_a), cross(far_3_b)]
    start, = kernel_call(sum_body, [((rows, share), BF16)], [table, near_3, *far_in], "sum")
    outs = after(outs, start)
    parts = {k: (outs[2 * n + 1], cross(outs[2 * n])) for n, k in enumerate((2, 1, 0))}

    def pair_sum(k):
        return parts[k][0].astype(F32) + parts[k][1].astype(F32)

    come = send(start, [(0, 1), (3, 2)])
    up_2, down_2 = send(up_1, up_pairs[1:]), send(down_1, down_pairs[:-1])
    going = (pair_sum(2) + come.astype(F32)).astype(BF16)
    two_g = up_2 + down_2
    three_g = send(two_g, [(2, 3), (1, 0)])

    up = send(going, up_pairs[:2])
    down = send(going, down_pairs[1:])

    slots = [shard_g, cross(shard_g), up_1, cross(up_1), down_1, cross(down_1)]
    carry = project(
        table, SLOTS["proj_a"], slots, w_out, after(acts, going), own_x, b_row, None, False, n_feat
    )
    base = own_x.astype(F32) - b_row - pair_sum(0)

    going_up, going_down = kernel_call(
        functools.partial(third_body, chips),
        [((rows, share), BF16)] * 2,
        [table, *parts[1], near_3, *far_in, up, down],
        "third",
    )
    going_up, going_down = after((going_up, going_down), carry, base)
    up = send(going_up, up_pairs)
    down = send(going_down, down_pairs)

    slots = [two_g, cross(two_g), three_g, cross(three_g)]
    feature_attr, attr = project(
        table, SLOTS["proj_b"], slots, w_out, after(acts, going_up, going_down), own_x, b_row, carry, True, n_feat
    )
    attr = attr[:1]
    attr = attr + cross(attr)
    others = [send(attr, [(a, a ^ k) for a in range(chips)]) for k in range(1, chips)]
    for other in others:
        attr = attr + other

    error = base - (up.astype(F32) + down.astype(F32))
    return feature_attr, error, attr.reshape(rows)


def gathered_program(resid, resid_grad, active, w_enc, b_enc, w_dec, b_dec):
    n_tok = lax.axis_size("tok")
    n_feat = lax.axis_size("feat")
    width = resid.shape[1]

    def rows_of(array):
        part = lax.all_to_all(array, "tok", split_axis=0, concat_axis=1, tiled=True)
        part = part.reshape(part.shape[0], n_tok, 1, width)
        part = lax.all_gather(part, "feat", axis=2, tiled=True)
        return part.reshape(part.shape[0], n_tok * n_feat * width)

    rows_x, rows_g = rows_of(resid), rows_of(resid_grad)
    tok_rows = rows_x.shape[0]
    feat_dev = w_enc.shape[1]
    blocks = feat_dev // BLOCK
    tiles_dev = active.shape[0]
    block_ids = lax.axis_index("feat") * blocks + jnp.arange(blocks, dtype=jnp.int32)
    hits = jnp.any(active[:, :, None] == block_ids[None, None, :], axis=1).astype(F32)
    pre = jnp.dot(rows_x, w_enc, preferred_element_type=F32) + b_enc
    shaped = jnp.maximum(pre, 0.0).reshape(tiles_dev, TILE, blocks, BLOCK) * hits[:, None, :, None]
    acts = shaped.reshape(tok_rows, feat_dev).astype(BF16)
    partial_recon = jnp.dot(acts, w_dec, preferred_element_type=F32)
    recon_share = lax.psum_scatter(
        partial_recon.astype(BF16), "feat", scatter_dimension=1, tiled=True
    ).astype(F32)
    share = recon_share.shape[1]
    start = lax.axis_index("feat") * share
    own_x = lax.dynamic_slice_in_dim(rows_x, start, share, 1)
    own_g = lax.dynamic_slice_in_dim(rows_g, start, share, 1)
    recon = recon_share + b_dec
    error = own_x.astype(F32) - recon
    local_sums = jnp.sum(error * own_g.astype(F32), axis=1)
    error_attr = lax.psum(local_sums, "feat")
    proj = lax.dot_general(rows_g, w_dec, (((1,), (1,)), ((), ())), preferred_element_type=F32)
    return acts.astype(F32) * proj, error, error_attr


def per_device(resid, *rest):
    fits = resid.shape[1] % 128 == 0 and lax.axis_size("tok") == 4 and lax.axis_size("feat") == 8
    return (line_program if fits else gathered_program)(resid, *rest)


def solution(mesh):
    placed = (
        P(None, ("tok", "feat")),
        P(None, ("tok", "feat")),
        P("tok", None),
        P(None, "feat"),
        P("feat"),
        P("feat", None),
        P("feat"),
    )
    return jax.shard_map(
        per_device,
        mesh=mesh,
        in_specs=placed,
        out_specs=(P("tok", "feat"), P("tok", "feat"), P("tok")),
        check_vma=False,
    )
```

```python
import functools

import jax
import jax.numpy as jnp
from jax import lax
from jax.experimental import pallas as pl
from jax.experimental.pallas import tpu as pltpu
from jax.sharding import PartitionSpec as P

BLOCK = 128
TILE = 128
X_STREAMS = ((0, 1), (2, 3))
PIECES = 8
PARAMS = pltpu.CompilerParams(vmem_limit_bytes=20 << 20)
F32 = jnp.float32
BF16 = jnp.bfloat16
LIGHT = pl.CostEstimate(flops=1, bytes_accessed=1, transcendentals=0)
VMEM = pl.BlockSpec(memory_space=pltpu.VMEM)
SMEM = pl.BlockSpec(memory_space=pltpu.SMEM)


def cost(flops, moved):
    return pl.CostEstimate(flops=flops, bytes_accessed=moved, transcendentals=0)


def after(value, *others):
    return lax.optimization_barrier((value, others))[0]


def kernel_call(body, outs, args, name, hint=LIGHT, scratch=()):
    return pl.pallas_call(
        body,
        in_specs=[SMEM] + [VMEM] * (len(args) - 1),
        out_specs=[VMEM] * len(outs),
        out_shape=[jax.ShapeDtypeStruct(shape, kind) for shape, kind in outs],
        scratch_shapes=list(scratch),
        compiler_params=PARAMS,
        cost_estimate=hint,
        name=name,
    )(*args)


def load_body(w_ref, through_ref, out_ref, same_ref, sems):
    step = w_ref.shape[0] // PIECES
    copies = []
    for n in range(PIECES):
        part = pl.ds(n * step, step)
        copies.append(pltpu.make_async_copy(w_ref.at[part], out_ref.at[part], sems.at[n]))
    for copy in copies:
        copy.start()
    for copy in copies:
        copy.wait()


def load(w, through, room):
    anywhere = pl.BlockSpec(memory_space=pl.ANY)
    return pl.pallas_call(
        load_body,
        in_specs=[anywhere, anywhere],
        out_specs=[VMEM, anywhere],
        out_shape=[
            pltpu.VMEM(w.shape, w.dtype),
            jax.ShapeDtypeStruct(through.shape, through.dtype),
        ],
        scratch_shapes=[pltpu.SemaphoreType.DMA((PIECES,))],
        input_output_aliases={1: 1},
        compiler_params=pltpu.CompilerParams(vmem_limit_bytes=room << 20),
        cost_estimate=cost(0, 2 * w.size),
        name="load",
    )(w, through)


SLOTS = {"enc_a": 4, "enc_b": 8, "dec": 12, "proj_a": 20, "proj_b": 32, "hits": 40}


def table_body(n_tok, n_feat, blocks, ids_ref, active_ref, out_ref):
    i, j = ids_ref[0], ids_ref[1]
    chips, ratio = n_feat // 2, n_feat // n_tok
    chip, core = j // 2, j % 2

    def both_cores(place):
        return [2 * place + core, 2 * place + 1 - core]

    def held_slots(*sources):
        values, seen = [], 0
        for place, valid in sources:
            seen = jnp.where(valid, place, seen)
            for source in both_cores(seen):
                values += [source, jnp.where(valid, 1, 0)]
        return values

    numbers = [i, j // ratio, j % ratio, chip]
    for k in range(chips):
        numbers += both_cores((chip + chips - k) % chips)
    for k in (3, 2, 1, 0):
        numbers += both_cores(chip ^ k)[::-1]
    numbers += held_slots((chip, chip >= 0), (chip - 1, chip >= 1), (chip + 1, chip <= chips - 2))
    numbers += held_slots((chip ^ 2, chip >= 0), (chip ^ 3, (chip == 0) | (chip == chips - 1)))
    for n, number in enumerate(numbers):
        out_ref[n] = number
    tiles, listed = active_ref.shape
    for t in range(tiles):
        for b in range(blocks):
            found = jnp.int32(0)
            for n in range(listed):
                found = jnp.where(active_ref[t, n] == j * blocks + b, 1, found)
            out_ref[SLOTS["hits"] + t * blocks + b] = found


def make_table(ids, active, n_tok, n_feat, blocks):
    size = SLOTS["hits"] + active.shape[0] * blocks
    return pl.pallas_call(
        functools.partial(table_body, n_tok, n_feat, blocks),
        in_specs=[SMEM, SMEM],
        out_specs=SMEM,
        out_shape=jax.ShapeDtypeStruct((size,), jnp.int32),
        compiler_params=PARAMS,
        cost_estimate=LIGHT,
        name="table",
    )(ids, active)


def pick_body(table, array_ref, *refs):
    outs, sems = refs[:-1], refs[-1]
    rows = outs[0].shape[0]
    copies = []
    for s, out_ref in enumerate(outs):
        part = array_ref.at[aligned(table[0] ^ s, rows)]
        copies.append(pltpu.make_async_copy(part, out_ref, sems.at[s]))
    for copy in copies:
        copy.start()
    for copy in copies:
        copy.wait()


def pick(table, array, n_tok):
    shape = (array.shape[0] // n_tok, array.shape[1])
    return pl.pallas_call(
        pick_body,
        in_specs=[SMEM, pl.BlockSpec(memory_space=pl.ANY)],
        out_specs=[VMEM] * n_tok,
        out_shape=[jax.ShapeDtypeStruct(shape, array.dtype)] * n_tok,
        scratch_shapes=[pltpu.SemaphoreType.DMA((n_tok,))],
        compiler_params=PARAMS,
        cost_estimate=LIGHT,
        name="pick",
    )(table, array)


def second_body(table, near_ref, far_ref, come_ref, *out_refs):
    rows = out_refs[0].shape[0]
    for h, out_ref in enumerate(out_refs):
        part = slice(h * rows, (h + 1) * rows)
        total = near_ref[part].astype(F32) + far_ref[part].astype(F32)
        out_ref[...] = (total + come_ref[part].astype(F32)).astype(BF16)


def third_body(chips, h, table, near_1, far_1, near_3, far_3, up_ref, down_ref, *targets):
    chip = table[3]
    rows = far_3.shape[0]
    part = slice(h * rows, (h + 1) * rows)
    for target, come_ref, turn in ((targets[0], up_ref, 1), (targets[1], down_ref, chips - 2)):

        @pl.when(chip == turn)
        def _():
            total = near_3[part].astype(F32) + far_3[...].astype(F32)
            target[...] = (total + come_ref[...].astype(F32)).astype(BF16)

        @pl.when(chip != turn)
        def _():
            total = near_1[part].astype(F32) + far_1[part].astype(F32)
            target[...] = (total + come_ref[...].astype(F32)).astype(BF16)


def pieces(refs, streams):
    return [refs[a].at[b] for a, stream in enumerate(streams) for b in range(len(stream))]


def aligned(index, width):
    return pl.ds(pl.multiple_of(index * width, width), width)


def enc_body(streams, count, first, last, n_feat, at, table, *refs):
    size = len(streams)
    slots = [pieces(refs[q * size:(q + 1) * size], streams) for q in range(count)]
    w_ref, bias_ref = refs[count * size:count * size + 2]
    refs = refs[count * size + 2:]
    carry_ref = None
    if not first:
        carry_ref, seen_ref, refs = refs[0], refs[1], refs[2:]
    out_ref, own_ref = refs[:2]
    total_ref = refs[2] if last else out_ref
    n_tok, width = len(slots[0]), slots[0][0].shape[1]
    if not first:
        own_ref[...] = seen_ref[...]
    for q, blocks in enumerate(slots):
        source = table[at + q]
        total = carry_ref if q == 0 else total_ref
        total = None if total is None else total[...]
        for s, x in enumerate(blocks):
            w = w_ref[(table[0] ^ s) * n_feat + source]
            term = jnp.dot(x[...], w, preferred_element_type=F32)
            total = term if total is None else total + term
        total_ref[...] = total
        for s, x in enumerate(blocks):

            @pl.when(((table[0] ^ s) == table[1]) & (source // n_tok == table[2]))
            def _():
                own_ref[:, aligned(source % n_tok, width)] = x[...]

    if last:
        blocks = out_ref.shape[1] // BLOCK
        for t in range(out_ref.shape[0] // TILE):
            for b in range(blocks):
                tile, block = slice(t * TILE, (t + 1) * TILE), slice(b * BLOCK, (b + 1) * BLOCK)
                pre = total_ref[tile, block] + bias_ref[:, block]
                live = table[SLOTS["hits"] + t * blocks + b].astype(F32)
                out_ref[tile, block] = (jnp.maximum(pre, 0.0) * live).astype(BF16)


def encode(table, at, slots, w, bias, carry, streams, last, n_feat):
    width, feats = w.shape[1:]
    rows = slots[0][0].shape[1]
    n_tok = w.shape[0] // n_feat
    args = [table] + [a for slot in slots for a in slot] + [w, bias]
    if carry is not None:
        args += carry
    return kernel_call(
        functools.partial(enc_body, streams, len(slots), carry is None, last, n_feat, at),
        [((rows, feats), BF16 if last else F32), ((rows, n_tok * width), BF16)],
        args,
        "encode",
        LIGHT if last else cost(2 * len(slots) * rows * n_tok * width * feats, 4 << 20),
        [pltpu.VMEM((rows, feats), F32)] if last else [],
    )


def dec_body(at, table, acts_ref, w_ref, *out_refs):
    share = out_refs[0].shape[1]
    for q, targets in enumerate([out_refs[:2]] + [(out_ref,) for out_ref in out_refs[2:]]):
        w = w_ref[:, aligned(table[at + q], share)]
        part = jnp.dot(acts_ref[...], w, preferred_element_type=F32).astype(BF16)
        rows = part.shape[0] // len(targets)
        for h, out_ref in enumerate(targets):
            out_ref[...] = part[h * rows:(h + 1) * rows]


def sum_body(table, near_ref, *refs):
    far_refs, out_ref = refs[:-1], refs[-1]
    rows = far_refs[0].shape[0]
    for h, far_ref in enumerate(far_refs):
        part = slice(h * rows, (h + 1) * rows)
        out_ref[part] = (near_ref[part].astype(F32) + far_ref[...].astype(F32)).astype(BF16)


def proj_body(count, first, last, n_feat, at, table, *refs):
    slots, refs = refs[:count], refs[count:]
    w_ref, acts_ref, x_ref, bias_ref = refs[:4]
    refs = refs[4:]
    if not first:
        carry_ref, seen_ref, refs = refs[0], refs[1], refs[2:]
    out_ref, sum_ref = refs[:2]
    if last:
        out_ref, line_ref, sum_ref = refs
    if first:
        sum_ref[...] = jnp.zeros_like(sum_ref)
    else:
        sum_ref[...] = seen_ref[...]
    for q, g_ref in enumerate(slots):
        n_tok, _, width = g_ref.shape
        source, held = table[at + 2 * q], table[at + 2 * q + 1] == 1

        @pl.when(held)
        def _():
            total = None if q == 0 and first else (carry_ref if q == 0 else out_ref)[...]
            for s in range(n_tok):
                w = w_ref[:, aligned((table[0] ^ s) * n_feat + source, width)]
                term = lax.dot_general(
                    g_ref[s], w, (((1,), (1,)), ((), ())), preferred_element_type=F32
                )
                total = term if total is None else total + term
            out_ref[...] = total

        @pl.when(held & (source // n_tok == table[2]))
        def _():
            cols = aligned(source % n_tok, width)
            term = x_ref[:, cols].astype(F32) - bias_ref[:, cols]
            term = term * g_ref[table[0] ^ table[1]].astype(F32)
            sum_ref[...] += jnp.sum(term, axis=1, keepdims=True)

    if last:
        attr = acts_ref[...].astype(F32) * out_ref[...]
        out_ref[...] = attr
        total = sum_ref[...] - jnp.sum(attr, axis=1, keepdims=True)
        line_ref[...] = jnp.broadcast_to(total, (total.shape[0], TILE)).T[:8]


def project(table, at, slots, w, acts, own_x, bias, carry, last, n_feat):
    rows, feats = acts.shape
    outs = [((rows, feats), F32), ((8, rows), F32) if last else ((rows, 1), F32)]
    return kernel_call(
        functools.partial(proj_body, len(slots), carry is None, last, n_feat, at),
        outs,
        [table, *slots, w, acts, own_x, bias, *(carry or [])],
        "project",
        LIGHT if last else cost(2 * len(slots) * slots[0].size * feats, 4 << 20),
        [pltpu.VMEM((rows, 1), F32)] if last else [],
    )


def line_program(resid, resid_grad, active, w_enc, b_enc, w_dec, b_dec):
    n_tok, n_feat = lax.axis_size("tok"), lax.axis_size("feat")
    i, j = lax.axis_index("tok"), lax.axis_index("feat")
    chips = n_feat // 2
    width = resid.shape[1]
    rows = resid.shape[0] // n_tok
    feats = w_enc.shape[1]
    share = n_tok * width

    def along(pairs):
        return [(2 * a + c, 2 * b + c) for a, b in pairs for c in range(2)]

    def send(array, pairs):
        return lax.ppermute(array, "feat", along(pairs))

    def cross(array):
        return lax.ppermute(array, "feat", [(a, a ^ 1) for a in range(n_feat)])

    def exchange(blocks, streams):
        blocks = list(blocks)
        for s in range(1, n_tok):
            blocks[s] = lax.ppermute(blocks[s], "tok", [(a, a ^ s) for a in range(n_tok)])
        return [jnp.stack([blocks[s] for s in stream]) for stream in streams]

    table = make_table(jnp.stack([i, j]), active, n_tok, n_feat, feats // BLOCK)
    bias = b_enc.reshape(1, feats)
    b_row = b_dec.reshape(1, share)

    ring = [(a, (a + 1) % chips) for a in range(chips)]
    cut_x = [lax.dynamic_slice_in_dim(resid, (i ^ s) * rows, rows, 0) for s in range(n_tok)]
    near_x = [exchange(cut_x, X_STREAMS)]
    cut_g = [lax.dynamic_slice_in_dim(resid_grad, (i ^ s) * rows, rows, 0) for s in range(n_tok)]
    shard_g, = exchange(cut_g, ((0, 1, 2, 3),))
    far_x = [[cross(a) for a in near_x[0]]]
    for k in range(1, chips):
        first, second = near_x[-1]
        if k == 1:
            second = after(second, table)
        if k == 2:
            second = after(second, shard_g)
            w_out, far_x[0][0] = load(w_dec, far_x[0][0], 44)
            first = after(first, far_x[0][0])
        if k == 3:
            far_x[0][1] = after(far_x[0][1], far_x[1][0])
            w_in, far_x[0][1] = load(w_enc.reshape(n_tok * n_feat, width, feats), far_x[0][1], 36)
            first = after(first, far_x[0][1])
        near_x[-1] = [first, second]
        if k > 1:
            far_x.append([cross(a) for a in near_x[-1]])
        near_x.append([send(first, ring), send(second, ring)])
    slots = [near_x[0], far_x[0], near_x[1], far_x[1]]
    carry = encode(
        after(table, near_x[3][0]), SLOTS["enc_a"], slots, w_in, bias, None, X_STREAMS, False, n_feat
    )
    far_x.append([cross(near_x[3][0]), cross(after(near_x[3][1], carry))])

    up_pairs = [(a, a + 1) for a in range(chips - 1)]
    down_pairs = [(a + 1, a) for a in range(chips - 1)]
    shard_g = after(shard_g, near_x[-1], carry)
    up_1, down_1 = send(shard_g, up_pairs), send(shard_g, down_pairs)

    slots = [near_x[2], far_x[2], near_x[3], far_x[3]]
    acts, own_x = encode(table, SLOTS["enc_b"], slots, w_in, bias, carry, X_STREAMS, True, n_feat)

    far_3_a, far_3_b, near_3, *outs = kernel_call(
        functools.partial(dec_body, SLOTS["dec"]),
        [((rows // 2, share), BF16)] * 2 + [((rows, share), BF16)] * (2 * chips - 1),
        [table, acts, w_out],
        "decode",
    )
    up_1, down_1 = after((up_1, down_1), far_3_a)
    far_in = [cross(far_3_a), cross(far_3_b)]
    start, = kernel_call(sum_body, [((rows, share), BF16)], [table, near_3, *far_in], "sum")
    outs = after(outs, start)
    parts = {k: (outs[2 * n + 1], cross(outs[2 * n])) for n, k in enumerate((2, 1, 0))}

    def pair_sum(k):
        return parts[k][0].astype(F32) + parts[k][1].astype(F32)

    come = send(start, [(0, 1), (3, 2)])
    up_2, down_2 = send(up_1, up_pairs[1:]), send(down_1, down_pairs[:-1])
    half = ((rows // 2, share), BF16)
    going = kernel_call(second_body, [half] * 2, [table, *parts[2], come], "second")
    two_g = up_2 + down_2
    three_g = send(two_g, [(2, 3), (1, 0)])

    up = [send(a, up_pairs[:2]) for a in going]
    down = [send(a, down_pairs[1:]) for a in going]

    slots = [shard_g, cross(shard_g), up_1, cross(up_1), down_1, cross(down_1)]
    carry = project(
        table, SLOTS["proj_a"], slots, w_out, after(acts, going), own_x, b_row, None, False, n_feat
    )
    base = own_x.astype(F32) - b_row - pair_sum(0)

    last, come = [], []
    for h in range(2):
        sums = kernel_call(
            functools.partial(third_body, chips, h),
            [half] * 2,
            [table, *parts[1], near_3, far_in[h], up[h], down[h]],
            "third",
        )
        going_up, going_down = after(tuple(sums), carry, base)
        last += [going_up, going_down]
        come.append(send(going_up, up_pairs).astype(F32) + send(going_down, down_pairs).astype(F32))

    slots = [two_g, cross(two_g), three_g, cross(three_g)]
    feature_attr, attr = project(
        table, SLOTS["proj_b"], slots, w_out, after(acts, *last), own_x, b_row, carry, True, n_feat
    )
    attr = attr[:1]
    attr = attr + cross(attr)
    others = [send(attr, [(a, a ^ k) for a in range(chips)]) for k in range(1, chips)]
    for other in others:
        attr = attr + other

    error = base - jnp.concatenate(come)
    return feature_attr, error, attr.reshape(rows)


def gathered_program(resid, resid_grad, active, w_enc, b_enc, w_dec, b_dec):
    n_tok = lax.axis_size("tok")
    n_feat = lax.axis_size("feat")
    width = resid.shape[1]

    def rows_of(array):
        part = lax.all_to_all(array, "tok", split_axis=0, concat_axis=1, tiled=True)
        part = part.reshape(part.shape[0], n_tok, 1, width)
        part = lax.all_gather(part, "feat", axis=2, tiled=True)
        return part.reshape(part.shape[0], n_tok * n_feat * width)

    rows_x, rows_g = rows_of(resid), rows_of(resid_grad)
    tok_rows = rows_x.shape[0]
    feat_dev = w_enc.shape[1]
    blocks = feat_dev // BLOCK
    tiles_dev = active.shape[0]
    block_ids = lax.axis_index("feat") * blocks + jnp.arange(blocks, dtype=jnp.int32)
    hits = jnp.any(active[:, :, None] == block_ids[None, None, :], axis=1).astype(F32)
    pre = jnp.dot(rows_x, w_enc, preferred_element_type=F32) + b_enc
    shaped = jnp.maximum(pre, 0.0).reshape(tiles_dev, TILE, blocks, BLOCK) * hits[:, None, :, None]
    acts = shaped.reshape(tok_rows, feat_dev).astype(BF16)
    partial_recon = jnp.dot(acts, w_dec, preferred_element_type=F32)
    recon_share = lax.psum_scatter(
        partial_recon.astype(BF16), "feat", scatter_dimension=1, tiled=True
    ).astype(F32)
    share = recon_share.shape[1]
    start = lax.axis_index("feat") * share
    own_x = lax.dynamic_slice_in_dim(rows_x, start, share, 1)
    own_g = lax.dynamic_slice_in_dim(rows_g, start, share, 1)
    recon = recon_share + b_dec
    error = own_x.astype(F32) - recon
    local_sums = jnp.sum(error * own_g.astype(F32), axis=1)
    error_attr = lax.psum(local_sums, "feat")
    proj = lax.dot_general(rows_g, w_dec, (((1,), (1,)), ((), ())), preferred_element_type=F32)
    return acts.astype(F32) * proj, error, error_attr


def per_device(resid, *rest):
    fits = resid.shape[1] % 128 == 0 and lax.axis_size("tok") == 4 and lax.axis_size("feat") == 8
    return (line_program if fits else gathered_program)(resid, *rest)


def solution(mesh):
    placed = (
        P(None, ("tok", "feat")),
        P(None, ("tok", "feat")),
        P("tok", None),
        P(None, "feat"),
        P("feat"),
        P("feat", None),
        P("feat"),
    )
    return jax.shard_map(
        per_device,
        mesh=mesh,
        in_specs=placed,
        out_specs=(P("tok", "feat"), P("tok", "feat"), P("tok")),
        check_vma=False,
    )
```

```python
import functools

import jax
import jax.numpy as jnp
from jax import lax
from jax.experimental import pallas as pl
from jax.experimental.pallas import tpu as pltpu
from jax.sharding import PartitionSpec as P

BLOCK = 128
TILE = 128
X_STREAMS = ((0, 1), (2, 3))
PIECES = 8
PARAMS = pltpu.CompilerParams(vmem_limit_bytes=20 << 20)
F32 = jnp.float32
BF16 = jnp.bfloat16
LIGHT = pl.CostEstimate(flops=1, bytes_accessed=1, transcendentals=0)
VMEM = pl.BlockSpec(memory_space=pltpu.VMEM)
SMEM = pl.BlockSpec(memory_space=pltpu.SMEM)


def cost(flops, moved):
    return pl.CostEstimate(flops=flops, bytes_accessed=moved, transcendentals=0)


def after(value, *others):
    return lax.optimization_barrier((value, others))[0]


def kernel_call(body, outs, args, name, hint=LIGHT, scratch=()):
    return pl.pallas_call(
        body,
        in_specs=[SMEM] + [VMEM] * (len(args) - 1),
        out_specs=[VMEM] * len(outs),
        out_shape=[jax.ShapeDtypeStruct(shape, kind) for shape, kind in outs],
        scratch_shapes=list(scratch),
        compiler_params=PARAMS,
        cost_estimate=hint,
        name=name,
    )(*args)


def load_body(w_ref, through_ref, out_ref, same_ref, sems):
    step = w_ref.shape[0] // PIECES
    copies = []
    for n in range(PIECES):
        part = pl.ds(n * step, step)
        copies.append(pltpu.make_async_copy(w_ref.at[part], out_ref.at[part], sems.at[n]))
    for copy in copies:
        copy.start()
    for copy in copies:
        copy.wait()


def load(w, through, room):
    anywhere = pl.BlockSpec(memory_space=pl.ANY)
    return pl.pallas_call(
        load_body,
        in_specs=[anywhere, anywhere],
        out_specs=[VMEM, anywhere],
        out_shape=[
            pltpu.VMEM(w.shape, w.dtype),
            jax.ShapeDtypeStruct(through.shape, through.dtype),
        ],
        scratch_shapes=[pltpu.SemaphoreType.DMA((PIECES,))],
        input_output_aliases={1: 1},
        compiler_params=pltpu.CompilerParams(vmem_limit_bytes=room << 20),
        cost_estimate=cost(0, 2 * w.size),
        name="load",
    )(w, through)


SLOTS = {"enc_a": 4, "enc_b": 8, "dec": 12, "proj_a": 20, "proj_b": 32, "hits": 40}


def table_body(n_tok, n_feat, blocks, ids_ref, active_ref, out_ref):
    i, j = ids_ref[0], ids_ref[1]
    chips, ratio = n_feat // 2, n_feat // n_tok
    chip, core = j // 2, j % 2

    def both_cores(place):
        return [2 * place + core, 2 * place + 1 - core]

    def held_slots(*sources):
        values, seen = [], 0
        for place, valid in sources:
            seen = jnp.where(valid, place, seen)
            for source in both_cores(seen):
                values += [source, jnp.where(valid, 1, 0)]
        return values

    numbers = [i, j // ratio, j % ratio, chip]
    for k in range(chips):
        numbers += both_cores((chip + chips - k) % chips)
    for k in (3, 2, 1, 0):
        numbers += both_cores(chip ^ k)[::-1]
    numbers += held_slots((chip, chip >= 0), (chip - 1, chip >= 1), (chip + 1, chip <= chips - 2))
    numbers += held_slots((chip ^ 2, chip >= 0), (chip ^ 3, (chip == 0) | (chip == chips - 1)))
    for n, number in enumerate(numbers):
        out_ref[n] = number
    tiles, listed = active_ref.shape
    for t in range(tiles):
        for b in range(blocks):
            found = jnp.int32(0)
            for n in range(listed):
                found = jnp.where(active_ref[t, n] == j * blocks + b, 1, found)
            out_ref[SLOTS["hits"] + t * blocks + b] = found


def make_table(ids, active, n_tok, n_feat, blocks):
    size = SLOTS["hits"] + active.shape[0] * blocks
    return pl.pallas_call(
        functools.partial(table_body, n_tok, n_feat, blocks),
        in_specs=[SMEM, SMEM],
        out_specs=SMEM,
        out_shape=jax.ShapeDtypeStruct((size,), jnp.int32),
        compiler_params=PARAMS,
        cost_estimate=LIGHT,
        name="table",
    )(ids, active)


def pick_body(table, array_ref, *refs):
    outs, sems = refs[:-1], refs[-1]
    rows = outs[0].shape[0]
    copies = []
    for s, out_ref in enumerate(outs):
        part = array_ref.at[aligned(table[0] ^ s, rows)]
        copies.append(pltpu.make_async_copy(part, out_ref, sems.at[s]))
    for copy in copies:
        copy.start()
    for copy in copies:
        copy.wait()


def pick(table, array, n_tok):
    shape = (array.shape[0] // n_tok, array.shape[1])
    return pl.pallas_call(
        pick_body,
        in_specs=[SMEM, pl.BlockSpec(memory_space=pl.ANY)],
        out_specs=[VMEM] * n_tok,
        out_shape=[jax.ShapeDtypeStruct(shape, array.dtype)] * n_tok,
        scratch_shapes=[pltpu.SemaphoreType.DMA((n_tok,))],
        compiler_params=PARAMS,
        cost_estimate=LIGHT,
        name="pick",
    )(table, array)


def third_body(chips, table, *refs):
    near_1, far_1, near_3, far_3, up_ref, down_ref = refs[:3] + (refs[3:-4],) + refs[-4:-2]
    chip = table[3]
    for target, come_ref, turn in ((refs[-2], up_ref, 1), (refs[-1], down_ref, chips - 2)):

        @pl.when(chip == turn)
        def _():
            rows = far_3[0].shape[0]
            for h, far_ref in enumerate(far_3):
                part = slice(h * rows, (h + 1) * rows)
                total = near_3[part].astype(F32) + far_ref[...].astype(F32)
                target[part] = (total + come_ref[part].astype(F32)).astype(BF16)

        @pl.when(chip != turn)
        def _():
            total = near_1[...].astype(F32) + far_1[...].astype(F32)
            target[...] = (total + come_ref[...].astype(F32)).astype(BF16)


def pieces(refs, streams):
    return [refs[a].at[b] for a, stream in enumerate(streams) for b in range(len(stream))]


def aligned(index, width):
    return pl.ds(pl.multiple_of(index * width, width), width)


def enc_body(streams, count, first, last, n_feat, at, table, *refs):
    size = len(streams)
    slots = [pieces(refs[q * size:(q + 1) * size], streams) for q in range(count)]
    w_ref, bias_ref = refs[count * size:count * size + 2]
    refs = refs[count * size + 2:]
    carry_ref = None
    if not first:
        carry_ref, seen_ref, refs = refs[0], refs[1], refs[2:]
    out_ref, own_ref = refs[:2]
    total_ref = refs[2] if last else out_ref
    n_tok, width = len(slots[0]), slots[0][0].shape[1]
    if not first:
        own_ref[...] = seen_ref[...]
    for q, blocks in enumerate(slots):
        source = table[at + q]
        total = carry_ref if q == 0 else total_ref
        total = None if total is None else total[...]
        for s, x in enumerate(blocks):
            w = w_ref[(table[0] ^ s) * n_feat + source]
            term = jnp.dot(x[...], w, preferred_element_type=F32)
            total = term if total is None else total + term
        total_ref[...] = total
        for s, x in enumerate(blocks):

            @pl.when(((table[0] ^ s) == table[1]) & (source // n_tok == table[2]))
            def _():
                own_ref[:, aligned(source % n_tok, width)] = x[...]

    if last:
        blocks = out_ref.shape[1] // BLOCK
        for t in range(out_ref.shape[0] // TILE):
            for b in range(blocks):
                tile, block = slice(t * TILE, (t + 1) * TILE), slice(b * BLOCK, (b + 1) * BLOCK)
                pre = total_ref[tile, block] + bias_ref[:, block]
                live = table[SLOTS["hits"] + t * blocks + b].astype(F32)
                out_ref[tile, block] = (jnp.maximum(pre, 0.0) * live).astype(BF16)


def encode(table, at, slots, w, bias, carry, streams, last, n_feat):
    width, feats = w.shape[1:]
    rows = slots[0][0].shape[1]
    n_tok = w.shape[0] // n_feat
    args = [table] + [a for slot in slots for a in slot] + [w, bias]
    if carry is not None:
        args += carry
    return kernel_call(
        functools.partial(enc_body, streams, len(slots), carry is None, last, n_feat, at),
        [((rows, feats), BF16 if last else F32), ((rows, n_tok * width), BF16)],
        args,
        "encode",
        LIGHT if last else cost(2 * len(slots) * rows * n_tok * width * feats, 4 << 20),
        [pltpu.VMEM((rows, feats), F32)] if last else [],
    )


def dec_body(at, table, acts_ref, w_ref, *out_refs):
    share = out_refs[0].shape[1]
    for q, targets in enumerate([out_refs[:2]] + [(out_ref,) for out_ref in out_refs[2:]]):
        w = w_ref[:, aligned(table[at + q], share)]
        part = jnp.dot(acts_ref[...], w, preferred_element_type=F32).astype(BF16)
        rows = part.shape[0] // len(targets)
        for h, out_ref in enumerate(targets):
            out_ref[...] = part[h * rows:(h + 1) * rows]


def sum_body(table, near_ref, *refs):
    far_refs, out_ref = refs[:-1], refs[-1]
    rows = far_refs[0].shape[0]
    for h, far_ref in enumerate(far_refs):
        part = slice(h * rows, (h + 1) * rows)
        out_ref[part] = (near_ref[part].astype(F32) + far_ref[...].astype(F32)).astype(BF16)


def proj_body(count, first, last, n_feat, at, table, *refs):
    slots, refs = refs[:count], refs[count:]
    w_ref, acts_ref, x_ref, bias_ref = refs[:4]
    refs = refs[4:]
    if not first:
        carry_ref, seen_ref, refs = refs[0], refs[1], refs[2:]
    out_ref, sum_ref = refs[:2]
    if last:
        out_ref, line_ref, sum_ref = refs
    if first:
        sum_ref[...] = jnp.zeros_like(sum_ref)
    else:
        sum_ref[...] = seen_ref[...]
    for q, g_ref in enumerate(slots):
        n_tok, _, width = g_ref.shape
        source, held = table[at + 2 * q], table[at + 2 * q + 1] == 1

        @pl.when(held)
        def _():
            total = None if q == 0 and first else (carry_ref if q == 0 else out_ref)[...]
            for s in range(n_tok):
                w = w_ref[:, aligned((table[0] ^ s) * n_feat + source, width)]
                term = lax.dot_general(
                    g_ref[s], w, (((1,), (1,)), ((), ())), preferred_element_type=F32
                )
                total = term if total is None else total + term
            out_ref[...] = total

        @pl.when(held & (source // n_tok == table[2]))
        def _():
            cols = aligned(source % n_tok, width)
            term = x_ref[:, cols].astype(F32) - bias_ref[:, cols]
            term = term * g_ref[table[0] ^ table[1]].astype(F32)
            sum_ref[...] += jnp.sum(term, axis=1, keepdims=True)

    if last:
        attr = acts_ref[...].astype(F32) * out_ref[...]
        out_ref[...] = attr
        total = sum_ref[...] - jnp.sum(attr, axis=1, keepdims=True)
        line_ref[...] = jnp.broadcast_to(total, (total.shape[0], TILE)).T[:8]


def project(table, at, slots, w, acts, own_x, bias, carry, last, n_feat):
    rows, feats = acts.shape
    outs = [((rows, feats), F32), ((8, rows), F32) if last else ((rows, 1), F32)]
    return kernel_call(
        functools.partial(proj_body, len(slots), carry is None, last, n_feat, at),
        outs,
        [table, *slots, w, acts, own_x, bias, *(carry or [])],
        "project",
        LIGHT if last else cost(2 * len(slots) * slots[0].size * feats, 4 << 20),
        [pltpu.VMEM((rows, 1), F32)] if last else [],
    )


def line_program(resid, resid_grad, active, w_enc, b_enc, w_dec, b_dec):
    n_tok, n_feat = lax.axis_size("tok"), lax.axis_size("feat")
    i, j = lax.axis_index("tok"), lax.axis_index("feat")
    chips = n_feat // 2
    width = resid.shape[1]
    rows = resid.shape[0] // n_tok
    feats = w_enc.shape[1]
    share = n_tok * width

    def along(pairs):
        return [(2 * a + c, 2 * b + c) for a, b in pairs for c in range(2)]

    def send(array, pairs):
        return lax.ppermute(array, "feat", along(pairs))

    def cross(array):
        return lax.ppermute(array, "feat", [(a, a ^ 1) for a in range(n_feat)])

    def exchange(blocks, streams):
        blocks = list(blocks)
        for s in range(1, n_tok):
            blocks[s] = lax.ppermute(blocks[s], "tok", [(a, a ^ s) for a in range(n_tok)])
        return [jnp.stack([blocks[s] for s in stream]) for stream in streams]

    table = make_table(jnp.stack([i, j]), active, n_tok, n_feat, feats // BLOCK)
    bias = b_enc.reshape(1, feats)
    b_row = b_dec.reshape(1, share)

    ring = [(a, (a + 1) % chips) for a in range(chips)]
    cut_x = [lax.dynamic_slice_in_dim(resid, (i ^ s) * rows, rows, 0) for s in range(n_tok)]
    near_x = [exchange(cut_x, X_STREAMS)]
    far_x = [[cross(a) for a in near_x[0]]]
    for k in range(1, chips):
        first, second = near_x[-1]
        if k == 1:
            second = after(second, table)
        if k == 2:
            w_out, far_x[0][0] = load(w_dec, far_x[0][0], 44)
            first = after(first, far_x[0][0])
        if k == 3:
            far_x[0][1] = after(far_x[0][1], far_x[1][0])
            w_in, far_x[0][1] = load(w_enc.reshape(n_tok * n_feat, width, feats), far_x[0][1], 36)
            first = after(first, far_x[0][1])
            shard_g, = exchange(pick(table, after(resid_grad, first), n_tok), ((0, 1, 2, 3),))
        near_x[-1] = [first, second]
        if k > 1:
            far_x.append([cross(a) for a in near_x[-1]])
        near_x.append([send(first, ring), send(second, ring)])
    slots = [near_x[0], far_x[0], near_x[1], far_x[1]]
    carry = encode(
        after(table, near_x[3][0]), SLOTS["enc_a"], slots, w_in, bias, None, X_STREAMS, False, n_feat
    )
    far_x.append([cross(after(near_x[3][0], shard_g)), cross(after(near_x[3][1], carry))])

    up_pairs = [(a, a + 1) for a in range(chips - 1)]
    down_pairs = [(a + 1, a) for a in range(chips - 1)]
    shard_g = after(shard_g, near_x[-1], carry)
    up_1, down_1 = send(shard_g, up_pairs), send(shard_g, down_pairs)

    slots = [near_x[2], far_x[2], near_x[3], far_x[3]]
    acts, own_x = encode(table, SLOTS["enc_b"], slots, w_in, bias, carry, X_STREAMS, True, n_feat)

    far_3_a, far_3_b, near_3, *outs = kernel_call(
        functools.partial(dec_body, SLOTS["dec"]),
        [((rows // 2, share), BF16)] * 2 + [((rows, share), BF16)] * (2 * chips - 1),
        [table, acts, w_out],
        "decode",
    )
    up_1, down_1 = after((up_1, down_1), far_3_a)
    far_in = [cross(far_3_a), cross(far_3_b)]
    start, = kernel_call(sum_body, [((rows, share), BF16)], [table, near_3, *far_in], "sum")
    outs = after(outs, start)
    parts = {k: (outs[2 * n + 1], cross(outs[2 * n])) for n, k in enumerate((2, 1, 0))}

    def pair_sum(k):
        return parts[k][0].astype(F32) + parts[k][1].astype(F32)

    come = send(start, [(0, 1), (3, 2)])
    up_2, down_2 = send(up_1, up_pairs[1:]), send(down_1, down_pairs[:-1])
    going = (pair_sum(2) + come.astype(F32)).astype(BF16)
    two_g = up_2 + down_2
    three_g = send(two_g, [(2, 3), (1, 0)])

    up = send(going, up_pairs[:2])
    down = send(going, down_pairs[1:])

    slots = [shard_g, cross(shard_g), up_1, cross(up_1), down_1, cross(down_1)]
    carry = project(
        table, SLOTS["proj_a"], slots, w_out, after(acts, going), own_x, b_row, None, False, n_feat
    )
    base = own_x.astype(F32) - b_row - pair_sum(0)

    going_up, going_down = kernel_call(
        functools.partial(third_body, chips),
        [((rows, share), BF16)] * 2,
        [table, *parts[1], near_3, *far_in, up, down],
        "third",
    )
    going_up, going_down = after((going_up, going_down), carry, base)
    up = send(going_up, up_pairs)
    down = send(going_down, down_pairs)

    slots = [two_g, cross(two_g), three_g, cross(three_g)]
    feature_attr, attr = project(
        table, SLOTS["proj_b"], slots, w_out, after(acts, going_up, going_down), own_x, b_row, carry, True, n_feat
    )
    attr = attr[:1]
    attr = attr + cross(attr)
    others = [send(attr, [(a, a ^ k) for a in range(chips)]) for k in range(1, chips)]
    for other in others:
        attr = attr + other

    error = base - (up.astype(F32) + down.astype(F32))
    return feature_attr, error, attr.reshape(rows)


def gathered_program(resid, resid_grad, active, w_enc, b_enc, w_dec, b_dec):
    n_tok = lax.axis_size("tok")
    n_feat = lax.axis_size("feat")
    width = resid.shape[1]

    def rows_of(array):
        part = lax.all_to_all(array, "tok", split_axis=0, concat_axis=1, tiled=True)
        part = part.reshape(part.shape[0], n_tok, 1, width)
        part = lax.all_gather(part, "feat", axis=2, tiled=True)
        return part.reshape(part.shape[0], n_tok * n_feat * width)

    rows_x, rows_g = rows_of(resid), rows_of(resid_grad)
    tok_rows = rows_x.shape[0]
    feat_dev = w_enc.shape[1]
    blocks = feat_dev // BLOCK
    tiles_dev = active.shape[0]
    block_ids = lax.axis_index("feat") * blocks + jnp.arange(blocks, dtype=jnp.int32)
    hits = jnp.any(active[:, :, None] == block_ids[None, None, :], axis=1).astype(F32)
    pre = jnp.dot(rows_x, w_enc, preferred_element_type=F32) + b_enc
    shaped = jnp.maximum(pre, 0.0).reshape(tiles_dev, TILE, blocks, BLOCK) * hits[:, None, :, None]
    acts = shaped.reshape(tok_rows, feat_dev).astype(BF16)
    partial_recon = jnp.dot(acts, w_dec, preferred_element_type=F32)
    recon_share = lax.psum_scatter(
        partial_recon.astype(BF16), "feat", scatter_dimension=1, tiled=True
    ).astype(F32)
    share = recon_share.shape[1]
    start = lax.axis_index("feat") * share
    own_x = lax.dynamic_slice_in_dim(rows_x, start, share, 1)
    own_g = lax.dynamic_slice_in_dim(rows_g, start, share, 1)
    recon = recon_share + b_dec
    error = own_x.astype(F32) - recon
    local_sums = jnp.sum(error * own_g.astype(F32), axis=1)
    error_attr = lax.psum(local_sums, "feat")
    proj = lax.dot_general(rows_g, w_dec, (((1,), (1,)), ((), ())), preferred_element_type=F32)
    return acts.astype(F32) * proj, error, error_attr


def per_device(resid, *rest):
    fits = resid.shape[1] % 128 == 0 and lax.axis_size("tok") == 4 and lax.axis_size("feat") == 8
    return (line_program if fits else gathered_program)(resid, *rest)


def solution(mesh):
    placed = (
        P(None, ("tok", "feat")),
        P(None, ("tok", "feat")),
        P("tok", None),
        P(None, "feat"),
        P("feat"),
        P("feat", None),
        P("feat"),
    )
    return jax.shard_map(
        per_device,
        mesh=mesh,
        in_specs=placed,
        out_specs=(P("tok", "feat"), P("tok", "feat"), P("tok")),
        check_vma=False,
    )
```
